32 devices in a mesh: batch: 8 (over y, x, core), tensor: 4 (over z).
Axes of the slice: x: 2, y: 2, z: 4, core: 2. Of those that a mesh axis runs over, the one named last changes fastest.
Arguments:
- inputs: bfloat16 [16, 1024, 512], P('batch'), may hold values from -6 to 6
- doc_lengths: int32 [16, 4], P('batch'), may hold values from 1 to 512, 1024 in all within a row
- ln1_gain: float32 [512], replicated, may hold values from 0.5 to 1.5
- ln1_bias: float32 [512], replicated, may hold values from -2.5 to 2.5
- w_qkv: bfloat16 [3, 512, 512], P(None, None, 'tensor'), may hold values from -0.25 to 0.25
- entmax_alpha: float32 [8], P('tensor'), may hold values from 1.15 to 1.5
- w_out: bfloat16 [512, 512], P('tensor'), may hold values from -0.75 to 0.75
- ln2_gain: float32 [512], replicated, may hold values from 0.5 to 1.5
- ln2_bias: float32 [512], replicated, may hold values from -2.5 to 2.5
- w_up: bfloat16 [512, 2048], P(None, 'tensor'), may hold values from -0.25 to 0.25
- up_bias: float32 [2048], P('tensor'), may hold values from -2.5 to 2.5
- w_down: bfloat16 [2048, 512], P('tensor'), may hold values from -0.125 to 0.125
- down_bias: float32 [512], replicated, may hold values from -2.5 to 2.5
- cotangent: bfloat16 [16, 1024, 512], P('batch'), may hold values from -6 to 6
Outputs:
- output: bfloat16 [16, 1024, 512], P('batch')
- grad_input: bfloat16 [16, 1024, 512], P('batch')
- grad_ln1_gain: float32 [512], replicated
- grad_ln1_bias: float32 [512], replicated
- grad_w_qkv: float32 [3, 512, 512], P(None, None, 'tensor')
- grad_alpha: float32 [8], P('tensor')
- grad_w_out: float32 [512, 512], P('tensor')
- grad_ln2_gain: float32 [512], replicated
- grad_ln2_bias: float32 [512], replicated
- grad_w_up: float32 [512, 2048], P(None, 'tensor')
- grad_up_bias: float32 [2048], P('tensor')
- grad_w_down: float32 [2048, 512], P('tensor')
- grad_down_bias: float32 [512], replicated
The draws below stay inside these ranges and needn't reach their ends.
Inputs may be any that keep to these rules, and one draw needn't show every extreme that they name: `doc_lengths`: each row's 4 lengths sum to 1024, and the largest in each row is 512.
All inputs are finite; a program needn't handle non-finite values.
Results may differ from the reference program's by a relative error of at most 0.03.
Values may be sent and summed in bfloat16 or wider, within the bound.
No kernel may reach another device: no remote copies, remote signals or barrier semaphores. Data moves between devices by JAX's collectives and lax.ppermute only.
A program may use at most 128 MiB of HBM per device.

```python
import math
import jax
import jax.numpy as jnp
import numpy as np
from jax import lax

D = 512
HEADS = 8
HEAD_DIM = 64
FF = 2048
SEQ_LEN = 1024
DOCS = 4
BISECT = 10
SEQS = 16


def level_of(stream_key, dims, pieces, smallest, high):
    factor_of = 1.0
    for position, shards_of in pieces:
        heights = jax.random.uniform(jax.random.fold_in(jax.random.fold_in(stream_key, 6), position), (shards_of,), jnp.float32, smallest / len(pieces), high / len(pieces))
        factor_of = factor_of * jnp.repeat(jnp.exp(heights), dims[position] // shards_of).reshape((-1,) + (1,) * (len(dims) - 1 - position))
    return factor_of


def split_up(number_of, total, most, lean):
    portions = [(1 << 20) // math.isqrt(rank ** lean) + 1 for rank in range(2, number_of + 1)]
    surplus, counts = total - most - (number_of - 1), [1] * (number_of - 1)
    while surplus > 0:
        free = [i for i in range(number_of - 1) if counts[i] < most]
        whole, budget = sum([portions[i] for i in free]), surplus
        for i in free:
            extra = min(most - counts[i], max(1, budget * portions[i] // whole), surplus)
            counts[i] = counts[i] + extra
            surplus = surplus - extra
    return np.array([most] + counts)


def ragged(key, count, total, bound, skew):
    if count == 2:
        one = jax.random.randint(key, (), max(1, total - bound), min(bound, total - 1) + 1)
        return jnp.stack([one, total - one])
    sizes = jnp.asarray(split_up(count, total, bound, skew), jnp.int32)
    pairs = (count - 1) // 2
    source_of, sink = sizes[1:1 + 2 * pairs:2], sizes[2:2 + 2 * pairs:2]
    slack = jnp.minimum(source_of - 1, bound - sink)
    moved = jax.random.randint(jax.random.fold_in(key, 1), (pairs,), 0, 1 << 20) % (slack + 1)
    sizes = sizes.at[1:1 + 2 * pairs:2].set(source_of - moved).at[2:2 + 2 * pairs:2].set(sink + moved)
    return sizes[jax.random.permutation(jax.random.fold_in(key, 2), count)]


def scatter_about(stream_key, shape, width, bound, pieces=(), held_as=jnp.bfloat16):
    values = jax.random.normal(stream_key, shape, jnp.float32) * width
    if len(pieces) > 0:
        values = level_of(stream_key, shape, pieces, -0.22, 0.18) * values
    return jnp.clip(values, min=-bound, max=bound).astype(held_as)


def setup_inputs(seed: int = 0) -> dict:
    splits = jax.random.split(jax.random.key(seed), 15)
    inputs = scatter_about(splits[0], (SEQS, SEQ_LEN, D), 1.0, 6.0, ((0, 8),))
    doc_lengths = jax.vmap(lambda own: ragged(own, DOCS, SEQ_LEN, SEQ_LEN // 2, 2))(jax.random.split(splits[1], SEQS)).reshape((SEQS, DOCS)).astype(jnp.int32)
    ln1_gain = jnp.clip(1.0 + 0.1 * jax.random.normal(splits[2], (D,), jnp.float32), 0.5, 1.5)
    ln1_bias = scatter_about(splits[3], (D,), 0.3, 2.5, (), jnp.float32)
    w_qkv = scatter_about(splits[4], (3, D, D), D ** -0.5, 0.25, ((2, 4),))
    entmax_alpha = jnp.clip(1.15 + 0.35000002 * jax.random.uniform(splits[5], (HEADS,), jnp.float32) ** level_of(splits[5], (HEADS,), ((0, 4),), -0.2, 0.2), 1.15, 1.5)
    w_out = scatter_about(splits[6], (D, D), (D // 8) ** -0.5, 0.75, ((0, 4),))
    ln2_gain = jnp.clip(1.0 + 0.1 * jax.random.normal(splits[7], (D,), jnp.float32), 0.5, 1.5)
    ln2_bias = scatter_about(splits[8], (D,), 0.3, 2.5, (), jnp.float32)
    w_up = scatter_about(splits[9], (D, FF), D ** -0.5, 0.25, ((1, 4),))
    up_bias = scatter_about(splits[10], (FF,), 0.3, 2.5, ((0, 4),), jnp.float32)
    w_down = scatter_about(splits[11], (FF, D), FF ** -0.5, 0.125, ((0, 4),))
    down_bias = scatter_about(splits[12], (D,), 0.3, 2.5, (), jnp.float32)
    cotangent = scatter_about(splits[13], (SEQS, SEQ_LEN, D), 1.0, 6.0, ((0, 8),))
    return dict(inputs=inputs, doc_lengths=doc_lengths, ln1_gain=ln1_gain, ln1_bias=ln1_bias, w_qkv=w_qkv, entmax_alpha=entmax_alpha, w_out=w_out, ln2_gain=ln2_gain, ln2_bias=ln2_bias, w_up=w_up, up_bias=up_bias, w_down=w_down, down_bias=down_bias, cotangent=cotangent)


masked_level = -10000.0
tiny_base = 1e-30
norm_eps = 1e-05

@jax.custom_vjp
def low(v):
    return lax.optimization_barrier(v.astype(jnp.bfloat16)).astype(jnp.float32)

@jax.custom_vjp
def low_back(v):
    return v

def low_keep(v):
    return (low(v), None)

def low_pass(kept, grad):
    return (grad,)

def back_keep(v):
    return (v, None)

def back_low(kept, grad):
    return (low(grad),)
low.defvjp(low_keep, low_pass)
low_back.defvjp(back_keep, back_low)

def layer_norm(values, norm_gain, norm_shift):
    centre = values - lax.optimization_barrier(jnp.mean(values, axis=-1, keepdims=True))
    spread = lax.optimization_barrier(jnp.mean(centre * centre, axis=-1, keepdims=True))
    return centre * lax.rsqrt(spread + norm_eps) * norm_gain + norm_shift

def gelu_tanh(values):
    return jax.nn.gelu(values, approximate=True)

def pow_safe(margin, exponent):
    return jnp.where(margin > 0, jnp.exp(exponent * jnp.log(jnp.maximum(margin, tiny_base))), 0.0)

def entmax_threshold(shifted, allowed, alpha_minus):
    exponent = 1.0 / alpha_minus
    counted = lax.optimization_barrier(jnp.sum(allowed.astype(shifted.dtype), axis=-1, keepdims=True))
    highest = lax.optimization_barrier(jnp.max(shifted, axis=-1, keepdims=True))
    low_end = highest - 1.0
    bracket = highest - jnp.exp(-alpha_minus * jnp.log(counted)) - low_end
    for bisect_step in range(BISECT):
        bracket = bracket * 0.5
        middle = low_end + bracket
        summed = lax.optimization_barrier(jnp.sum(pow_safe(shifted - middle, exponent), axis=-1, keepdims=True))
        low_end = jnp.where(summed >= 1.0, middle, low_end)
    margin = shifted - low_end
    summed = lax.optimization_barrier(jnp.sum(pow_safe(margin, exponent), axis=-1, keepdims=True))
    slopes = lax.optimization_barrier(jnp.sum(exponent * pow_safe(margin, exponent - 1.0), axis=-1, keepdims=True))
    return low_end + (summed - 1.0) / slopes

def doc_index(lengths, length):
    doc_ends = jnp.cumsum(lengths)
    places = jnp.arange(length, dtype=jnp.int32)
    return lax.optimization_barrier(jnp.sum((places[:, None] >= doc_ends[None, :]).astype(jnp.int32), axis=1))

def reference(inputs, doc_lengths, ln1_gain, ln1_bias, w_qkv, entmax_alpha, w_out, ln2_gain, ln2_bias, w_up, up_bias, w_down, down_bias, cotangent):
    top_precision = lax.Precision.HIGHEST

    def forward(token_rows, gain_one, shift_one, weight_qkv, alpha_values, weight_out, gain_two, shift_two, weight_up, bias_up, weight_down, bias_down):
        normed_one = low(layer_norm(token_rows, gain_one, shift_one))
        projected = low(low_back(jnp.einsum('nd,cde->cne', normed_one, weight_qkv, precision=top_precision)))
        split_heads = projected.reshape(3, SEQS, SEQ_LEN, HEADS, HEAD_DIM)

        def sequence_attention(packed):
            query_rows, key_rows, value_rows, lengths = packed
            doc_ids = doc_index(lengths, SEQ_LEN)
            places = jnp.arange(SEQ_LEN, dtype=jnp.int32)
            allowed = (places[None, :] <= places[:, None]) & (doc_ids[None, :] == doc_ids[:, None])

            def head_attention(head_pack):
                head_query, head_key, head_value, alpha_one = head_pack
                scores = low_back(jnp.dot(head_query, head_key.T, precision=top_precision) * HEAD_DIM ** (-0.5))
                alpha_minus = alpha_one - 1.0
                shifted = jnp.where(allowed, alpha_minus * scores, masked_level)
                threshold = entmax_threshold(shifted, allowed, alpha_minus)
                entmax_probs = pow_safe(shifted - threshold, 1.0 / alpha_minus)
                return jnp.dot(low(entmax_probs), head_value, precision=top_precision)
            per_head = lax.map(jax.checkpoint(head_attention), (jnp.swapaxes(query_rows, 0, 1), jnp.swapaxes(key_rows, 0, 1), jnp.swapaxes(value_rows, 0, 1), alpha_values))
            return jnp.swapaxes(per_head, 0, 1).reshape(SEQ_LEN, HEADS * HEAD_DIM)
        attended = lax.map(sequence_attention, (split_heads[0], split_heads[1], split_heads[2], doc_lengths))
        attended = low(low_back(attended.reshape(SEQS * SEQ_LEN, D)))
        resid_one = token_rows + low_back(jnp.dot(attended, weight_out, precision=top_precision))
        normed_two = low(layer_norm(resid_one, gain_two, shift_two))
        pre_act = low_back(jnp.dot(normed_two, weight_up, precision=top_precision) + bias_up)
        act_low = low(gelu_tanh(pre_act))
        branch = low_back(jnp.dot(act_low, weight_down, precision=top_precision))
        return resid_one + branch + bias_down
    primals = (inputs.reshape(SEQS * SEQ_LEN, D).astype(jnp.float32), ln1_gain, ln1_bias, w_qkv.astype(jnp.float32), entmax_alpha, w_out.astype(jnp.float32), ln2_gain, ln2_bias, w_up.astype(jnp.float32), up_bias, w_down.astype(jnp.float32), down_bias)
    result, pullback = jax.vjp(forward, *primals)
    gradients = pullback(cotangent.reshape(SEQS * SEQ_LEN, D).astype(jnp.float32))
    output = result.astype(jnp.bfloat16).reshape(SEQS, SEQ_LEN, D)
    grad_input = gradients[0].astype(jnp.bfloat16).reshape(SEQS, SEQ_LEN, D)
    return (output, grad_input, gradients[1], gradients[2], gradients[3], gradients[4], gradients[5], gradients[6], gradients[7], gradients[8], gradients[9], gradients[10], gradients[11])
```

```python
import functools

import jax
import jax.numpy as jnp
from jax import lax
from jax.experimental import pallas as pl
from jax.experimental.pallas import tpu as pltpu
from jax.sharding import PartitionSpec as P

BISECT = 10
MASKED = -10000.0
NORM_EPS = 1e-05
LN2 = 0.6931471805599453
TILE = 128
PLANE = 8
ORDER = (0, 2, 4, 6, 1, 3, 5, 7)
VMEM_BYTES = 48 * 1024 * 1024
BF16 = jnp.bfloat16
F32 = jnp.float32


def layer_norm(values, norm_gain, norm_shift):
    centre = values - jnp.mean(values, axis=-1, keepdims=True)
    spread = jnp.mean(centre * centre, axis=-1, keepdims=True)
    return centre * lax.rsqrt(spread + NORM_EPS) * norm_gain + norm_shift


def gelu_tanh(values):
    return jax.nn.gelu(values, approximate=True)


def dot_nt(left, right):
    return lax.dot_general(left, right, (((1,), (1,)), ((), ())), preferred_element_type=F32)


def dot_nn(left, right):
    return lax.dot_general(left, right, (((1,), (0,)), ((), ())), preferred_element_type=F32)


def dot_tn(left, right):
    return lax.dot_general(left, right, (((0,), (0,)), ((), ())), preferred_element_type=F32)


def tile_mask(first, starts_ref):
    keys = lax.broadcasted_iota(jnp.int32, (first + TILE, TILE), 0)
    queries = lax.broadcasted_iota(jnp.int32, (first + TILE, TILE), 1) + first
    return (keys <= queries) & (keys >= starts_ref[:, first : first + TILE])


def head_lanes(values, head):
    lanes = lax.broadcasted_iota(jnp.int32, values.shape, 1)
    return jnp.where((lanes >= head * 64) & (lanes < head * 64 + 64), values, jnp.zeros_like(values))


def attend_forward(heads, place_ref, alpha_ref, normed_ref, weight_ref, starts_ref,
                   qkv_ref, weight_out_ref, attended_ref, tau_ref, shifted_ref):
    rows = normed_ref.shape[0]
    if len(weight_ref.shape) == 2:
        weight_out_ref[...] = weight_ref[...]
    else:
        part = weight_ref.shape[2]
        for slot, hop in enumerate(ORDER):
            row = pl.multiple_of((place_ref[0] ^ hop) * part, part)
            weight_out_ref[pl.ds(row, part), :] = weight_ref[slot, 0]
    width = heads * 64
    qkv = dot_nn(normed_ref[...], weight_out_ref[...]).astype(BF16)
    qkv_ref[...] = qkv
    queries = qkv[:, :width]
    keys = qkv[:, width : 2 * width]
    values_t = jnp.transpose(qkv[:, 2 * width :].astype(F32)).astype(BF16)
    tiles = [(h, first) for h in range(heads) for first in range(0, rows, TILE)]
    offsets = []
    total = 0
    for h, first in tiles:
        offsets.append(total)
        total += first + TILE
    lows, brackets = [], []
    for (h, first), offset in zip(tiles, offsets):
        alpha_minus = alpha_ref[h] - 1.0
        query = head_lanes(queries[first : first + TILE], h)
        scores = dot_nt(keys[: first + TILE], query) * 0.125
        shifted = jnp.where(tile_mask(first, starts_ref), alpha_minus * scores, MASKED)
        shifted_ref[offset : offset + first + TILE, :] = shifted
        spots = lax.broadcasted_iota(jnp.int32, (1, TILE), 1) + (first + 1)
        counted = (spots - starts_ref[:, first : first + TILE]).astype(F32)
        highest = jnp.max(shifted, axis=0, keepdims=True)
        low = highest - 1.0
        lows.append(low)
        brackets.append(highest - jnp.exp(-alpha_minus * jnp.log(counted)) - low)

    def bisect(step, carry):
        lows, brackets = carry
        new_lows, new_brackets = [], []
        for (h, first), offset, low, bracket in zip(tiles, offsets, lows, brackets):
            bracket = bracket * 0.5
            middle = low + bracket
            power = 1.0 / ((alpha_ref[h] - 1.0) * LN2)
            margin = jnp.maximum(shifted_ref[offset : offset + first + TILE, :] - middle, 0.0)
            summed = jnp.sum(jnp.exp2(power * jnp.log(margin)), axis=0, keepdims=True)
            new_lows.append(jnp.where(summed >= 1.0, middle, low))
            new_brackets.append(bracket)
        return tuple(new_lows), tuple(new_brackets)

    lows, _ = lax.fori_loop(0, BISECT, bisect, (tuple(lows), tuple(brackets)))
    for (h, first), offset, low in zip(tiles, offsets, lows):
        exponent = 1.0 / (alpha_ref[h] - 1.0)
        shifted = shifted_ref[offset : offset + first + TILE, :]
        margin = jnp.maximum(shifted - low, 0.0)
        slope = jnp.exp2((exponent - 1.0) * (1.0 / LN2) * jnp.log(margin))
        slopes = exponent * jnp.sum(slope, axis=0, keepdims=True)
        summed = jnp.sum(slope * margin, axis=0, keepdims=True)
        tau = low + (summed - 1.0) / slopes
        tau_ref[h : h + 1, first : first + TILE] = tau
        margin = jnp.maximum(shifted - tau, 0.0)
        probs = jnp.exp2(exponent * (1.0 / LN2) * jnp.log(margin)).astype(BF16)
        out = dot_nn(values_t[h * 64 : h * 64 + 64, : first + TILE], probs)
        attended_ref[first : first + TILE, h * 64 : h * 64 + 64] = jnp.transpose(out).astype(BF16)


def attend_backward(heads, place_ref, alpha_ref, normed_ref, qkv_ref, tau_ref, starts_ref, dattended_ref,
                    dqkv_ref, grad_ref, dalpha_ref, dkeys_ref, dvalues_ref):
    rows = normed_ref.shape[0]
    width = heads * 64
    queries = qkv_ref[:, :width]
    keys = qkv_ref[:, width : 2 * width]
    values = qkv_ref[:, 2 * width :]
    keys_t = jnp.transpose(keys.astype(F32)).astype(BF16)
    dkeys_ref[...] = jnp.zeros_like(dkeys_ref)
    dvalues_ref[...] = jnp.zeros_like(dvalues_ref)
    for h in range(heads):
        alpha_minus = alpha_ref[h] - 1.0
        exponent = 1.0 / alpha_minus
        dalpha = jnp.zeros((1, TILE), F32)
        for first in range(0, rows, TILE):
            end = first + TILE
            query = head_lanes(queries[first:end], h)
            dout = head_lanes(dattended_ref[first:end, :], h)
            scores = dot_nt(keys[:end], query) * 0.125
            shifted = jnp.where(tile_mask(first, starts_ref), alpha_minus * scores, MASKED)
            margin = jnp.maximum(shifted - tau_ref[h : h + 1, first:end], 0.0)
            log_margin = jnp.log(margin)
            slope = jnp.exp2((exponent - 1.0) * (1.0 / LN2) * log_margin)
            probs = slope * margin
            slope = exponent * slope
            dprobs = dot_nt(values[:end], dout)
            slope_sum = jnp.sum(slope, axis=0, keepdims=True)
            mixed = jnp.sum(slope * dprobs, axis=0, keepdims=True)
            centred = dprobs - mixed / slope_sum
            log_margin = jnp.where(margin > 0.0, log_margin, 0.0)
            alpha_part = slope * scores - (exponent * exponent) * (probs * log_margin)
            dalpha = dalpha + jnp.sum(alpha_part * centred, axis=0, keepdims=True)
            dscores = (alpha_minus * (slope * centred)).astype(BF16)
            dvalues_ref[:end, :] += dot_nn(probs.astype(BF16), dout)
            dkeys_ref[:end, :] += dot_nn(dscores, query)
            dquery_t = dot_nn(keys_t[h * 64 : h * 64 + 64, :end], dscores) * 0.125
            dqkv_ref[first:end, h * 64 : h * 64 + 64] = jnp.transpose(dquery_t).astype(BF16)
        dalpha_ref[h : h + 1, :] = dalpha
    dqkv_ref[:, width : 2 * width] = (dkeys_ref[...] * 0.125).astype(BF16)
    dqkv_ref[:, 2 * width :] = dvalues_ref[...].astype(BF16)
    grad = dot_tn(normed_ref[...], dqkv_ref[...]).astype(BF16)
    part = grad_ref.shape[1]
    for spot in range(PLANE):
        hop = place_ref[0] ^ spot
        grad_ref[(hop % 2) * 4 + hop // 2] = grad[spot * part : (spot + 1) * part]


def whole(shape):
    return pl.BlockSpec(shape, lambda *_: (0,) * len(shape), memory_space=pltpu.VMEM)


def run_forward(heads, place, alpha, normed, weight, slot, starts):
    rows, width = normed.shape
    columns = 3 * heads * 64
    total = heads * sum(range(TILE, rows + 1, TILE))
    if slot == 0:
        weight_spec = whole(weight.shape)
    else:
        block = (weight.shape[0], 1) + weight.shape[2:]
        weight_spec = pl.BlockSpec(block, lambda _: (0, slot - 1, 0, 0), memory_space=pltpu.VMEM)
    smem = pl.BlockSpec(memory_space=pltpu.SMEM)
    return pl.pallas_call(
        functools.partial(attend_forward, heads),
        out_shape=(
            jax.ShapeDtypeStruct((rows, columns), BF16),
            jax.ShapeDtypeStruct((width, columns), BF16),
            jax.ShapeDtypeStruct((rows, heads * 64), BF16),
            jax.ShapeDtypeStruct((heads, rows), F32),
        ),
        grid=(1,),
        in_specs=[smem, smem, whole(normed.shape), weight_spec, whole(starts.shape)],
        out_specs=(
            whole((rows, columns)),
            whole((width, columns)),
            whole((rows, heads * 64)),
            whole((heads, rows)),
        ),
        scratch_shapes=[pltpu.VMEM((total, TILE), F32)],
        compiler_params=pltpu.CompilerParams(vmem_limit_bytes=VMEM_BYTES),
        cost_estimate=pl.CostEstimate(flops=3 * 10**9, bytes_accessed=2 * 10**6, transcendentals=10**7),
        name="attend_forward",
    )(place, alpha, normed, weight, starts)


def run_backward(heads, place, alpha, normed, qkv, tau, starts, dattended):
    rows, width = normed.shape
    columns = 3 * heads * 64
    smem = pl.BlockSpec(memory_space=pltpu.SMEM)
    return pl.pallas_call(
        functools.partial(attend_backward, heads),
        out_shape=(
            jax.ShapeDtypeStruct((rows, columns), BF16),
            jax.ShapeDtypeStruct((PLANE, width // PLANE, columns), BF16),
            jax.ShapeDtypeStruct((heads, TILE), F32),
        ),
        grid=(1,),
        in_specs=[smem, smem] + [whole(a.shape) for a in (normed, qkv, tau, starts, dattended)],
        out_specs=(
            whole((rows, columns)),
            whole((PLANE, width // PLANE, columns)),
            whole((heads, TILE)),
        ),
        scratch_shapes=[pltpu.VMEM((rows, heads * 64), F32), pltpu.VMEM((rows, heads * 64), F32)],
        compiler_params=pltpu.CompilerParams(vmem_limit_bytes=VMEM_BYTES),
        cost_estimate=pl.CostEstimate(flops=3 * 10**9, bytes_accessed=2 * 10**6, transcendentals=10**7),
        name="attend_backward",
    )(place, alpha, normed, qkv, tau, starts, dattended)


def solution(mesh):
    batch_size = mesh.shape["batch"]
    tensor_size = mesh.shape["tensor"]

    def over_batch(array, hop):
        return lax.ppermute(array, "batch", [(i, i ^ hop) for i in range(batch_size)])

    def over_tensor(array, hop):
        return lax.ppermute(array, "tensor", [(i, i ^ hop) for i in range(tensor_size)])

    def gather_plane(array):
        across = jnp.stack([array] + [over_batch(array, hop) for hop in (2, 4, 6)])
        return jnp.concatenate([across, over_batch(across, 1)])

    def gather_weight(part):
        received = jnp.stack([over_tensor(part, hop) for hop in range(1, tensor_size)])
        return gather_plane(received)

    def reduce_all(grads):
        half = (grads[:, :4].astype(F32) + over_batch(grads[:, 4:], 1).astype(F32)).astype(BF16)
        across = [over_batch(half[:, hop // 2], hop).astype(F32) for hop in (2, 4, 6)]
        quarter = (half[:, 0].astype(F32) + across[0]) + (across[1] + across[2])
        hop = PLANE
        while hop < batch_size:
            quarter = quarter + over_batch(quarter.astype(BF16), hop).astype(F32)
            hop *= 2
        quarter = quarter.astype(BF16)
        lines = [over_tensor(quarter[hop], hop).astype(F32) for hop in range(1, tensor_size)]
        return (quarter[0].astype(F32) + lines[0]) + (lines[1] + lines[2])

    def sum_small(array):
        hops = [array] + [over_batch(array, hop) for hop in range(1, PLANE)]
        array = ((hops[0] + hops[1]) + (hops[2] + hops[3])) + ((hops[4] + hops[5]) + (hops[6] + hops[7]))
        hop = PLANE
        while hop < batch_size:
            array = array + over_batch(array, hop)
            hop *= 2
        return array

    def shards(inputs, doc_lengths, ln1_gain, ln1_bias, w_qkv, entmax_alpha, w_out, ln2_gain, ln2_bias,
               w_up, up_bias, w_down, down_bias, cotangent):
        seq_count, length, width = inputs.shape
        heads = entmax_alpha.shape[0]
        hidden = w_up.shape[1]
        rows = length // 2
        columns = heads * 64
        place = lax.axis_index("batch") % PLANE
        line = lax.axis_index("tensor")
        hops = [place ^ hop for hop in ORDER]

        ends = jnp.cumsum(doc_lengths, axis=1)
        firsts = ends - doc_lengths
        big = jnp.sum(jnp.where(doc_lengths == rows, firsts, 0), axis=1)

        def unit_start(unit):
            return (jnp.take(big, unit // 2) + rows * (unit % 2)) % length

        start = unit_start(line)
        doc_places = (jnp.take(firsts, line // 2, axis=0) - start) % length
        spots = jnp.arange(rows, dtype=jnp.int32)
        starts = jnp.max(
            jnp.where(doc_places[:, None] <= spots[None, :], doc_places[:, None], 0), axis=0, keepdims=True
        )

        def own_rows(array):
            one = lax.dynamic_index_in_dim(array, line // 2, 0, keepdims=False)
            return lax.dynamic_slice_in_dim(jnp.concatenate([one, one[:rows]]), start, rows)

        def relative(array):
            parts = array.reshape((PLANE, array.shape[0] // PLANE) + array.shape[1:])
            return jnp.concatenate([lax.dynamic_index_in_dim(parts, hop, 0, keepdims=False) for hop in hops])

        def own_part(array):
            return lax.dynamic_slice_in_dim(array, place * (array.shape[0] // PLANE), array.shape[0] // PLANE)

        def natural(parts):
            spots = [(spot ^ place) for spot in range(PLANE)]
            return jnp.concatenate(
                [
                    lax.dynamic_index_in_dim(parts, (spot % 2) * 4 + spot // 2, 0, keepdims=False)
                    for spot in spots
                ]
            )

        qkv_own = jnp.transpose(w_qkv, (1, 0, 2)).reshape(width, 3 * columns)
        up_own = jnp.transpose(w_up)
        qkv_far = gather_weight(own_part(qkv_own))
        rest_far = gather_weight(jnp.concatenate([own_part(w_out), own_part(up_own), own_part(w_down)]))
        small = jnp.concatenate([up_bias, entmax_alpha])
        small_far = [over_tensor(small, hop) for hop in range(1, tensor_size)]
        alphas = [entmax_alpha] + [far[hidden:] for far in small_far]
        out_part = w_out.shape[0] // PLANE
        up_part = hidden // PLANE

        tokens = own_rows(inputs).astype(F32)
        cot_low = own_rows(cotangent)
        normed_one, pull_one = jax.vjp(layer_norm, tokens, ln1_gain, ln1_bias)
        normed_low = normed_one.astype(BF16)
        place_ref = place.reshape(1)

        qkvs, weights, attendeds, taus = [], [], [], []
        for slot in range(tensor_size):
            qkv, weight, attended, tau = run_forward(
                heads, place_ref, alphas[slot], normed_low, qkv_own if slot == 0 else qkv_far, slot, starts
            )
            qkvs.append(qkv)
            weights.append(weight)
            attendeds.append(attended)
            taus.append(tau)

        out_weights = jnp.concatenate(
            [w_out] + [natural(rest_far[:, hop, :out_part]) for hop in range(tensor_size - 1)]
        )
        up_weights = jnp.concatenate(
            [relative(up_own)]
            + [
                rest_far[:, hop, out_part : out_part + up_part].reshape(hidden, width)
                for hop in range(tensor_size - 1)
            ]
        )
        down_weights = jnp.concatenate(
            [relative(w_down)]
            + [rest_far[:, hop, out_part + up_part :].reshape(hidden, width) for hop in range(tensor_size - 1)]
        )
        up_biases = jnp.concatenate([relative(up_bias)] + [relative(far[:hidden]) for far in small_far])
        attended = jnp.concatenate(attendeds, axis=1)

        resid = tokens + dot_nn(attended, out_weights)
        normed_two, pull_two = jax.vjp(layer_norm, resid, ln2_gain, ln2_bias)
        normed_low_two = normed_two.astype(BF16)
        pre_act = dot_nt(normed_low_two, up_weights) + up_biases
        act, pull_gelu = jax.vjp(gelu_tanh, pre_act)
        act_low = act.astype(BF16)
        out_low = (resid + dot_nn(act_low, down_weights) + down_bias).astype(BF16)

        def gather_units(chunk):
            far = [chunk] + [over_tensor(chunk, hop) for hop in range(1, tensor_size)]
            here = jnp.concatenate(far[:2])
            there = jnp.concatenate(far[2:])
            here = jnp.roll(here, start, axis=0)
            there = jnp.roll(there, unit_start(line ^ 2), axis=0)
            first = line // 2 == 0
            return jnp.stack([jnp.where(first, here, there), jnp.where(first, there, here)])

        output = gather_units(out_low)

        grad_down = dot_tn(act_low, cot_low).astype(BF16)
        cot_full = cot_low.astype(F32)
        dact = dot_nt(cot_low, down_weights)
        dpre = pull_gelu(dact)[0].astype(BF16)
        grad_up = dot_tn(dpre, normed_low_two).astype(BF16)
        dnormed_two = dot_nn(dpre, up_weights)
        dresid_part, grad_ln2_gain, grad_ln2_bias = pull_two(dnormed_two)
        dresid = cot_full + dresid_part
        dresid_low = dresid.astype(BF16)
        dattended = dot_nt(dresid_low, out_weights).astype(BF16)
        grad_out = dot_tn(attended, dresid_low).astype(BF16)

        grad_qkv, dqkvs, dalphas = [], [], []
        for slot in range(tensor_size):
            dqkv, grad, dalpha = run_backward(
                heads, place_ref, alphas[slot], normed_low, qkvs[slot], taus[slot], starts,
                dattended[:, slot * columns : (slot + 1) * columns],
            )
            dqkvs.append(dqkv)
            grad_qkv.append(grad)
            dalphas.append(jnp.sum(dalpha, axis=1))
        dnormed_one = dot_nt(jnp.concatenate(dqkvs, axis=1), jnp.concatenate(weights, axis=1))
        dinput_part, grad_ln1_gain, grad_ln1_bias = pull_one(dnormed_one)
        grad_input = gather_units((dresid + dinput_part).astype(BF16))

        def by_part(array):
            return array.reshape(tensor_size, PLANE, array.shape[0] // (tensor_size * PLANE), array.shape[1])

        grad_ffn = jnp.concatenate([by_part(grad_up), by_part(grad_down)], axis=2)
        ffn_sum = gather_plane(reduce_all(grad_ffn).astype(BF16))
        qkv_sum = gather_plane(reduce_all(jnp.stack(grad_qkv)).astype(BF16))
        out_parts = by_part(grad_out)
        out_parts = jnp.stack([relative(out_parts[slot]) for slot in range(tensor_size)])
        out_sum = gather_plane(reduce_all(out_parts).astype(BF16))
        grad_w_up = jnp.transpose(natural(ffn_sum[:, :up_part]).astype(F32))
        grad_w_down = natural(ffn_sum[:, up_part:]).astype(F32)
        grad_w_qkv = jnp.transpose(natural(qkv_sum).astype(F32).reshape(width, 3, columns), (1, 0, 2))
        grad_w_out = natural(out_sum).astype(F32)

        grad_bias = jnp.sum(dpre.astype(F32), axis=0).reshape(tensor_size, PLANE, up_part)
        grad_bias = jnp.stack([natural(grad_bias[slot]) for slot in range(tensor_size)])
        common = jnp.concatenate(
            [grad_ln1_gain, grad_ln1_bias, grad_ln2_gain, grad_ln2_bias, jnp.sum(cot_full, axis=0)]
        )
        lines = jnp.concatenate([grad_bias, jnp.stack(dalphas)], axis=1)
        small_sum = sum_small(jnp.concatenate([common, lines.reshape(-1)]))
        common = small_sum[: 5 * width]
        lines = small_sum[5 * width :].reshape(tensor_size, hidden + heads)
        commons = [common] + [over_tensor(common, hop) for hop in range(1, tensor_size)]
        common = ((commons[0] + commons[1]) + (commons[2] + commons[3])).reshape(5, width)
        own = [lines[0]] + [over_tensor(lines[hop], hop) for hop in range(1, tensor_size)]
        own = (own[0] + own[1]) + (own[2] + own[3])
        return (
            output,
            grad_input,
            common[0],
            common[1],
            grad_w_qkv,
            own[hidden:],
            grad_w_out,
            common[2],
            common[3],
            grad_w_up,
            own[:hidden],
            grad_w_down,
            common[4],
        )

    return jax.shard_map(
        shards,
        mesh=mesh,
        in_specs=(
            P("batch", None, None),
            P("batch", None),
            P(),
            P(),
            P(None, None, "tensor"),
            P("tensor"),
            P("tensor", None),
            P(),
            P(),
            P(None, "tensor"),
            P("tensor"),
            P("tensor", None),
            P(),
            P("batch", None, None),
        ),
        out_specs=(
            P("batch", None, None),
            P("batch", None, None),
            P(),
            P(),
            P(None, None, "tensor"),
            P("tensor"),
            P("tensor", None),
            P(),
            P(),
            P(None, "tensor"),
            P("tensor"),
            P("tensor", None),
            P(),
        ),
        check_vma=False,
    )
```

```python
import functools

import jax
import jax.numpy as jnp
from jax import lax
from jax.experimental import pallas as pl
from jax.experimental.pallas import tpu as pltpu
from jax.sharding import PartitionSpec as P

BISECT = 10
MASKED = -10000.0
NORM_EPS = 1e-05
LN2 = 0.6931471805599453
TILE = 128
EXTRA = 16
PLANE = 8
MIB = 1024 * 1024
BF16 = jnp.bfloat16
F32 = jnp.float32
GELU_A = 0.7978845608028654
GELU_B = 0.044715


def layer_norm(values, norm_gain, norm_shift):
    centre = values - jnp.mean(values, axis=-1, keepdims=True)
    spread = jnp.mean(centre * centre, axis=-1, keepdims=True)
    return centre * lax.rsqrt(spread + NORM_EPS) * norm_gain + norm_shift


def dot_nt(left, right):
    return lax.dot_general(left, right, (((1,), (1,)), ((), ())), preferred_element_type=F32)


def dot_nn(left, right):
    return lax.dot_general(left, right, (((1,), (0,)), ((), ())), preferred_element_type=F32)


def dot_tn(left, right):
    return lax.dot_general(left, right, (((0,), (0,)), ((), ())), preferred_element_type=F32)


def tile_mask(first, starts_ref):
    keys = lax.broadcasted_iota(jnp.int32, (first + TILE, TILE), 0)
    queries = lax.broadcasted_iota(jnp.int32, (first + TILE, TILE), 1) + first
    return (keys <= queries) & (keys >= starts_ref[:, first : first + TILE])


def head_lanes(values, head):
    lanes = lax.broadcasted_iota(jnp.int32, values.shape, 1)
    return jnp.where((lanes >= head * 64) & (lanes < head * 64 + 64), values, jnp.zeros_like(values))


def rolled(values, shift, rows):
    return pltpu.roll(values, shift, 0)[:rows]


def prepare(scalars_ref, inputs_ref, cotangent_ref, gain_ref, bias_ref, tokens_ref, cot_ref, normed_ref):
    rows, length = tokens_ref.shape[0], inputs_ref.shape[1]
    shift = length - scalars_ref[5]
    tokens = rolled(inputs_ref[0].astype(F32), shift, rows)
    tokens_ref[...] = tokens.astype(BF16)
    normed_ref[...] = layer_norm(tokens, gain_ref[...], bias_ref[...]).astype(BF16)
    cot_ref[...] = rolled(cotangent_ref[0].astype(F32), shift, rows).astype(BF16)


def pack_qkv(place_ref, weight_ref, bias_ref, alpha_ref, out_ref):
    part, columns = weight_ref.shape[1:]
    for index in range(3):
        out_ref[:part, index * columns : (index + 1) * columns] = weight_ref[index]
    rest = jnp.concatenate([bias_ref[:, 3 * columns :], alpha_ref[...]], axis=1)
    rest = jnp.concatenate([rest, jnp.zeros((1, 3 * columns - rest.shape[1]), F32)], axis=1)
    values = jnp.concatenate([bias_ref[:, : 3 * columns], rest])
    high = values.astype(BF16).astype(F32)
    middle = (values - high).astype(BF16).astype(F32)
    low = values - high - middle
    blank = jnp.zeros((EXTRA - 6, 3 * columns), F32)
    out_ref[part:, :] = jnp.concatenate([high, middle, low, blank]).astype(BF16)


def pack_rest(place_ref, out_weight_ref, up_ref, down_ref, *refs):
    part_ref, turned_ref, turn_ref = refs[-3:]
    out_part = out_weight_ref.shape[0]
    up_part = down_ref.shape[0]
    turn_ref[...] = jnp.transpose(up_ref[...].astype(F32))
    turned_ref[...] = turn_ref[...].astype(BF16)
    rows = pl.ds(pl.multiple_of(place_ref[0] * up_part, up_part), up_part)
    part_ref[:out_part, :] = out_weight_ref[...]
    part_ref[out_part : out_part + up_part, :] = turn_ref[rows, :].astype(BF16)
    part_ref[out_part + up_part :, :] = down_ref[...]


def stack_four(*refs):
    for index in range(4):
        refs[-1][index] = refs[index][...]


def assemble(scalars_ref, own_ref, right_one, left_one, right_two, left_two, far_ref, *refs):
    out_ref, both_ref = refs[-2:]
    pair = pl.program_id(0)
    rows = own_ref.shape[0]
    sources = ((own_ref, 0), (right_one, -1), (left_one, 1), (right_two, -2), (left_two, 2), (far_ref, 3), (far_ref, -3))
    for half in range(2):
        away = 2 * pair + half - scalars_ref[2]
        for ref, distance in sources:

            @pl.when(away == distance)
            def _():
                both_ref[half * rows : (half + 1) * rows, :] = ref[...].astype(F32)

    out_ref[0] = pltpu.roll(both_ref[...], scalars_ref[3 + pair], 0).astype(BF16)


def add_parts(keep_ref, sent_ref, *out_refs):
    for index, ref in enumerate(out_refs):

        @pl.when(pl.program_id(0) == index)
        def _():
            ref[...] = (keep_ref[0].astype(F32) + sent_ref[0].astype(F32)).astype(BF16)


def attend_forward(heads, weight_count, dep_count, scalars_ref, alpha_ref, normed_ref, starts_ref, *refs):
    weight_refs = refs[:weight_count]
    qkv_ref, weight_out_ref, attended_ref, tau_ref, shifted_ref = refs[weight_count + dep_count :]
    rows = normed_ref.shape[0]
    if weight_count == 1:
        (weight_ref,) = weight_refs
        for index in range(3):
            weight_out_ref[:, index * heads * 64 : (index + 1) * heads * 64] = weight_ref[index]
    else:
        for core, weight_ref in enumerate(weight_refs):
            part = weight_ref.shape[2]
            for chip in range(4):
                row = pl.multiple_of((scalars_ref[0] ^ (2 * chip + core)) * part, part)
                weight_out_ref[pl.ds(row, part), :] = weight_ref[chip, 0]
    width = heads * 64
    qkv = dot_nn(normed_ref[...], weight_out_ref[...]).astype(BF16)
    qkv_ref[...] = qkv
    queries = qkv[:, :width]
    keys = qkv[:, width : 2 * width]
    values_t = jnp.transpose(qkv[:, 2 * width :].astype(F32)).astype(BF16)
    tiles = [(h, first) for h in range(heads) for first in range(0, rows, TILE)]
    offsets = []
    total = 0
    for h, first in tiles:
        offsets.append(total)
        total += first + TILE
    lows, brackets = [], []
    for (h, first), offset in zip(tiles, offsets):
        alpha_minus = alpha_ref[h] - 1.0
        query = head_lanes(queries[first : first + TILE], h)
        scores = dot_nt(keys[: first + TILE], query) * 0.125
        shifted = jnp.where(tile_mask(first, starts_ref), alpha_minus * scores, MASKED)
        shifted_ref[offset : offset + first + TILE, :] = shifted
        spots = lax.broadcasted_iota(jnp.int32, (1, TILE), 1) + (first + 1)
        counted = (spots - starts_ref[:, first : first + TILE]).astype(F32)
        highest = jnp.max(shifted, axis=0, keepdims=True)
        low = highest - 1.0
        lows.append(low)
        brackets.append(highest - jnp.exp(-alpha_minus * jnp.log(counted)) - low)

    def bisect(step, carry):
        lows, brackets = carry
        new_lows, new_brackets = [], []
        for (h, first), offset, low, bracket in zip(tiles, offsets, lows, brackets):
            bracket = bracket * 0.5
            middle = low + bracket
            power = 1.0 / ((alpha_ref[h] - 1.0) * LN2)
            margin = jnp.maximum(shifted_ref[offset : offset + first + TILE, :] - middle, 0.0)
            summed = jnp.sum(jnp.exp2(power * jnp.log(margin)), axis=0, keepdims=True)
            new_lows.append(jnp.where(summed >= 1.0, middle, low))
            new_brackets.append(bracket)
        return tuple(new_lows), tuple(new_brackets)

    lows, _ = lax.fori_loop(0, BISECT, bisect, (tuple(lows), tuple(brackets)))
    for (h, first), offset, low in zip(tiles, offsets, lows):
        exponent = 1.0 / (alpha_ref[h] - 1.0)
        shifted = shifted_ref[offset : offset + first + TILE, :]
        margin = jnp.maximum(shifted - low, 0.0)
        slope = jnp.exp2((exponent - 1.0) * (1.0 / LN2) * jnp.log(margin))
        slopes = exponent * jnp.sum(slope, axis=0, keepdims=True)
        summed = jnp.sum(slope * margin, axis=0, keepdims=True)
        tau = low + (summed - 1.0) / slopes
        tau_ref[h : h + 1, first : first + TILE] = tau
        margin = jnp.maximum(shifted - tau, 0.0)
        probs = jnp.exp2(exponent * (1.0 / LN2) * jnp.log(margin)).astype(BF16)
        out = dot_nn(values_t[h * 64 : h * 64 + 64, : first + TILE], probs)
        attended_ref[first : first + TILE, h * 64 : h * 64 + 64] = jnp.transpose(out).astype(BF16)


def attend_backward(heads, scalars_ref, alpha_ref, normed_ref, qkv_ref, tau_ref, starts_ref, dattended_ref, *refs):
    dqkv_ref, keep_ref, send_ref, dalpha_ref, dkeys_ref, dvalues_ref, grad_ref = refs[-7:]
    rows = normed_ref.shape[0]
    width = heads * 64
    queries = qkv_ref[:, :width]
    keys = qkv_ref[:, width : 2 * width]
    values = qkv_ref[:, 2 * width :]
    keys_t = jnp.transpose(keys.astype(F32)).astype(BF16)
    dkeys_ref[...] = jnp.zeros_like(dkeys_ref)
    dvalues_ref[...] = jnp.zeros_like(dvalues_ref)
    for h in range(heads):
        alpha_minus = alpha_ref[h] - 1.0
        exponent = 1.0 / alpha_minus
        dalpha = jnp.zeros((1, TILE), F32)
        for first in range(0, rows, TILE):
            end = first + TILE
            query = head_lanes(queries[first:end], h)
            dout = head_lanes(dattended_ref[first:end, :], h)
            scores = dot_nt(keys[:end], query) * 0.125
            shifted = jnp.where(tile_mask(first, starts_ref), alpha_minus * scores, MASKED)
            margin = jnp.maximum(shifted - tau_ref[h : h + 1, first:end], 0.0)
            log_margin = jnp.log(margin)
            slope = jnp.exp2((exponent - 1.0) * (1.0 / LN2) * log_margin)
            probs = slope * margin
            slope = exponent * slope
            dprobs = dot_nt(values[:end], dout)
            slope_sum = jnp.sum(slope, axis=0, keepdims=True)
            mixed = jnp.sum(slope * dprobs, axis=0, keepdims=True)
            centred = dprobs - mixed / slope_sum
            log_margin = jnp.where(margin > 0.0, log_margin, 0.0)
            alpha_part = slope * scores - (exponent * exponent) * (probs * log_margin)
            dalpha = dalpha + jnp.sum(alpha_part * centred, axis=0, keepdims=True)
            dscores = (alpha_minus * (slope * centred)).astype(BF16)
            dvalues_ref[:end, :] += dot_nn(probs.astype(BF16), dout)
            dkeys_ref[:end, :] += dot_nn(dscores, query)
            dquery_t = dot_nn(keys_t[h * 64 : h * 64 + 64, :end], dscores) * 0.125
            dqkv_ref[first:end, h * 64 : h * 64 + 64] = jnp.transpose(dquery_t).astype(BF16)
        dalpha_ref[h : h + 1, :] = dalpha
    dqkv_ref[:, width : 2 * width] = (dkeys_ref[...] * 0.125).astype(BF16)
    dqkv_ref[:, 2 * width :] = dvalues_ref[...].astype(BF16)
    grad = dot_tn(normed_ref[...], dqkv_ref[...]).astype(BF16)
    grad_ref[...] = grad.reshape(grad_ref.shape)
    for chip in range(4):
        keep_ref[chip] = grad_ref[scalars_ref[0] ^ (2 * chip)]
        send_ref[chip] = grad_ref[scalars_ref[0] ^ (2 * chip + 1)]


def norm_back(values, gain, dnormed):
    centre = values - jnp.mean(values, axis=-1, keepdims=True)
    scale = lax.rsqrt(jnp.mean(centre * centre, axis=-1, keepdims=True) + NORM_EPS)
    unit = centre * scale
    scaled = dnormed * gain
    mean = jnp.mean(scaled, axis=-1, keepdims=True)
    mixed = jnp.mean(scaled * unit, axis=-1, keepdims=True)
    dvalues = scale * (scaled - mean - unit * mixed)
    return dvalues, jnp.sum(dnormed * unit, axis=0, keepdims=True), jnp.sum(dnormed, axis=0, keepdims=True)


def feed_forward(slots, scalars_ref, tokens_ref, cot_ref, gain_ref, bias_ref, up_bias_ref, down_bias_ref, *refs):
    attended_refs = refs[:slots]
    out_own, up_own, down_own, far_zero, far_one = refs[slots : slots + 5]
    out_ref, dresid_ref, dattended_ref, keep_ref, send_ref, small_ref = refs[slots + 5 : slots + 11]
    w_out, w_up, w_down, sums, dnormed_ref, grad_out, grad_up, grad_down, copies = refs[slots + 11 :]
    place = scalars_ref[0]
    out_part = w_out.shape[1] // PLANE
    up_part = w_up.shape[1] // PLANE
    moves = [(out_own, w_out.at[0]), (up_own, w_up.at[0]), (down_own, w_down.at[0])]
    for core, far in enumerate((far_zero, far_one)):
        for chip in range(4):
            spot = place ^ (2 * chip + core)
            out_rows = pl.ds(pl.multiple_of(spot * out_part, out_part), out_part)
            up_rows = pl.ds(pl.multiple_of(spot * up_part, up_part), up_part)
            moves.append((far.at[chip, :, :out_part], w_out.at[1:, out_rows]))
            moves.append((far.at[chip, :, out_part : out_part + up_part], w_up.at[1:, up_rows]))
            moves.append((far.at[chip, :, out_part + up_part :], w_down.at[1:, up_rows]))
    started = []
    for index, (source, target) in enumerate(moves):
        copy = pltpu.make_async_copy(source, target, copies.at[index])
        copy.start()
        started.append(copy)
    for copy in started:
        copy.wait()

    width = tokens_ref.shape[1]
    attended = jnp.concatenate([ref[...] for ref in attended_refs], axis=1)
    out_weights = w_out[...].reshape(slots * w_out.shape[1], width)
    resid = tokens_ref[...].astype(F32) + dot_nn(attended, out_weights)
    sums[...] = resid
    normed = layer_norm(resid, gain_ref[...], bias_ref[...]).astype(BF16)
    dnormed_ref[...] = jnp.zeros_like(dnormed_ref)
    cot = cot_ref[...]
    for slot in range(slots):
        pre = dot_nt(normed, w_up[slot]) + up_bias_ref[slot : slot + 1, :]
        square = pre * pre
        bend = jnp.tanh(pre * (GELU_A + GELU_A * GELU_B * square))
        half = 0.5 + 0.5 * bend
        act = (pre * half).astype(BF16)
        slope = half + (0.5 * pre) * (1.0 - bend * bend) * (GELU_A + 3.0 * GELU_A * GELU_B * square)
        sums[...] += dot_nn(act, w_down[slot])
        dpre = (dot_nt(cot, w_down[slot]) * slope).astype(BF16)
        small_ref[3 + slot : 4 + slot, :] = jnp.sum(dpre.astype(F32), axis=0, keepdims=True)
        dnormed_ref[...] += dot_nn(dpre, w_up[slot])
        grad_down[slot] = dot_tn(act, cot).astype(BF16).reshape(PLANE, up_part, width)
        grad_up[slot] = dot_tn(dpre, normed).astype(BF16).reshape(PLANE, up_part, width)
    out_ref[...] = (sums[...] + down_bias_ref[...]).astype(BF16)
    dresid, small_ref[0:1, :], small_ref[1:2, :] = norm_back(resid, gain_ref[...], dnormed_ref[...])
    cot_full = cot.astype(F32)
    small_ref[2:3, :] = jnp.sum(cot_full, axis=0, keepdims=True)
    dresid = cot_full + dresid
    dresid_ref[...] = dresid
    dresid_low = dresid.astype(BF16)
    dattended_ref[...] = dot_nt(dresid_low, out_weights).astype(BF16)
    grad_out[...] = dot_tn(attended, dresid_low).astype(BF16).reshape(grad_out.shape)
    for core, target in enumerate((keep_ref, send_ref)):
        for chip in range(4):
            spot = place ^ (2 * chip + core)
            for slot in range(slots):
                target[chip, slot, :out_part] = grad_out[slot, spot]
                target[chip, slot, out_part : out_part + up_part] = grad_up[slot, spot]
                target[chip, slot, out_part + up_part :] = grad_down[slot, spot]


def finish(slots, tokens_ref, dresid_ref, gain_ref, *refs):
    dqkv = jnp.concatenate([ref[...] for ref in refs[:slots]], axis=1)
    weights = jnp.concatenate([ref[...] for ref in refs[slots : 2 * slots]], axis=1)
    out_ref, small_ref = refs[-2:]
    dnormed = dot_nt(dqkv, weights)
    dinput, small_ref[0:1, :], small_ref[1:2, :] = norm_back(
        tokens_ref[...].astype(F32), gain_ref[...], dnormed
    )
    out_ref[...] = (dresid_ref[...] + dinput).astype(BF16)


def unpack(out_part, up_part, scalars_ref, zero_ref, one_ref, qkv_ref, out_ref, up_ref, down_ref, turn_ref):
    columns = qkv_ref.shape[2]
    for core, ref in enumerate((zero_ref, one_ref)):
        for chip in range(4):
            spot = scalars_ref[0] ^ (2 * chip + core)
            out_rows = pl.ds(pl.multiple_of(spot * out_part, out_part), out_part)
            up_rows = pl.ds(pl.multiple_of(spot * up_part, up_part), up_part)
            first = out_part
            out_ref[out_rows, :] = ref[chip, :first].astype(F32)
            turn_ref[up_rows, :] = ref[chip, first : first + up_part].astype(F32)
            first = first + up_part
            down_ref[up_rows, :] = ref[chip, first : first + up_part].astype(F32)
            first = first + up_part
            part = ref.shape[1] - first
            qkv_rows = pl.ds(pl.multiple_of(spot * part, part), part)
            for index in range(3):
                qkv_ref[index, qkv_rows, :] = ref[chip, first:, index * columns : (index + 1) * columns].astype(F32)
    up_ref[...] = jnp.transpose(turn_ref[...])


def whole(shape):
    return pl.BlockSpec(shape, lambda *_: (0,) * len(shape), memory_space=pltpu.VMEM)


def kernel_call(body, name, scalars, operands, in_specs, out_shapes, scratch=(), out_specs=None, grid=1, flops=10**9, vmem=16):
    spec = pltpu.PrefetchScalarGridSpec(
        num_scalar_prefetch=len(scalars),
        grid=(grid,),
        in_specs=in_specs,
        out_specs=out_specs or tuple(whole(shape.shape) for shape in out_shapes),
        scratch_shapes=list(scratch),
    )
    return pl.pallas_call(
        body,
        out_shape=tuple(out_shapes),
        grid_spec=spec,
        compiler_params=pltpu.CompilerParams(vmem_limit_bytes=vmem * MIB),
        cost_estimate=pl.CostEstimate(flops=flops, bytes_accessed=10**6, transcendentals=0),
        name=name,
    )(*scalars, *operands)


def shaped(*shape, dtype=BF16):
    return jax.ShapeDtypeStruct(shape, dtype)


ANYWHERE = pl.BlockSpec(memory_space=pl.ANY)


def run_forward(heads, scalars, alpha, normed, weights, slot, starts, deps):
    rows, width = normed.shape
    columns = 3 * heads * 64
    total = heads * sum(range(TILE, rows + 1, TILE))
    if slot == 0:
        weight_specs = [whole(weights[0].shape)]
    else:
        block = (4, 1) + weights[0].shape[2:]
        weight_specs = [pl.BlockSpec(block, lambda *_: (0, slot - 1, 0, 0), memory_space=pltpu.VMEM)] * 2
    smem = pl.BlockSpec(memory_space=pltpu.SMEM)
    return kernel_call(
        functools.partial(attend_forward, heads, len(weights), len(deps)),
        "attend_forward",
        [scalars],
        [alpha, normed, starts, *weights, *deps],
        [smem, whole(normed.shape), whole(starts.shape)] + weight_specs + [ANYWHERE] * len(deps),
        [
            shaped(rows, columns),
            shaped(width, columns),
            shaped(rows, heads * 64),
            shaped(heads, rows, dtype=F32),
        ],
        [pltpu.VMEM((total, TILE), F32)],
        flops=5 * 10**9,
    )


def run_backward(heads, scalars, alpha, normed, qkv, tau, starts, dattended, slot, deps):
    rows, width = normed.shape
    columns = 3 * heads * 64
    smem = pl.BlockSpec(memory_space=pltpu.SMEM)
    dattended_spec = pl.BlockSpec((rows, heads * 64), lambda *_: (0, slot), memory_space=pltpu.VMEM)
    parts = (width // PLANE, columns)
    return kernel_call(
        functools.partial(attend_backward, heads),
        "attend_backward",
        [scalars],
        [alpha, normed, qkv, tau, starts, dattended, *deps],
        [smem] + [whole(a.shape) for a in (normed, qkv, tau, starts)] + [dattended_spec] + [ANYWHERE] * len(deps),
        [
            shaped(rows, columns),
            shaped(4, *parts),
            shaped(4, *parts),
            shaped(heads, TILE, dtype=F32),
        ],
        [
            pltpu.VMEM((rows, heads * 64), F32),
            pltpu.VMEM((rows, heads * 64), F32),
            pltpu.VMEM((PLANE,) + parts, BF16),
        ],
        flops=4 * 10**9,
    )


def split_wide(values):
    high = lax.reduce_precision(values, exponent_bits=8, mantissa_bits=7)
    return jnp.concatenate([high.astype(BF16), (values - high).astype(BF16)])


def join_wide(pair):
    pair = pair.astype(F32)
    half = pair.shape[0] // 2
    return pair[:half] + pair[half:]


def solution(mesh):
    batch_size = mesh.shape["batch"]
    tensor_size = mesh.shape["tensor"]

    def over_batch(array, hop):
        return lax.ppermute(array, "batch", [(i, i ^ hop) for i in range(batch_size)])

    def over_tensor(array, hop):
        return lax.ppermute(array, "tensor", [(i, i ^ hop) for i in range(tensor_size)])

    def line_gather(part):
        return [over_tensor(part, hop) for hop in range(1, tensor_size)]

    def chip_gather(part):
        return [part] + [over_batch(part, hop) for hop in (2, 4, 6)]

    def upper_sum(array, split):
        hop = PLANE
        while hop < batch_size:
            array = array + join(over_batch(cut(array, split), hop), split)
            hop *= 2
        return array

    def cut(array, split):
        return split_wide(array) if split else array.astype(BF16)

    def join(array, split):
        return join_wide(array) if split else array.astype(F32)

    def tree(four):
        return (four[0] + four[1]) + (four[2] + four[3])

    def shards(inputs, doc_lengths, ln1_gain, ln1_bias, w_qkv, entmax_alpha, w_out, ln2_gain, ln2_bias,
               w_up, up_bias, w_down, down_bias, cotangent):
        seq_count, length, width = inputs.shape
        heads = entmax_alpha.shape[0]
        hidden = w_up.shape[1]
        rows = length // 2
        columns = heads * 64
        place = lax.axis_index("batch") % PLANE
        line = lax.axis_index("tensor")

        def own_part(array):
            return lax.dynamic_slice_in_dim(array, place * (array.shape[0] // PLANE), array.shape[0] // PLANE)

        out_part = w_out.shape[0] // PLANE
        up_part = hidden // PLANE
        part = width // PLANE
        span = 3 * columns
        rest_rows = out_part + 2 * up_part
        spot = place.reshape(1).astype(jnp.int32)
        row = lambda array: array.reshape(1, -1)
        by_place = lambda rows: pl.BlockSpec((rows, width), lambda i, ref: (ref[0], 0), memory_space=pltpu.VMEM)

        (qkv_part,) = kernel_call(
            pack_qkv,
            "pack_qkv",
            [spot],
            [w_qkv, row(up_bias), jnp.pad(row(entmax_alpha), ((0, 0), (0, TILE - heads)))],
            [
                pl.BlockSpec((3, part, columns), lambda i, ref: (0, ref[0], 0), memory_space=pltpu.VMEM),
                whole((1, hidden)),
                whole((1, TILE)),
            ],
            [shaped(part + EXTRA, span)],
        )
        qkv_line = line_gather(qkv_part)
        extras = [far[part : part + 6].astype(F32) for far in qkv_line]
        extras = [(far[:2] + far[2:4] + far[4:]).reshape(-1) for far in extras]
        alphas = [entmax_alpha] + [far[hidden : hidden + heads] for far in extras]
        up_biases = jnp.stack([up_bias] + [far[:hidden] for far in extras])
        qkv_far = chip_gather(jnp.stack([far[:part] for far in qkv_line]))

        ends = jnp.cumsum(doc_lengths, axis=1)
        firsts = ends - doc_lengths
        big = jnp.sum(jnp.where(doc_lengths == rows, firsts, 0), axis=1)

        def unit_start(unit):
            return (jnp.take(big, unit // 2) + rows * (unit % 2)) % length

        start = unit_start(line)
        doc_places = (jnp.take(firsts, line // 2, axis=0) - start) % length
        spots = jnp.arange(rows, dtype=jnp.int32)
        starts = jnp.max(
            jnp.where(doc_places[:, None] <= spots[None, :], doc_places[:, None], 0), axis=0, keepdims=True
        )
        scalars = jnp.stack([place, line // 2, line, big[0], big[1], start]).astype(jnp.int32)

        rest_part, up_own = kernel_call(
            pack_rest,
            "pack_rest",
            [spot],
            [w_out, w_up, w_down, *qkv_line],
            [by_place(out_part), whole(w_up.shape), by_place(up_part)] + [ANYWHERE] * len(qkv_line),
            [shaped(rest_rows, width), shaped(hidden, width)],
            [pltpu.VMEM((hidden, width), F32)],
        )
        rest_line = line_gather(rest_part)

        sequence = pl.BlockSpec((1, length, width), lambda i, ref: (ref[1], 0, 0), memory_space=pltpu.VMEM)
        tokens, cot, normed = kernel_call(
            prepare,
            "prepare",
            [scalars],
            [inputs, cotangent, row(ln1_gain), row(ln1_bias)],
            [sequence, sequence, whole((1, width)), whole((1, width))],
            [shaped(rows, width)] * 3,
        )

        def stack(pieces, deps):
            (out,) = kernel_call(
                stack_four,
                "stack_four",
                [],
                [*pieces, *deps],
                [whole(pieces[0].shape)] * 4 + [ANYWHERE] * len(deps),
                [shaped(4, *pieces[0].shape)],
            )
            return out

        qkvs, weights, attendeds, taus = [], [], [], []
        for slot in range(tensor_size):
            deps = {0: qkv_line, 1: rest_line}.get(slot, [])
            if slot == 1:
                qkv_zero = stack(qkv_far, attendeds)
                qkv_one = over_batch(qkv_zero, 1)
            qkv, weight, attended, tau = run_forward(
                heads, scalars, alphas[slot], normed, [w_qkv] if slot == 0 else [qkv_zero, qkv_one], slot, starts, deps
            )
            qkvs.append(qkv)
            weights.append(weight)
            attendeds.append(attended)
            taus.append(tau)

        rest_zero = stack(chip_gather(jnp.stack(rest_line)), attendeds[:3])
        rest_one = over_batch(rest_zero, 1)
        out_low, dresid, dattended, keep, send, small_two = kernel_call(
            functools.partial(feed_forward, tensor_size),
            "feed_forward",
            [scalars],
            [tokens, cot, row(ln2_gain), row(ln2_bias), up_biases, row(down_bias)]
            + attendeds
            + [w_out, up_own, w_down, rest_zero, rest_one],
            [whole((rows, width))] * 2
            + [whole((1, width))] * 2
            + [whole((tensor_size, hidden)), whole((1, width))]
            + [whole((rows, columns))] * tensor_size
            + [ANYWHERE] * 5,
            [
                shaped(rows, width),
                shaped(rows, width, dtype=F32),
                shaped(rows, tensor_size * columns),
                shaped(4, tensor_size, rest_rows, width),
                shaped(4, tensor_size, rest_rows, width),
                shaped(3 + tensor_size, width, dtype=F32),
            ],
            [
                pltpu.VMEM((tensor_size, columns, width), BF16),
                pltpu.VMEM((tensor_size, hidden, width), BF16),
                pltpu.VMEM((tensor_size, hidden, width), BF16),
                pltpu.VMEM((rows, width), F32),
                pltpu.VMEM((rows, width), F32),
                pltpu.VMEM((tensor_size, PLANE, out_part, width), BF16),
                pltpu.VMEM((tensor_size, PLANE, up_part, width), BF16),
                pltpu.VMEM((tensor_size, PLANE, up_part, width), BF16),
                pltpu.SemaphoreType.DMA((3 + 3 * PLANE,)),
            ],
            flops=8 * 10**9,
            vmem=36,
        )

        def relay_two(first):
            right = lax.ppermute(first[0], "tensor", [(i, i + 1) for i in range(1, tensor_size - 1)])
            left = lax.ppermute(first[1], "tensor", [(i, i - 1) for i in range(1, tensor_size - 1)])
            return [right, left]

        def relay_one(chunk):
            right = lax.ppermute(chunk, "tensor", [(i, i + 1) for i in range(tensor_size - 1)])
            left = lax.ppermute(chunk, "tensor", [(i + 1, i) for i in range(tensor_size - 1)])
            return [right, left]

        def relay_three(second):
            return [lax.ppermute(jnp.where(line >= 2, second[0], second[1]), "tensor", [(2, 3), (1, 0)])]

        def gather_units(far, deps):
            spec = pl.BlockSpec((1, length, width), lambda i, ref: (i, 0, 0), memory_space=pltpu.VMEM)
            (out,) = kernel_call(
                assemble,
                "assemble",
                [scalars],
                [*far, *deps],
                [whole((rows, width))] * 6 + [ANYWHERE] * len(deps),
                [shaped(seq_count, length, width)],
                [pltpu.VMEM((length, width), F32)],
                out_specs=(spec,),
                grid=2,
            )
            return out

        out_one = relay_one(out_low)
        out_two = relay_two(out_one)
        out_far = [out_low] + out_one + out_two + relay_three(out_two)
        piece = pl.BlockSpec((1, tensor_size, rest_rows, width), lambda i: (i, 0, 0, 0), memory_space=pltpu.VMEM)
        rest_half = kernel_call(
            add_parts,
            "add_parts",
            [],
            [keep, over_batch(send, 1)],
            [piece] * 2,
            [shaped(tensor_size, rest_rows, width)] * 4,
            grid=4,
        )

        keeps, sends, dqkvs, dalphas = [], [], [], []
        for slot in range(tensor_size):
            deps = dqkvs[-1:] + {1: list(rest_half), 2: out_one}.get(slot, [])
            dqkv, kept, sent, dalpha = run_backward(
                heads, scalars, alphas[slot], normed, qkvs[slot], taus[slot], starts, dattended, slot, deps
            )
            dqkvs.append(dqkv)
            keeps.append(kept)
            sends.append(sent)
            dalphas.append(jnp.sum(dalpha, axis=1))
        grad_chunk, small_one = kernel_call(
            functools.partial(finish, tensor_size),
            "finish",
            [],
            [tokens, dresid, row(ln1_gain)] + dqkvs + weights + out_two,
            [whole((rows, width))] * 2
            + [whole((1, width))]
            + [whole((rows, 3 * columns))] * tensor_size
            + [whole((width, 3 * columns))] * tensor_size
            + [ANYWHERE] * 2,
            [shaped(rows, width), shaped(2, width, dtype=F32)],
        )
        grad_one = relay_one(grad_chunk)
        grad_two = relay_two(grad_one)
        grad_far = [grad_chunk] + grad_one + grad_two + relay_three(grad_two)

        rest_far = [rest_half[0].astype(F32)] + [over_batch(rest_half[hop // 2], hop).astype(F32) for hop in (2, 4, 6)]
        rest_sum = upper_sum(tree(rest_far), False).astype(BF16)
        rest_far = [rest_sum[0].astype(F32)] + [over_tensor(rest_sum[hop], hop).astype(F32) for hop in range(1, tensor_size)]
        rest_sum = tree(rest_far).astype(BF16)

        small_rows = jnp.concatenate([small_one.reshape(-1), small_two.reshape(-1)] + dalphas)
        count = small_rows.shape[0]
        depth = -(-count // (span * 8)) * 8
        small_rows = jnp.pad(small_rows, (0, depth * span - count)).reshape(depth, span)
        keep = jnp.stack(keeps, axis=1)
        block = tensor_size * part
        sent = over_batch(
            jnp.concatenate([jnp.stack(sends, axis=1).reshape(4 * block, span), split_wide(small_rows)]), 1
        )
        half = (keep.astype(F32) + sent[: 4 * block].astype(F32).reshape(keep.shape)).astype(BF16)
        small_rows = small_rows + join_wide(sent[4 * block :])
        pair = split_wide(small_rows)
        far = [over_batch(jnp.concatenate([half[hop // 2].reshape(block, span), pair]), hop) for hop in (2, 4, 6)]
        total = tree([half[0].astype(F32)] + [one[:block].astype(F32).reshape(half[0].shape) for one in far])
        small_rows = tree([small_rows] + [join_wide(one[block:]) for one in far])
        total = upper_sum(total, False).astype(BF16)
        small_rows = upper_sum(small_rows, True)
        pair = split_wide(small_rows)
        far = [over_tensor(jnp.concatenate([total[hop], pair]), hop) for hop in range(1, tensor_size)]
        qkv_sum = tree([total[0].astype(F32)] + [one[:part].astype(F32) for one in far]).astype(BF16)
        smalls = [small_rows] + [join_wide(one[part:]) for one in far]
        common = tree(smalls).reshape(-1)
        lines = [one.reshape(-1) for one in smalls]
        first = 5 * width
        own_bias = tree([lines[hop][first + hop * hidden : first + (hop + 1) * hidden] for hop in range(tensor_size)])
        first = first + tensor_size * hidden
        own_alpha = tree([lines[hop][first + hop * heads : first + (hop + 1) * heads] for hop in range(tensor_size)])

        gathered = jnp.concatenate([rest_sum, jnp.pad(qkv_sum, ((0, 0), (0, width - span)))])
        output = gather_units(out_far, [gathered])
        gathered = jnp.stack(chip_gather(gathered))
        other = over_batch(gathered, 1)
        grad_w_qkv, grad_w_out, grad_w_up, grad_w_down = kernel_call(
            functools.partial(unpack, out_part, up_part),
            "unpack",
            [scalars],
            [gathered, other],
            [whole(gathered.shape)] * 2,
            [
                shaped(3, width, columns, dtype=F32),
                shaped(columns, width, dtype=F32),
                shaped(width, hidden, dtype=F32),
                shaped(hidden, width, dtype=F32),
            ],
            [pltpu.VMEM((hidden, width), F32)],
        )
        grad_input = gather_units(grad_far, [grad_w_qkv])
        return (
            output,
            grad_input,
            common[:width],
            common[width : 2 * width],
            grad_w_qkv,
            own_alpha,
            grad_w_out,
            common[2 * width : 3 * width],
            common[3 * width : 4 * width],
            grad_w_up,
            own_bias,
            grad_w_down,
            common[4 * width : 5 * width],
        )

    return jax.shard_map(
        shards,
        mesh=mesh,
        in_specs=(
            P("batch", None, None),
            P("batch", None),
            P(),
            P(),
            P(None, None, "tensor"),
            P("tensor"),
            P("tensor", None),
            P(),
            P(),
            P(None, "tensor"),
            P("tensor"),
            P("tensor", None),
            P(),
            P("batch", None, None),
        ),
        out_specs=(
            P("batch", None, None),
            P("batch", None, None),
            P(),
            P(),
            P(None, None, "tensor"),
            P("tensor"),
            P("tensor", None),
            P(),
            P(),
            P(None, "tensor"),
            P("tensor"),
            P("tensor", None),
            P(),
        ),
        check_vma=False,
    )
```

```python
import functools

import jax
import jax.numpy as jnp
from jax import lax
from jax.experimental import pallas as pl
from jax.experimental.pallas import tpu as pltpu
from jax.sharding import PartitionSpec as P

BISECT = 10
MASKED = -10000.0
NORM_EPS = 1e-05
LN2 = 0.6931471805599453
TILE = 128
EXTRA = 16
SMALL = 16
PLANE = 8
MIB = 1024 * 1024
BF16 = jnp.bfloat16
F32 = jnp.float32
GELU_A = 0.7978845608028654
GELU_B = 0.044715


def layer_norm(values, norm_gain, norm_shift):
    centre = values - jnp.mean(values, axis=-1, keepdims=True)
    spread = jnp.mean(centre * centre, axis=-1, keepdims=True)
    return centre * lax.rsqrt(spread + NORM_EPS) * norm_gain + norm_shift


def dot_nt(left, right):
    return lax.dot_general(left, right, (((1,), (1,)), ((), ())), preferred_element_type=F32)


def dot_nn(left, right):
    return lax.dot_general(left, right, (((1,), (0,)), ((), ())), preferred_element_type=F32)


def dot_tn(left, right):
    return lax.dot_general(left, right, (((0,), (0,)), ((), ())), preferred_element_type=F32)


def tile_mask(first, starts_ref):
    keys = lax.broadcasted_iota(jnp.int32, (first + TILE, TILE), 0)
    queries = lax.broadcasted_iota(jnp.int32, (first + TILE, TILE), 1) + first
    return (keys <= queries) & (keys >= starts_ref[:, first : first + TILE])


def head_lanes(values, head):
    lanes = lax.broadcasted_iota(jnp.int32, values.shape, 1)
    return jnp.where((lanes >= head * 64) & (lanes < head * 64 + 64), values, jnp.zeros_like(values))


def rolled(values, shift, rows):
    return pltpu.roll(values, shift, 0)[:rows]


def prepare_cotangent(scalars_ref, cotangent_ref, dep_ref, cot_ref):
    shift = cotangent_ref.shape[1] - scalars_ref[5]
    cot_ref[...] = rolled(cotangent_ref[0].astype(F32), shift, cot_ref.shape[0]).astype(BF16)


def prepare(scalars_ref, inputs_ref, gain_ref, bias_ref, tokens_ref, normed_ref):
    rows, length = tokens_ref.shape[0], inputs_ref.shape[1]
    shift = length - scalars_ref[5]
    tokens = rolled(inputs_ref[0].astype(F32), shift, rows)
    tokens_ref[...] = tokens.astype(BF16)
    normed_ref[...] = layer_norm(tokens, gain_ref[...], bias_ref[...]).astype(BF16)


def pack_qkv(place_ref, weight_ref, bias_ref, alpha_ref, out_ref):
    part, columns = weight_ref.shape[1:]
    for index in range(3):
        out_ref[:part, index * columns : (index + 1) * columns] = weight_ref[index]
    rest = jnp.concatenate([bias_ref[:, 3 * columns :], alpha_ref[...]], axis=1)
    rest = jnp.concatenate([rest, jnp.zeros((1, 3 * columns - rest.shape[1]), F32)], axis=1)
    values = jnp.concatenate([bias_ref[:, : 3 * columns], rest])
    high = values.astype(BF16).astype(F32)
    middle = (values - high).astype(BF16).astype(F32)
    low = values - high - middle
    blank = jnp.zeros((EXTRA - 6, 3 * columns), F32)
    out_ref[part:, :] = jnp.concatenate([high, middle, low, blank]).astype(BF16)


def pack_rest(place_ref, out_weight_ref, up_ref, down_ref, *refs):
    part_ref, turned_ref, turn_ref = refs[-3:]
    out_part = out_weight_ref.shape[0]
    up_part = down_ref.shape[0]
    turn_ref[...] = jnp.transpose(up_ref[...].astype(F32))
    turned_ref[...] = turn_ref[...].astype(BF16)
    rows = pl.ds(pl.multiple_of(place_ref[0] * up_part, up_part), up_part)
    part_ref[:out_part, :] = out_weight_ref[...]
    part_ref[out_part : out_part + up_part, :] = turn_ref[rows, :].astype(BF16)
    part_ref[out_part + up_part :, :] = down_ref[...]


def stack_four(*refs):
    for index in range(4):
        refs[-1][index] = refs[index][...]


def assemble(scalars_ref, own_ref, right_one, left_one, right_two, left_two, far_ref, *refs):
    out_ref, both_ref = refs[-2:]
    pair = pl.program_id(0)
    rows = own_ref.shape[0]
    sources = ((own_ref, 0), (right_one, -1), (left_one, 1), (right_two, -2), (left_two, 2), (far_ref, 3), (far_ref, -3))
    for half in range(2):
        away = 2 * pair + half - scalars_ref[2]
        for ref, distance in sources:

            @pl.when(away == distance)
            def _():
                both_ref[half * rows : (half + 1) * rows, :] = ref[...].astype(F32)

    out_ref[0] = pltpu.roll(both_ref[...], scalars_ref[3 + pair], 0).astype(BF16)


def assemble_all(scalars_ref, all_ref, *refs):
    rows = all_ref.shape[1]
    both = all_ref[...].reshape(2 * rows, all_ref.shape[2]).astype(F32)
    refs[-1][0] = pltpu.roll(both, scalars_ref[3 + pl.program_id(0)], 0).astype(BF16)


def add_parts(keep_ref, sent_ref, *out_refs):
    for index, ref in enumerate(out_refs):

        @pl.when(pl.program_id(0) == index)
        def _():
            ref[...] = (keep_ref[0].astype(F32) + sent_ref[0].astype(F32)).astype(BF16)


def attend_forward(heads, base, weight_count, dep_count, scalars_ref, alpha_ref, normed_ref, starts_ref, *refs):
    slot = (base + pl.program_id(0)) * heads
    weight_refs = refs[:weight_count]
    qkv_ref, weight_out_ref, attended_ref, tau_ref, shifted_ref = refs[weight_count + dep_count :]
    rows = normed_ref.shape[0]
    if weight_count == 1:
        (weight_ref,) = weight_refs
        for index in range(3):
            weight_out_ref[:, index * heads * 64 : (index + 1) * heads * 64] = weight_ref[index]
    else:
        for core, weight_ref in enumerate(weight_refs):
            part = weight_ref.shape[1]
            for chip in range(4):
                row = pl.multiple_of((scalars_ref[0] ^ (2 * chip + core)) * part, part)
                weight_out_ref[pl.ds(row, part), :] = weight_ref[chip]
    width = heads * 64
    qkv = dot_nn(normed_ref[...], weight_out_ref[...]).astype(BF16)
    qkv_ref[...] = qkv
    queries = qkv[:, :width]
    keys = qkv[:, width : 2 * width]
    values_t = jnp.transpose(qkv[:, 2 * width :].astype(F32)).astype(BF16)
    tiles = [(h, first) for h in range(heads) for first in range(0, rows, TILE)]
    offsets = []
    total = 0
    for h, first in tiles:
        offsets.append(total)
        total += first + TILE
    highs, counts = [], []
    for (h, first), offset in zip(tiles, offsets):
        alpha_minus = alpha_ref[slot + h] - 1.0
        query = head_lanes(queries[first : first + TILE], h)
        scores = dot_nt(keys[: first + TILE], query) * 0.125
        shifted = jnp.where(tile_mask(first, starts_ref), alpha_minus * scores, MASKED)
        shifted_ref[offset : offset + first + TILE, :] = shifted
        spots = lax.broadcasted_iota(jnp.int32, (1, TILE), 1) + (first + 1)
        counts.append((spots - starts_ref[:, first : first + TILE]).astype(F32))
        highs.append(jnp.max(shifted, axis=0, keepdims=True))
    alpha_rows = jnp.concatenate(
        [jnp.full((rows // TILE, TILE), alpha_ref[slot + h] - 1.0, F32) for h in range(heads)]
    )
    bottom = jnp.concatenate(highs) - 1.0
    bracket = jnp.concatenate(highs) - jnp.exp(-alpha_rows * jnp.log(jnp.concatenate(counts))) - bottom
    cell = bracket * (1.0 / 2**BISECT)
    top = float(2**BISECT - 1)

    def evaluate(point):
        sums, slopes = [], []
        for index, ((h, first), offset) in enumerate(zip(tiles, offsets)):
            power = (1.0 / (alpha_ref[slot + h] - 1.0) - 1.0) * (1.0 / LN2)
            margin = jnp.maximum(shifted_ref[offset : offset + first + TILE, :] - point[index : index + 1], 0.0)
            slope = jnp.exp2(power * jnp.log(margin))
            slopes.append(jnp.sum(slope, axis=0, keepdims=True))
            sums.append(jnp.sum(slope * margin, axis=0, keepdims=True))
        return jnp.concatenate(sums), jnp.concatenate(slopes)

    def newton(point, sums, slopes):
        return point + (sums - jnp.exp((1.0 - alpha_rows) * jnp.log(sums))) / slopes

    def index_of(point):
        return jnp.clip(jnp.floor((point - bottom) / jnp.maximum(cell, 1e-30)), 0.0, top)

    point = bottom + 0.5 * bracket
    for _ in range(3):
        point = jnp.maximum(newton(point, *evaluate(point)), bottom)

    def unsettled(state):
        return state[1] > 0.0

    def settle(state):
        spot = state[0]
        after = bottom + (spot + 1.0) * cell
        sums, slopes = evaluate(after)
        higher = (sums >= 1.0) & (spot < top) & (after > bottom + spot * cell)
        spot = jnp.where(higher, jnp.maximum(spot + 1.0, index_of(newton(after, sums, slopes))), spot)
        return spot, jnp.max(jnp.where(higher, 1.0, 0.0))

    spot, _ = lax.while_loop(unsettled, settle, (index_of(point), jnp.float32(1.0)))
    low_rows = bottom + spot * cell
    lows = [low_rows[index : index + 1] for index in range(len(tiles))]
    for (h, first), offset, low in zip(tiles, offsets, lows):
        exponent = 1.0 / (alpha_ref[slot + h] - 1.0)
        shifted = shifted_ref[offset : offset + first + TILE, :]
        margin = jnp.maximum(shifted - low, 0.0)
        slope = jnp.exp2((exponent - 1.0) * (1.0 / LN2) * jnp.log(margin))
        slopes = exponent * jnp.sum(slope, axis=0, keepdims=True)
        summed = jnp.sum(slope * margin, axis=0, keepdims=True)
        tau = low + (summed - 1.0) / slopes
        tau_ref[h : h + 1, first : first + TILE] = tau
        margin = jnp.maximum(shifted - tau, 0.0)
        probs = jnp.exp2(exponent * (1.0 / LN2) * jnp.log(margin)).astype(BF16)
        out = dot_nn(values_t[h * 64 : h * 64 + 64, : first + TILE], probs)
        attended_ref[first : first + TILE, h * 64 : h * 64 + 64] = jnp.transpose(out).astype(BF16)


def attend_backward(heads, base, scalars_ref, alpha_ref, normed_ref, qkv_ref, tau_ref, starts_ref, dattended_ref, *refs):
    slot = (base + pl.program_id(0)) * heads
    dqkv_ref, keep_ref, send_ref, dalpha_ref, dkeys_ref, dvalues_ref, grad_ref = refs[-7:]
    rows = normed_ref.shape[0]
    width = heads * 64
    queries = qkv_ref[:, :width]
    keys = qkv_ref[:, width : 2 * width]
    values = qkv_ref[:, 2 * width :]
    keys_t = jnp.transpose(keys.astype(F32)).astype(BF16)
    dkeys_ref[...] = jnp.zeros_like(dkeys_ref)
    dvalues_ref[...] = jnp.zeros_like(dvalues_ref)
    for h in range(heads):
        alpha_minus = alpha_ref[slot + h] - 1.0
        exponent = 1.0 / alpha_minus
        dalpha = jnp.zeros((1, TILE), F32)
        for first in range(0, rows, TILE):
            end = first + TILE
            query = head_lanes(queries[first:end], h)
            dout = head_lanes(dattended_ref[first:end, :], h)
            scores = dot_nt(keys[:end], query) * 0.125
            shifted = jnp.where(tile_mask(first, starts_ref), alpha_minus * scores, MASKED)
            margin = jnp.maximum(shifted - tau_ref[h : h + 1, first:end], 0.0)
            log_margin = jnp.log(margin)
            slope = jnp.exp2((exponent - 1.0) * (1.0 / LN2) * log_margin)
            probs = slope * margin
            slope = exponent * slope
            dprobs = dot_nt(values[:end], dout)
            slope_sum = jnp.sum(slope, axis=0, keepdims=True)
            mixed = jnp.sum(slope * dprobs, axis=0, keepdims=True)
            centred = dprobs - mixed / slope_sum
            log_margin = jnp.where(margin > 0.0, log_margin, 0.0)
            alpha_part = slope * scores - (exponent * exponent) * (probs * log_margin)
            dalpha = dalpha + jnp.sum(alpha_part * centred, axis=0, keepdims=True)
            dscores = (alpha_minus * (slope * centred)).astype(BF16)
            dvalues_ref[:end, :] += dot_nn(probs.astype(BF16), dout)
            dkeys_ref[:end, :] += dot_nn(dscores, query)
            dquery_t = dot_nn(keys_t[h * 64 : h * 64 + 64, :end], dscores) * 0.125
            dqkv_ref[first:end, h * 64 : h * 64 + 64] = jnp.transpose(dquery_t).astype(BF16)
        dalpha_ref[h : h + 1, :] = dalpha
    dqkv_ref[:, width : 2 * width] = (dkeys_ref[...] * 0.125).astype(BF16)
    dqkv_ref[:, 2 * width :] = dvalues_ref[...].astype(BF16)
    grad = dot_tn(normed_ref[...], dqkv_ref[...]).astype(BF16)
    grad_ref[...] = grad.reshape(grad_ref.shape)
    for chip in range(4):
        keep_ref[chip] = grad_ref[scalars_ref[0] ^ (2 * chip)]
        send_ref[chip] = grad_ref[scalars_ref[0] ^ (2 * chip + 1)]


def norm_back(values, gain, dnormed):
    centre = values - jnp.mean(values, axis=-1, keepdims=True)
    scale = lax.rsqrt(jnp.mean(centre * centre, axis=-1, keepdims=True) + NORM_EPS)
    unit = centre * scale
    scaled = dnormed * gain
    mean = jnp.mean(scaled, axis=-1, keepdims=True)
    mixed = jnp.mean(scaled * unit, axis=-1, keepdims=True)
    dvalues = scale * (scaled - mean - unit * mixed)
    return dvalues, jnp.sum(dnormed * unit, axis=0, keepdims=True), jnp.sum(dnormed, axis=0, keepdims=True)


def feed_forward(slots, scalars_ref, tokens_ref, cot_ref, gain_ref, bias_ref, up_bias_ref, down_bias_ref, *refs):
    attended_refs = refs[:2]
    out_own, up_own, down_own, far_zero, far_one = refs[2:7]
    out_ref, dresid_ref, dattended_ref, keep_ref, send_ref, small_ref = refs[7:13]
    w_out, w_up, w_down, sums, dnormed_ref, grad_out, grad_up, grad_down, copies = refs[13:]
    place = scalars_ref[0]
    out_part = w_out.shape[1] // PLANE
    up_part = w_up.shape[1] // PLANE
    out_moves = [(out_own, w_out.at[0])]
    moves = [(up_own, w_up.at[0]), (down_own, w_down.at[0])]
    for core, far in enumerate((far_zero, far_one)):
        for chip in range(4):
            spot = place ^ (2 * chip + core)
            out_rows = pl.ds(pl.multiple_of(spot * out_part, out_part), out_part)
            up_rows = pl.ds(pl.multiple_of(spot * up_part, up_part), up_part)
            out_moves.append((far.at[chip, :, :out_part], w_out.at[1:, out_rows]))
            moves.append((far.at[chip, :, out_part : out_part + up_part], w_up.at[1:, up_rows]))
            moves.append((far.at[chip, :, out_part + up_part :], w_down.at[1:, up_rows]))
    started = []

    def begin(source, target):
        copy = pltpu.make_async_copy(source, target, copies.at[len(started)])
        copy.start()
        started.append(copy)

    for source, target in out_moves + moves:
        begin(source, target)
    for copy in started[: len(out_moves)]:
        copy.wait()

    width = tokens_ref.shape[1]
    attended = jnp.concatenate([ref[...] for ref in attended_refs], axis=1)
    out_weights = w_out[...].reshape(slots * w_out.shape[1], width)
    resid = tokens_ref[...].astype(F32) + dot_nn(attended, out_weights)
    sums[...] = resid
    normed = layer_norm(resid, gain_ref[...], bias_ref[...]).astype(BF16)
    dnormed_ref[...] = jnp.zeros_like(dnormed_ref)
    cot = cot_ref[...]
    for copy in started[len(out_moves) :]:
        copy.wait()
    for slot in range(slots):
        pre = dot_nt(normed, w_up[slot]) + up_bias_ref[slot : slot + 1, :]
        square = pre * pre
        bend = jnp.tanh(pre * (GELU_A + GELU_A * GELU_B * square))
        half = 0.5 + 0.5 * bend
        act = (pre * half).astype(BF16)
        slope = half + (0.5 * pre) * (1.0 - bend * bend) * (GELU_A + 3.0 * GELU_A * GELU_B * square)
        sums[...] += dot_nn(act, w_down[slot])
        dpre = (dot_nt(cot, w_down[slot]) * slope).astype(BF16)
        small_ref[3 + slot : 4 + slot, :] = jnp.sum(dpre.astype(F32), axis=0, keepdims=True)
        dnormed_ref[...] += dot_nn(dpre, w_up[slot])
        grad_down[slot] = dot_tn(act, cot).astype(BF16).reshape(PLANE, up_part, width)
        grad_up[slot] = dot_tn(dpre, normed).astype(BF16).reshape(PLANE, up_part, width)
    out_ref[...] = (sums[...] + down_bias_ref[...]).astype(BF16)
    dresid, small_ref[0:1, :], small_ref[1:2, :] = norm_back(resid, gain_ref[...], dnormed_ref[...])
    cot_full = cot.astype(F32)
    small_ref[2:3, :] = jnp.sum(cot_full, axis=0, keepdims=True)
    dresid = cot_full + dresid
    dresid_ref[...] = dresid
    dresid_low = dresid.astype(BF16)
    dattended_ref[...] = dot_nt(dresid_low, out_weights).astype(BF16)
    grad_out[...] = dot_tn(attended, dresid_low).astype(BF16).reshape(grad_out.shape)
    for core, target in enumerate((keep_ref, send_ref)):
        for chip in range(4):
            spot = place ^ (2 * chip + core)
            for slot in range(slots):
                target[chip, slot, :out_part] = grad_out[slot, spot]
                target[chip, slot, out_part : out_part + up_part] = grad_up[slot, spot]
                target[chip, slot, out_part + up_part :] = grad_down[slot, spot]


def finish(slots, heads, tokens_ref, dresid_ref, gain_ref, two_ref, *refs):
    dqkv_first, dqkv_rest, weight_first, weight_rest, alpha_first, alpha_rest = refs[:6]
    out_ref, message_ref, small_ref = refs[-3:]
    dqkv = jnp.concatenate([dqkv_first[...]] + [dqkv_rest[slot] for slot in range(slots - 1)], axis=1)
    weights = jnp.concatenate([weight_first[...]] + [weight_rest[slot] for slot in range(slots - 1)], axis=1)
    dnormed = dot_nt(dqkv, weights)
    dinput, gain, bias = norm_back(tokens_ref[...].astype(F32), gain_ref[...], dnormed)
    out_ref[...] = (dresid_ref[...] + dinput).astype(BF16)
    width = gain.shape[1]
    lanes = lax.broadcasted_iota(jnp.int32, (1, width), 1)
    alphas = []
    for slot in range(slots):
        values = alpha_first[...] if slot == 0 else alpha_rest[slot - 1]
        totals = jnp.sum(values, axis=1, keepdims=True)
        line = jnp.zeros((1, width), F32)
        for head in range(heads):
            line = jnp.where(lanes == head, totals[head : head + 1], line)
        alphas.append(line)
    blank = jnp.zeros((SMALL - 5 - 2 * slots, width), F32)
    values = jnp.concatenate([gain, bias, two_ref[...]] + alphas + [blank])
    span = message_ref.shape[2]
    side = jnp.concatenate([values[:, span:], jnp.zeros((SMALL, 2 * span - width), F32)], axis=1)
    small = jnp.concatenate([values[:, :span], side])
    small_ref[...] = small
    message_ref[0] = pair_of(small)


def pair_of(values):
    high = values.astype(BF16)
    return jnp.concatenate([high, (values - high.astype(F32)).astype(BF16)])


def value_of(pair):
    half = pair.shape[0] // 2
    return pair[:half].astype(F32) + pair[half:].astype(F32)


def tree(four):
    return (four[0] + four[1]) + (four[2] + four[3])


def sum_core(slots, keep_ref, received_ref, small_ref, *refs):
    total = small_ref[...] + value_of(received_ref[4 * slots])
    refs[4][...] = total
    pair = pair_of(total)
    for chip in range(4):
        for slot in range(slots):
            index = 4 * slot + chip
            refs[chip][slot] = (keep_ref[index].astype(F32) + received_ref[index].astype(F32)).astype(BF16)
        refs[chip][slots] = pair


def sum_plane(slots, own_ref, one_ref, two_ref, three_ref, small_ref, *refs):
    part = own_ref.shape[1]
    inputs = (own_ref, one_ref, two_ref, three_ref)
    small = tree([small_ref[...]] + [value_of(ref[slots]) for ref in inputs[1:]])
    refs[slots][...] = small
    pair = pair_of(small)
    for slot in range(slots):
        total = tree([ref[slot].astype(F32) for ref in inputs])
        if slot == 0:
            refs[0][...] = total
        else:
            refs[slot][:part] = total.astype(BF16)
            refs[slot][part:] = pair


def sum_rest(slots, own_ref, one_ref, two_ref, three_ref, *refs):
    inputs = (own_ref, one_ref, two_ref, three_ref)
    for slot in range(slots):
        total = tree([ref[slot].astype(F32) for ref in inputs])
        refs[slot][...] = total if slot == 0 else total.astype(BF16)


def sum_line(slots, *refs):
    rest_refs, qkv_refs = refs[:slots], refs[slots : 2 * slots]
    small_ref, out_ref, total_ref = refs[2 * slots :]
    rows = rest_refs[0].shape[0]
    part, span = qkv_refs[0].shape
    out_ref[:rows] = tree([ref[...].astype(F32) for ref in rest_refs]).astype(BF16)
    out_ref[rows:, :span] = tree(
        [qkv_refs[0][...]] + [ref[:part].astype(F32) for ref in qkv_refs[1:]]
    ).astype(BF16)
    out_ref[rows:, span:] = jnp.zeros((part, out_ref.shape[1] - span), BF16)
    smalls = [small_ref[...]] + [value_of(ref[part:]) for ref in qkv_refs[1:]]
    width = out_ref.shape[1]
    smalls = [jnp.concatenate([one[:SMALL], one[SMALL:, : width - span]], axis=1) for one in smalls]
    common = tree([one[:5] for one in smalls])
    bias = tree([one[5 + slot : 6 + slot] for slot, one in enumerate(smalls)])
    alpha = tree([one[5 + slots + slot : 6 + slots + slot] for slot, one in enumerate(smalls)])
    total_ref[...] = jnp.concatenate([common, bias, alpha, jnp.zeros((1, width), F32)])


def unpack(out_part, up_part, scalars_ref, zero_ref, one_ref, qkv_ref, out_ref, up_ref, down_ref, turn_ref):
    columns = qkv_ref.shape[2]
    for core, ref in enumerate((zero_ref, one_ref)):
        for chip in range(4):
            spot = scalars_ref[0] ^ (2 * chip + core)
            out_rows = pl.ds(pl.multiple_of(spot * out_part, out_part), out_part)
            up_rows = pl.ds(pl.multiple_of(spot * up_part, up_part), up_part)
            first = out_part
            out_ref[out_rows, :] = ref[chip, :first].astype(F32)
            turn_ref[up_rows, :] = ref[chip, first : first + up_part].astype(F32)
            first = first + up_part
            down_ref[up_rows, :] = ref[chip, first : first + up_part].astype(F32)
            first = first + up_part
            part = ref.shape[1] - first
            qkv_rows = pl.ds(pl.multiple_of(spot * part, part), part)
            for index in range(3):
                qkv_ref[index, qkv_rows, :] = ref[chip, first:, index * columns : (index + 1) * columns].astype(F32)
    up_ref[...] = jnp.transpose(turn_ref[...])


def whole(shape):
    return pl.BlockSpec(shape, lambda *_: (0,) * len(shape), memory_space=pltpu.VMEM)


def kernel_call(body, name, scalars, operands, in_specs, out_shapes, scratch=(), out_specs=None, grid=1, flops=10**9, vmem=16,
                aliases=None, far_in=False, far_out=()):
    spec = pltpu.PrefetchScalarGridSpec(
        num_scalar_prefetch=len(scalars),
        grid=(grid,),
        in_specs=in_specs,
        out_specs=out_specs or tuple(whole(shape.shape) for shape in out_shapes),
        scratch_shapes=list(scratch),
    )
    far = lambda array: pltpu.with_memory_space_constraint(array, pltpu.HBM) if far_in else array
    return pl.pallas_call(
        body,
        out_shape=tuple(
            pltpu.HBM(shape.shape, shape.dtype) if index in far_out else shape for index, shape in enumerate(out_shapes)
        ),
        grid_spec=spec,
        compiler_params=pltpu.CompilerParams(vmem_limit_bytes=vmem * MIB),
        input_output_aliases=aliases or {},
        cost_estimate=pl.CostEstimate(flops=flops, bytes_accessed=10**6, transcendentals=0),
        name=name,
    )(*map(far, scalars), *map(far, operands))


def shaped(*shape, dtype=BF16):
    return jax.ShapeDtypeStruct(shape, dtype)


ANYWHERE = pl.BlockSpec(memory_space=pl.ANY)


def run_forward(heads, scalars, alpha, normed, weights, base, count, starts, deps):
    rows, width = normed.shape
    columns = 3 * heads * 64
    total = heads * sum(range(TILE, rows + 1, TILE))
    stacked = lambda *shape: pl.BlockSpec((None,) + shape, lambda i, *_: (i, 0, 0), memory_space=pltpu.VMEM)
    if base == 0:
        weight_specs = [whole(weights[0].shape)]
    else:
        block = (4, None) + weights[0].shape[2:]
        weight_specs = [pl.BlockSpec(block, lambda i, *_: (0, i, 0, 0), memory_space=pltpu.VMEM)] * 2
    smem = pl.BlockSpec(memory_space=pltpu.SMEM)
    return kernel_call(
        functools.partial(attend_forward, heads, base, len(weights), len(deps)),
        "attend_forward",
        [scalars],
        [alpha, normed, starts, *weights, *deps],
        [smem, whole(normed.shape), whole(starts.shape)] + weight_specs + [ANYWHERE] * len(deps),
        [
            shaped(count, rows, columns),
            shaped(count, width, columns),
            shaped(rows, count * heads * 64),
            shaped(count, heads, rows, dtype=F32),
        ],
        [pltpu.VMEM((total, TILE), F32)],
        out_specs=(
            stacked(rows, columns),
            stacked(width, columns),
            pl.BlockSpec((rows, heads * 64), lambda i, *_: (0, i), memory_space=pltpu.VMEM),
            stacked(heads, rows),
        ),
        grid=count,
        flops=5 * 10**9 * count,
    )


def run_backward(heads, scalars, alpha, normed, qkv, tau, starts, dattended, base, count, slots, buffers, deps):
    rows, width = normed.shape
    columns = 3 * heads * 64
    smem = pl.BlockSpec(memory_space=pltpu.SMEM)
    stacked = lambda *shape: pl.BlockSpec((None,) + shape, lambda i, *_: (i, 0, 0), memory_space=pltpu.VMEM)
    dattended_spec = pl.BlockSpec((rows, heads * 64), lambda i, *_: (0, base + i), memory_space=pltpu.VMEM)
    parts = (width // PLANE, columns)
    message = pl.BlockSpec((4,) + parts, lambda i, *_: (base + i, 0, 0), memory_space=pltpu.VMEM)
    return kernel_call(
        functools.partial(attend_backward, heads, base),
        "attend_backward",
        [scalars],
        [alpha, normed, qkv, tau, starts, dattended, *buffers, *deps],
        [smem, whole(normed.shape), stacked(rows, columns), stacked(heads, rows), whole(starts.shape)]
        + [dattended_spec]
        + [ANYWHERE] * (len(buffers) + len(deps)),
        [
            shaped(count, rows, columns),
            shaped(4 * slots, *parts),
            shaped(4 * slots + 1, *parts),
            shaped(count, heads, TILE, dtype=F32),
        ],
        [
            pltpu.VMEM((rows, heads * 64), F32),
            pltpu.VMEM((rows, heads * 64), F32),
            pltpu.VMEM((PLANE,) + parts, BF16),
        ],
        out_specs=(stacked(rows, columns), message, message, stacked(heads, TILE)),
        grid=count,
        flops=4 * 10**9 * count,
        aliases={7: 1, 8: 2} if buffers else None,
        far_in=True,
    )


def split_wide(values):
    high = lax.reduce_precision(values, exponent_bits=8, mantissa_bits=7)
    return jnp.concatenate([high.astype(BF16), (values - high).astype(BF16)])


def join_wide(pair):
    pair = pair.astype(F32)
    half = pair.shape[0] // 2
    return pair[:half] + pair[half:]


def solution(mesh):
    batch_size = mesh.shape["batch"]
    tensor_size = mesh.shape["tensor"]

    def over_batch(array, hop):
        return lax.ppermute(array, "batch", [(i, i ^ hop) for i in range(batch_size)])

    def over_tensor(array, hop):
        return lax.ppermute(array, "tensor", [(i, i ^ hop) for i in range(tensor_size)])

    def line_gather(part):
        return [over_tensor(part, hop) for hop in range(1, tensor_size)]

    def chip_gather(part):
        return [part] + [over_batch(part, hop) for hop in (2, 4, 6)]

    def upper_sum(array, split):
        hop = PLANE
        while hop < batch_size:
            array = array + join(over_batch(cut(array, split), hop), split)
            hop *= 2
        return array

    def cut(array, split):
        return split_wide(array) if split else array.astype(BF16)

    def join(array, split):
        return join_wide(array) if split else array.astype(F32)

    def shards(inputs, doc_lengths, ln1_gain, ln1_bias, w_qkv, entmax_alpha, w_out, ln2_gain, ln2_bias,
               w_up, up_bias, w_down, down_bias, cotangent):
        seq_count, length, width = inputs.shape
        heads = entmax_alpha.shape[0]
        hidden = w_up.shape[1]
        rows = length // 2
        columns = heads * 64
        place = lax.axis_index("batch") % PLANE
        line = lax.axis_index("tensor")

        def own_part(array):
            return lax.dynamic_slice_in_dim(array, place * (array.shape[0] // PLANE), array.shape[0] // PLANE)

        out_part = w_out.shape[0] // PLANE
        up_part = hidden // PLANE
        part = width // PLANE
        span = 3 * columns
        rest_rows = out_part + 2 * up_part
        spot = place.reshape(1).astype(jnp.int32)
        row = lambda array: array.reshape(1, -1)
        by_place = lambda rows: pl.BlockSpec((rows, width), lambda i, ref: (ref[0], 0), memory_space=pltpu.VMEM)

        (qkv_part,) = kernel_call(
            pack_qkv,
            "pack_qkv",
            [spot],
            [w_qkv, row(up_bias), jnp.pad(row(entmax_alpha), ((0, 0), (0, TILE - heads)))],
            [
                pl.BlockSpec((3, part, columns), lambda i, ref: (0, ref[0], 0), memory_space=pltpu.VMEM),
                whole((1, hidden)),
                whole((1, TILE)),
            ],
            [shaped(part + EXTRA, span)],
        )
        qkv_line = line_gather(qkv_part)
        extras = [far[part : part + 6].astype(F32) for far in qkv_line]
        extras = [(far[:2] + far[2:4] + far[4:]).reshape(-1) for far in extras]
        alphas = jnp.concatenate([entmax_alpha] + [far[hidden : hidden + heads] for far in extras])
        up_biases = jnp.stack([up_bias] + [far[:hidden] for far in extras])
        qkv_far = chip_gather(jnp.stack([far[:part] for far in qkv_line]))

        ends = jnp.cumsum(doc_lengths, axis=1)
        firsts = ends - doc_lengths
        big = jnp.sum(jnp.where(doc_lengths == rows, firsts, 0), axis=1)

        def unit_start(unit):
            return (jnp.take(big, unit // 2) + rows * (unit % 2)) % length

        start = unit_start(line)
        doc_places = (jnp.take(firsts, line // 2, axis=0) - start) % length
        spots = jnp.arange(rows, dtype=jnp.int32)
        starts = jnp.max(
            jnp.where(doc_places[:, None] <= spots[None, :], doc_places[:, None], 0), axis=0, keepdims=True
        )
        scalars = jnp.stack([place, line // 2, line, big[0], big[1], start]).astype(jnp.int32)

        rest_part, up_own = kernel_call(
            pack_rest,
            "pack_rest",
            [spot],
            [w_out, w_up, w_down],
            [by_place(out_part), whole(w_up.shape), by_place(up_part)],
            [shaped(rest_rows, width), shaped(hidden, width)],
            [pltpu.VMEM((hidden, width), F32)],
        )
        rest_line = line_gather(rest_part)

        sequence = pl.BlockSpec((1, length, width), lambda i, ref: (ref[1], 0, 0), memory_space=pltpu.VMEM)
        tokens, normed = kernel_call(
            prepare,
            "prepare",
            [scalars],
            [inputs, row(ln1_gain), row(ln1_bias)],
            [sequence, whole((1, width)), whole((1, width))],
            [shaped(rows, width)] * 2,
        )

        def stack(pieces, deps):
            (out,) = kernel_call(
                stack_four,
                "stack_four",
                [],
                [*pieces, *deps],
                [whole(pieces[0].shape)] * 4 + [ANYWHERE] * len(deps),
                [shaped(4, *pieces[0].shape)],
            )
            return out

        qkv_first, weight_first, attended_first, tau_first = run_forward(
            heads, scalars, entmax_alpha, normed, [w_qkv], 0, 1, starts, qkv_line
        )
        qkv_zero = stack(qkv_far, [attended_first])
        (cot,) = kernel_call(
            prepare_cotangent,
            "prepare_cotangent",
            [scalars],
            [cotangent, attended_first],
            [sequence, ANYWHERE],
            [shaped(rows, width)],
        )
        qkv_one = over_batch(qkv_zero, 1)
        qkv_rest, weight_rest, attended_rest, tau_rest = run_forward(
            heads, scalars, alphas, normed, [qkv_zero, qkv_one], 1, tensor_size - 1, starts, rest_line + [cot]
        )
        rest_zero = stack(chip_gather(jnp.stack(rest_line)), [attended_rest])
        rest_one = over_batch(rest_zero, 1)
        out_low, dresid, dattended, keep, send, small_two = kernel_call(
            functools.partial(feed_forward, tensor_size),
            "feed_forward",
            [scalars],
            [tokens, cot, row(ln2_gain), row(ln2_bias), up_biases, row(down_bias)]
            + [attended_first, attended_rest]
            + [w_out, up_own, w_down, rest_zero, rest_one],
            [whole((rows, width))] * 2
            + [whole((1, width))] * 2
            + [whole((tensor_size, hidden)), whole((1, width))]
            + [whole(attended_first.shape), whole(attended_rest.shape)]
            + [ANYWHERE] * 5,
            [
                shaped(rows, width),
                shaped(rows, width, dtype=F32),
                shaped(rows, tensor_size * columns),
                shaped(4, tensor_size, rest_rows, width),
                shaped(4, tensor_size, rest_rows, width),
                shaped(3 + tensor_size, width, dtype=F32),
            ],
            [
                pltpu.VMEM((tensor_size, columns, width), BF16),
                pltpu.VMEM((tensor_size, hidden, width), BF16),
                pltpu.VMEM((tensor_size, hidden, width), BF16),
                pltpu.VMEM((rows, width), F32),
                pltpu.VMEM((rows, width), F32),
                pltpu.VMEM((tensor_size, PLANE, out_part, width), BF16),
                pltpu.VMEM((tensor_size, PLANE, up_part, width), BF16),
                pltpu.VMEM((tensor_size, PLANE, up_part, width), BF16),
                pltpu.SemaphoreType.DMA((3 + 3 * PLANE,)),
            ],
            flops=8 * 10**9,
            far_out=(0, 1, 2),
            vmem=36,
        )

        def relay_two(first):
            right = lax.ppermute(first[0], "tensor", [(i, i + 1) for i in range(1, tensor_size - 1)])
            left = lax.ppermute(first[1], "tensor", [(i, i - 1) for i in range(1, tensor_size - 1)])
            return [right, left]

        def relay_one(chunk):
            right = lax.ppermute(chunk, "tensor", [(i, i + 1) for i in range(tensor_size - 1)])
            left = lax.ppermute(chunk, "tensor", [(i + 1, i) for i in range(tensor_size - 1)])
            return [right, left]

        def relay_three(second):
            return [lax.ppermute(jnp.where(line >= 2, second[0], second[1]), "tensor", [(2, 3), (1, 0)])]

        def gather_units(far, deps):
            spec = pl.BlockSpec((1, length, width), lambda i, ref: (i, 0, 0), memory_space=pltpu.VMEM)
            (out,) = kernel_call(
                assemble,
                "assemble",
                [scalars],
                [*far, *deps],
                [whole((rows, width))] * 6 + [ANYWHERE] * len(deps),
                [shaped(seq_count, length, width)],
                [pltpu.VMEM((length, width), F32)],
                out_specs=(spec,),
                grid=2,
            )
            return out

        out_all = lax.all_gather(out_low, "tensor")
        piece = pl.BlockSpec((1, tensor_size, rest_rows, width), lambda i: (i, 0, 0, 0), memory_space=pltpu.VMEM)
        rest_half = kernel_call(
            add_parts,
            "add_parts",
            [],
            [keep, over_batch(send, 1)],
            [piece] * 2,
            [shaped(tensor_size, rest_rows, width)] * 4,
            grid=4,
        )

        dqkv_first, keep, message, alpha_first = run_backward(
            heads, scalars, entmax_alpha, normed, qkv_first, tau_first, starts, dattended, 0, 1, tensor_size, [], []
        )
        dqkv_rest, keep, message, alpha_rest = run_backward(
            heads, scalars, alphas, normed, qkv_rest, tau_rest, starts, dattended, 1, tensor_size - 1, tensor_size,
            [keep, message], list(rest_half),
        )
        def call(body, name, operands, out_shapes):
            return kernel_call(
                functools.partial(body, tensor_size),
                name,
                [],
                operands,
                [whole(array.shape) for array in operands],
                out_shapes,
            )

        def chip_exchange(pieces):
            return [over_batch(pieces[hop // 2], hop) for hop in (2, 4, 6)]

        rest_sum = call(
            sum_rest,
            "sum_rest",
            [rest_half[0]] + chip_exchange(rest_half),
            [shaped(rest_rows, width, dtype=F32)] + [shaped(rest_rows, width)] * (tensor_size - 1),
        )
        if batch_size > PLANE:
            rest_sum = [upper_sum(one, False).astype(one.dtype) for one in rest_sum]
        rest_sum = [rest_sum[0]] + [over_tensor(rest_sum[hop], hop) for hop in range(1, tensor_size)]

        operands = [tokens, dresid, row(ln1_gain), small_two, dqkv_first[0], dqkv_rest, weight_first[0], weight_rest]
        operands += [alpha_first[0], alpha_rest]
        grad_chunk, message, small = kernel_call(
            functools.partial(finish, tensor_size, heads),
            "finish",
            [],
            operands + [message, rest_sum[0]],
            [whole(array.shape) for array in operands] + [ANYWHERE] * 2,
            [shaped(rows, width), shaped(*message.shape), shaped(2 * SMALL, span, dtype=F32)],
            out_specs=(
                whole((rows, width)),
                pl.BlockSpec((1, part, span), lambda *_: (4 * tensor_size, 0, 0), memory_space=pltpu.VMEM),
                whole((2 * SMALL, span)),
            ),
            aliases={len(operands): 1},
        )
        grad_one = relay_one(grad_chunk)
        grad_two = relay_two(grad_one)
        grad_far = [grad_chunk] + grad_one + grad_two + relay_three(grad_two)

        halves = call(
            sum_core,
            "sum_core",
            [keep, over_batch(message, 1), small],
            [shaped(tensor_size + 1, part, span)] * 4 + [shaped(2 * SMALL, span, dtype=F32)],
        )
        totals = call(
            sum_plane,
            "sum_plane",
            [halves[0]] + chip_exchange(halves) + [halves[4]],
            [shaped(part, span, dtype=F32)]
            + [shaped(2 * part, span)] * (tensor_size - 1)
            + [shaped(2 * SMALL, span, dtype=F32)],
        )
        small = totals[-1]
        if batch_size > PLANE:
            small = upper_sum(small, True)
            rest = [upper_sum(one[:part], False).astype(BF16) for one in totals[1:-1]]
            rest = [jnp.concatenate([one, split_wide(small)]) for one in rest]
            totals = [upper_sum(totals[0], False)] + rest
        qkv_sum = [totals[0]] + [over_tensor(totals[hop], hop) for hop in range(1, tensor_size)]
        gathered, common = call(
            sum_line,
            "sum_line",
            rest_sum + qkv_sum + [small],
            [shaped(rest_rows + part, width), shaped(8, width, dtype=F32)],
        )
        spec = pl.BlockSpec((1, length, width), lambda i, ref: (i, 0, 0), memory_space=pltpu.VMEM)
        (output,) = kernel_call(
            assemble_all,
            "assemble_all",
            [scalars],
            [out_all, gathered],
            [pl.BlockSpec((2, rows, width), lambda i, ref: (i, 0, 0), memory_space=pltpu.VMEM), ANYWHERE],
            [shaped(seq_count, length, width)],
            out_specs=(spec,),
            grid=seq_count,
        )
        gathered = jnp.stack(chip_gather(gathered))
        other = over_batch(gathered, 1)
        grad_w_qkv, grad_w_out, grad_w_up, grad_w_down = kernel_call(
            functools.partial(unpack, out_part, up_part),
            "unpack",
            [scalars],
            [gathered, other],
            [whole(gathered.shape)] * 2,
            [
                shaped(3, width, columns, dtype=F32),
                shaped(columns, width, dtype=F32),
                shaped(width, hidden, dtype=F32),
                shaped(hidden, width, dtype=F32),
            ],
            [pltpu.VMEM((hidden, width), F32)],
        )
        grad_input = gather_units(grad_far, [grad_w_qkv])
        return (
            output,
            grad_input,
            common[0],
            common[1],
            grad_w_qkv,
            common[6, :heads],
            grad_w_out,
            common[2],
            common[3],
            grad_w_up,
            common[5],
            grad_w_down,
            common[4],
        )

    return jax.shard_map(
        shards,
        mesh=mesh,
        in_specs=(
            P("batch", None, None),
            P("batch", None),
            P(),
            P(),
            P(None, None, "tensor"),
            P("tensor"),
            P("tensor", None),
            P(),
            P(),
            P(None, "tensor"),
            P("tensor"),
            P("tensor", None),
            P(),
            P("batch", None, None),
        ),
        out_specs=(
            P("batch", None, None),
            P("batch", None, None),
            P(),
            P(),
            P(None, None, "tensor"),
            P("tensor"),
            P("tensor", None),
            P(),
            P(),
            P(None, "tensor"),
            P("tensor"),
            P("tensor", None),
            P(),
        ),
        check_vma=False,
    )
```

```python
import functools

import jax
import jax.numpy as jnp
from jax import lax
from jax.experimental import pallas as pl
from jax.experimental.pallas import tpu as pltpu
from jax.sharding import PartitionSpec as P

BISECT = 10
MASKED = -10000.0
NORM_EPS = 1e-05
LN2 = 0.6931471805599453
TILE = 128
EXTRA = 16
SMALL = 16
PLANE = 8
MIB = 1024 * 1024
BF16 = jnp.bfloat16
F32 = jnp.float32
GELU_A = 0.7978845608028654
GELU_B = 0.044715


def layer_norm(values, norm_gain, norm_shift):
    centre = values - jnp.mean(values, axis=-1, keepdims=True)
    spread = jnp.mean(centre * centre, axis=-1, keepdims=True)
    return centre * lax.rsqrt(spread + NORM_EPS) * norm_gain + norm_shift


def dot_nt(left, right):
    return lax.dot_general(left, right, (((1,), (1,)), ((), ())), preferred_element_type=F32)


def dot_nn(left, right):
    return lax.dot_general(left, right, (((1,), (0,)), ((), ())), preferred_element_type=F32)


def dot_tn(left, right):
    return lax.dot_general(left, right, (((0,), (0,)), ((), ())), preferred_element_type=F32)


def tile_mask(first, starts_ref):
    keys = lax.broadcasted_iota(jnp.int32, (first + TILE, TILE), 0)
    queries = lax.broadcasted_iota(jnp.int32, (first + TILE, TILE), 1) + first
    return (keys <= queries) & (keys >= starts_ref[:, first : first + TILE])


def head_lanes(values, head):
    lanes = lax.broadcasted_iota(jnp.int32, values.shape, 1)
    return jnp.where((lanes >= head * 64) & (lanes < head * 64 + 64), values, jnp.zeros_like(values))


def rolled(values, shift, rows):
    return pltpu.roll(values, shift, 0)[:rows]


def prepare_cotangent(scalars_ref, cotangent_ref, dep_ref, cot_ref):
    shift = scalars_ref[5]
    cot_ref[...] = rolled(cotangent_ref[0].astype(F32), shift, cot_ref.shape[0]).astype(BF16)


def prepare(scalars_ref, inputs_ref, gain_ref, bias_ref, tokens_ref, normed_ref):
    rows, length = tokens_ref.shape[0], inputs_ref.shape[1]
    shift = scalars_ref[5]
    tokens = rolled(inputs_ref[0].astype(F32), shift, rows)
    tokens_ref[...] = tokens.astype(BF16)
    normed_ref[...] = layer_norm(tokens, gain_ref[...], bias_ref[...]).astype(BF16)


def pack_qkv(place_ref, weight_ref, bias_ref, alpha_ref, out_ref):
    part, columns = weight_ref.shape[1:]
    for index in range(3):
        out_ref[:part, index * columns : (index + 1) * columns] = weight_ref[index]
    lanes = lax.broadcasted_iota(jnp.int32, (1, 2 * columns), 1)
    alphas = jnp.zeros((1, 2 * columns), F32)
    for head in range(alpha_ref.shape[0]):
        alphas = jnp.where(lanes == head, alpha_ref[head], alphas)
    rest = jnp.concatenate([bias_ref[:, 3 * columns :], alphas], axis=1)
    values = jnp.concatenate([bias_ref[:, : 3 * columns], rest])
    high = values.astype(BF16).astype(F32)
    middle = (values - high).astype(BF16).astype(F32)
    low = values - high - middle
    blank = jnp.zeros((EXTRA - 6, 3 * columns), F32)
    out_ref[part:, :] = jnp.concatenate([high, middle, low, blank]).astype(BF16)


def pack_rest(place_ref, out_weight_ref, up_ref, down_ref, *refs):
    part_ref, turned_ref, turn_ref = refs[-3:]
    out_part = out_weight_ref.shape[0]
    up_part = down_ref.shape[0]
    turn_ref[...] = jnp.transpose(up_ref[...].astype(F32))
    turned_ref[...] = turn_ref[...].astype(BF16)
    rows = pl.ds(pl.multiple_of(place_ref[0] * up_part, up_part), up_part)
    part_ref[:out_part, :] = out_weight_ref[...]
    part_ref[out_part : out_part + up_part, :] = turn_ref[rows, :].astype(BF16)
    part_ref[out_part + up_part :, :] = down_ref[...]


def stack_four(*refs):
    for index in range(4):
        refs[-1][index] = refs[index][...]


def assemble(other, scalars_ref, own_ref, right_one, left_one, right_two, left_two, far_ref, *refs):
    out_ref, both_ref = refs[-2:]
    pair = scalars_ref[1] ^ other
    rows = own_ref.shape[0]
    sources = ((own_ref, 0), (right_one, -1), (left_one, 1), (right_two, -2), (left_two, 2), (far_ref, 3), (far_ref, -3))
    for half in range(2):
        away = 2 * pair + half - scalars_ref[2]
        for ref, distance in sources:

            @pl.when(away == distance)
            def _():
                both_ref[half * rows : (half + 1) * rows, :] = ref[...].astype(F32)

    out_ref[0] = pltpu.roll(both_ref[...], scalars_ref[3 + pair], 0).astype(BF16)


def assemble_all(scalars_ref, all_ref, *refs):
    rows = all_ref.shape[1]
    both = all_ref[...].reshape(2 * rows, all_ref.shape[2]).astype(F32)
    refs[-1][0] = pltpu.roll(both, scalars_ref[3 + pl.program_id(0)], 0).astype(BF16)


def add_parts(keep_ref, sent_ref, *out_refs):
    for index, ref in enumerate(out_refs):

        @pl.when(pl.program_id(0) == index)
        def _():
            ref[...] = (keep_ref[0].astype(F32) + sent_ref[0].astype(F32)).astype(BF16)


def attend_forward(heads, base, weight_count, dep_count, scalars_ref, alpha_ref, normed_ref, starts_ref, *refs):
    slot = (base + pl.program_id(0)) * heads
    weight_refs = refs[:weight_count]
    qkv_ref, weight_out_ref, attended_ref, tau_ref, shifted_ref = refs[weight_count + dep_count :]
    rows = normed_ref.shape[0]
    if weight_count == 1:
        (weight_ref,) = weight_refs
        for index in range(3):
            weight_out_ref[:, index * heads * 64 : (index + 1) * heads * 64] = weight_ref[index]
    else:
        for core, weight_ref in enumerate(weight_refs):
            part = weight_ref.shape[1]
            for chip in range(4):
                row = pl.multiple_of((scalars_ref[0] ^ (2 * chip + core)) * part, part)
                weight_out_ref[pl.ds(row, part), :] = weight_ref[chip]
    width = heads * 64
    qkv = dot_nn(normed_ref[...], weight_out_ref[...]).astype(BF16)
    qkv_ref[...] = qkv
    queries = qkv[:, :width]
    keys = qkv[:, width : 2 * width]
    values_t = jnp.transpose(qkv[:, 2 * width :].astype(F32)).astype(BF16)
    tiles = [(h, first) for h in range(heads) for first in range(0, rows, TILE)]
    offsets = []
    total = 0
    for h, first in tiles:
        offsets.append(total)
        total += first + TILE
    highs, counts = [], []
    for (h, first), offset in zip(tiles, offsets):
        alpha_minus = alpha_ref[slot + h] - 1.0
        query = head_lanes(queries[first : first + TILE], h)
        scores = dot_nt(keys[: first + TILE], query) * 0.125
        shifted = jnp.where(tile_mask(first, starts_ref), alpha_minus * scores, MASKED)
        shifted_ref[offset : offset + first + TILE, :] = shifted
        spots = lax.broadcasted_iota(jnp.int32, (1, TILE), 1) + (first + 1)
        counts.append((spots - starts_ref[:, first : first + TILE]).astype(F32))
        highs.append(jnp.max(shifted, axis=0, keepdims=True))
    alpha_rows = jnp.concatenate(
        [jnp.full((rows // TILE, TILE), alpha_ref[slot + h] - 1.0, F32) for h in range(heads)]
    )
    bottom = jnp.concatenate(highs) - 1.0
    bracket = jnp.concatenate(highs) - jnp.exp(-alpha_rows * jnp.log(jnp.concatenate(counts))) - bottom
    cell = bracket * (1.0 / 2**BISECT)
    top = float(2**BISECT - 1)

    def evaluate(point):
        sums, slopes = [], []
        for index, ((h, first), offset) in enumerate(zip(tiles, offsets)):
            power = (1.0 / (alpha_ref[slot + h] - 1.0) - 1.0) * (1.0 / LN2)
            margin = jnp.maximum(shifted_ref[offset : offset + first + TILE, :] - point[index : index + 1], 0.0)
            slope = jnp.exp2(power * jnp.log(margin))
            slopes.append(jnp.sum(slope, axis=0, keepdims=True))
            sums.append(jnp.sum(slope * margin, axis=0, keepdims=True))
        return jnp.concatenate(sums), jnp.concatenate(slopes)

    def newton(point, sums, slopes):
        return point + (sums - jnp.exp((1.0 - alpha_rows) * jnp.log(sums))) / slopes

    def index_of(point):
        return jnp.clip(jnp.floor((point - bottom) / jnp.maximum(cell, 1e-30)), 0.0, top)

    point = bottom + 0.5 * bracket
    for _ in range(3):
        point = jnp.maximum(newton(point, *evaluate(point)), bottom)

    def unsettled(state):
        return state[1] > 0.0

    def settle(state):
        spot = state[0]
        after = bottom + (spot + 1.0) * cell
        sums, slopes = evaluate(after)
        higher = (sums >= 1.0) & (spot < top) & (after > bottom + spot * cell)
        spot = jnp.where(higher, jnp.maximum(spot + 1.0, index_of(newton(after, sums, slopes))), spot)
        return spot, jnp.max(jnp.where(higher, 1.0, 0.0))

    spot, _ = lax.while_loop(unsettled, settle, (index_of(point), jnp.float32(1.0)))
    low_rows = bottom + spot * cell
    lows = [low_rows[index : index + 1] for index in range(len(tiles))]
    for (h, first), offset, low in zip(tiles, offsets, lows):
        exponent = 1.0 / (alpha_ref[slot + h] - 1.0)
        shifted = shifted_ref[offset : offset + first + TILE, :]
        margin = jnp.maximum(shifted - low, 0.0)
        slope = jnp.exp2((exponent - 1.0) * (1.0 / LN2) * jnp.log(margin))
        slopes = exponent * jnp.sum(slope, axis=0, keepdims=True)
        summed = jnp.sum(slope * margin, axis=0, keepdims=True)
        tau = low + (summed - 1.0) / slopes
        tau_ref[h : h + 1, first : first + TILE] = tau
        margin = jnp.maximum(shifted - tau, 0.0)
        probs = jnp.exp2(exponent * (1.0 / LN2) * jnp.log(margin)).astype(BF16)
        out = dot_nn(values_t[h * 64 : h * 64 + 64, : first + TILE], probs)
        attended_ref[first : first + TILE, h * 64 : h * 64 + 64] = jnp.transpose(out).astype(BF16)


def attend_backward(heads, base, scalars_ref, alpha_ref, normed_ref, qkv_ref, tau_ref, starts_ref, dattended_ref, *refs):
    slot = (base + pl.program_id(0)) * heads
    dqkv_ref, keep_ref, send_ref, dalpha_ref, dkeys_ref, dvalues_ref, grad_ref = refs[-7:]
    rows = normed_ref.shape[0]
    width = heads * 64
    queries = qkv_ref[:, :width]
    keys = qkv_ref[:, width : 2 * width]
    values = qkv_ref[:, 2 * width :]
    keys_t = jnp.transpose(keys.astype(F32)).astype(BF16)
    dkeys_ref[...] = jnp.zeros_like(dkeys_ref)
    dvalues_ref[...] = jnp.zeros_like(dvalues_ref)
    for h in range(heads):
        alpha_minus = alpha_ref[slot + h] - 1.0
        exponent = 1.0 / alpha_minus
        dalpha = jnp.zeros((1, TILE), F32)
        for first in range(0, rows, TILE):
            end = first + TILE
            query = head_lanes(queries[first:end], h)
            dout = head_lanes(dattended_ref[first:end, :], h)
            scores = dot_nt(keys[:end], query) * 0.125
            shifted = jnp.where(tile_mask(first, starts_ref), alpha_minus * scores, MASKED)
            margin = jnp.maximum(shifted - tau_ref[h : h + 1, first:end], 0.0)
            log_margin = jnp.log(margin)
            slope = jnp.exp2((exponent - 1.0) * (1.0 / LN2) * log_margin)
            probs = slope * margin
            slope = exponent * slope
            dprobs = dot_nt(values[:end], dout)
            slope_sum = jnp.sum(slope, axis=0, keepdims=True)
            mixed = jnp.sum(slope * dprobs, axis=0, keepdims=True)
            centred = dprobs - mixed / slope_sum
            log_margin = jnp.where(margin > 0.0, log_margin, 0.0)
            alpha_part = slope * scores - (exponent * exponent) * (probs * log_margin)
            dalpha = dalpha + jnp.sum(alpha_part * centred, axis=0, keepdims=True)
            dscores = (alpha_minus * (slope * centred)).astype(BF16)
            dvalues_ref[:end, :] += dot_nn(probs.astype(BF16), dout)
            dkeys_ref[:end, :] += dot_nn(dscores, query)
            dquery_t = dot_nn(keys_t[h * 64 : h * 64 + 64, :end], dscores) * 0.125
            dqkv_ref[first:end, h * 64 : h * 64 + 64] = jnp.transpose(dquery_t).astype(BF16)
        dalpha_ref[h : h + 1, :] = dalpha
    dqkv_ref[:, width : 2 * width] = (dkeys_ref[...] * 0.125).astype(BF16)
    dqkv_ref[:, 2 * width :] = dvalues_ref[...].astype(BF16)
    grad = dot_tn(normed_ref[...], dqkv_ref[...]).astype(BF16)
    grad_ref[...] = grad.reshape(grad_ref.shape)
    for chip in range(4):
        keep_ref[chip] = grad_ref[scalars_ref[0] ^ (2 * chip)]
        send_ref[chip] = grad_ref[scalars_ref[0] ^ (2 * chip + 1)]


def norm_back(values, gain, dnormed):
    centre = values - jnp.mean(values, axis=-1, keepdims=True)
    scale = lax.rsqrt(jnp.mean(centre * centre, axis=-1, keepdims=True) + NORM_EPS)
    unit = centre * scale
    scaled = dnormed * gain
    mean = jnp.mean(scaled, axis=-1, keepdims=True)
    mixed = jnp.mean(scaled * unit, axis=-1, keepdims=True)
    dvalues = scale * (scaled - mean - unit * mixed)
    return dvalues, jnp.sum(dnormed * unit, axis=0, keepdims=True), jnp.sum(dnormed, axis=0, keepdims=True)


def feed_forward(slots, scalars_ref, tokens_ref, cot_ref, gain_ref, bias_ref, up_bias_ref, down_bias_ref, *refs):
    attended_refs = refs[:2]
    out_own, up_own, down_own, far_zero, far_one = refs[2:7]
    out_ref, dresid_ref, dattended_ref, keep_ref, send_ref, small_ref = refs[7:13]
    w_out, w_up, w_down, sums, dnormed_ref, grad_out, grad_up, grad_down, copies = refs[13:]
    place = scalars_ref[0]
    out_part = w_out.shape[1] // PLANE
    up_part = w_up.shape[1] // PLANE
    out_moves = [(out_own, w_out.at[0])]
    moves = [(up_own, w_up.at[0]), (down_own, w_down.at[0])]
    for core, far in enumerate((far_zero, far_one)):
        for chip in range(4):
            spot = place ^ (2 * chip + core)
            out_rows = pl.ds(pl.multiple_of(spot * out_part, out_part), out_part)
            up_rows = pl.ds(pl.multiple_of(spot * up_part, up_part), up_part)
            out_moves.append((far.at[chip, :, :out_part], w_out.at[1:, out_rows]))
            moves.append((far.at[chip, :, out_part : out_part + up_part], w_up.at[1:, up_rows]))
            moves.append((far.at[chip, :, out_part + up_part :], w_down.at[1:, up_rows]))
    started = []

    def begin(source, target):
        copy = pltpu.make_async_copy(source, target, copies.at[len(started)])
        copy.start()
        started.append(copy)

    for source, target in out_moves + moves:
        begin(source, target)
    for copy in started[: len(out_moves)]:
        copy.wait()

    width = tokens_ref.shape[1]
    attended = jnp.concatenate([ref[...] for ref in attended_refs], axis=1)
    out_weights = w_out[...].reshape(slots * w_out.shape[1], width)
    resid = tokens_ref[...].astype(F32) + dot_nn(attended, out_weights)
    sums[...] = resid
    normed = layer_norm(resid, gain_ref[...], bias_ref[...]).astype(BF16)
    dnormed_ref[...] = jnp.zeros_like(dnormed_ref)
    cot = cot_ref[...]
    for copy in started[len(out_moves) :]:
        copy.wait()
    for slot in range(slots):
        pre = dot_nt(normed, w_up[slot]) + up_bias_ref[slot : slot + 1, :]
        square = pre * pre
        bend = jnp.tanh(pre * (GELU_A + GELU_A * GELU_B * square))
        half = 0.5 + 0.5 * bend
        act = (pre * half).astype(BF16)
        slope = half + (0.5 * pre) * (1.0 - bend * bend) * (GELU_A + 3.0 * GELU_A * GELU_B * square)
        sums[...] += dot_nn(act, w_down[slot])
        dpre = (dot_nt(cot, w_down[slot]) * slope).astype(BF16)
        small_ref[3 + slot : 4 + slot, :] = jnp.sum(dpre.astype(F32), axis=0, keepdims=True)
        dnormed_ref[...] += dot_nn(dpre, w_up[slot])
        grad_down[slot] = dot_tn(act, cot).astype(BF16).reshape(PLANE, up_part, width)
        grad_up[slot] = dot_tn(dpre, normed).astype(BF16).reshape(PLANE, up_part, width)
    out_ref[...] = (sums[...] + down_bias_ref[...]).astype(BF16)
    dresid, small_ref[0:1, :], small_ref[1:2, :] = norm_back(resid, gain_ref[...], dnormed_ref[...])
    cot_full = cot.astype(F32)
    small_ref[2:3, :] = jnp.sum(cot_full, axis=0, keepdims=True)
    dresid = cot_full + dresid
    dresid_ref[...] = dresid
    dresid_low = dresid.astype(BF16)
    dattended_ref[...] = dot_nt(dresid_low, out_weights).astype(BF16)
    grad_out[...] = dot_tn(attended, dresid_low).astype(BF16).reshape(grad_out.shape)
    for core, target in enumerate((keep_ref, send_ref)):
        for chip in range(4):
            spot = place ^ (2 * chip + core)
            for slot in range(slots):
                target[chip, slot, :out_part] = grad_out[slot, spot]
                target[chip, slot, out_part : out_part + up_part] = grad_up[slot, spot]
                target[chip, slot, out_part + up_part :] = grad_down[slot, spot]


def finish(slots, heads, tokens_ref, dresid_ref, gain_ref, two_ref, *refs):
    dqkv_first, dqkv_rest, weight_first, weight_rest, alpha_first, alpha_rest = refs[:6]
    out_ref, message_ref, small_ref = refs[-3:]
    dqkv = jnp.concatenate([dqkv_first[...]] + [dqkv_rest[slot] for slot in range(slots - 1)], axis=1)
    weights = jnp.concatenate([weight_first[...]] + [weight_rest[slot] for slot in range(slots - 1)], axis=1)
    dnormed = dot_nt(dqkv, weights)
    dinput, gain, bias = norm_back(tokens_ref[...].astype(F32), gain_ref[...], dnormed)
    out_ref[...] = (dresid_ref[...] + dinput).astype(BF16)
    width = gain.shape[1]
    lanes = lax.broadcasted_iota(jnp.int32, (1, width), 1)
    alphas = []
    for slot in range(slots):
        values = alpha_first[...] if slot == 0 else alpha_rest[slot - 1]
        totals = jnp.sum(values, axis=1, keepdims=True)
        line = jnp.zeros((1, width), F32)
        for head in range(heads):
            line = jnp.where(lanes == head, totals[head : head + 1], line)
        alphas.append(line)
    blank = jnp.zeros((SMALL - 5 - 2 * slots, width), F32)
    values = jnp.concatenate([gain, bias, two_ref[...]] + alphas + [blank])
    span = message_ref.shape[2]
    side = jnp.concatenate([values[:, span:], jnp.zeros((SMALL, 2 * span - width), F32)], axis=1)
    small = jnp.concatenate([values[:, :span], side])
    small_ref[...] = small
    message_ref[0] = pair_of(small)


def pair_of(values):
    high = values.astype(BF16)
    return jnp.concatenate([high, (values - high.astype(F32)).astype(BF16)])


def value_of(pair):
    half = pair.shape[0] // 2
    return pair[:half].astype(F32) + pair[half:].astype(F32)


def tree(four):
    return (four[0] + four[1]) + (four[2] + four[3])


def sum_core(slots, keep_ref, received_ref, small_ref, *refs):
    total = small_ref[...] + value_of(received_ref[4 * slots])
    refs[4][...] = total
    pair = pair_of(total)
    for chip in range(4):
        for slot in range(slots):
            index = 4 * slot + chip
            refs[chip][slot] = (keep_ref[index].astype(F32) + received_ref[index].astype(F32)).astype(BF16)
        refs[chip][slots] = pair


def gate(*refs):
    pass


def sum_plane(slots, *refs):
    rest_refs, qkv_refs, small_ref = refs[:4], refs[4:8], refs[8]
    rest_out, qkv_out, small_out = refs[9:12]
    messages = refs[12:]
    rows = rest_out.shape[0]
    part, span = qkv_out.shape
    width = rest_out.shape[1]
    small = tree([small_ref[...]] + [value_of(ref[slots]) for ref in qkv_refs[1:]])
    small = jnp.concatenate([small[:SMALL], small[SMALL:, : width - span]], axis=1)
    small_out[...] = small
    pair = pair_of(small)
    for slot in range(slots):
        rest = tree([ref[slot].astype(F32) for ref in rest_refs])
        qkv = tree([ref[slot].astype(F32) for ref in qkv_refs])
        if slot == 0:
            rest_out[...] = rest
            qkv_out[...] = qkv
        else:
            message = messages[slot - 1]
            message[:rows] = rest.astype(BF16)
            message[rows : rows + part, :span] = qkv.astype(BF16)
            message[rows : rows + part, span:] = jnp.zeros((part, width - span), BF16)
            message[rows + part :] = pair


def sum_line(slots, rest_ref, qkv_ref, small_ref, *refs):
    received, out_ref, total_ref = refs[: slots - 1], refs[-2], refs[-1]
    rows = rest_ref.shape[0]
    part, span = qkv_ref.shape
    width = rest_ref.shape[1]
    out_ref[:rows] = tree([rest_ref[...]] + [ref[:rows].astype(F32) for ref in received]).astype(BF16)
    qkv = [ref[rows : rows + part, :span].astype(F32) for ref in received]
    out_ref[rows:, :span] = tree([qkv_ref[...]] + qkv).astype(BF16)
    out_ref[rows:, span:] = jnp.zeros((part, width - span), BF16)
    smalls = [small_ref[...]] + [value_of(ref[rows + part :]) for ref in received]
    common = tree([one[:5] for one in smalls])
    bias = tree([one[5 + slot : 6 + slot] for slot, one in enumerate(smalls)])
    alpha = tree([one[5 + slots + slot : 6 + slots + slot] for slot, one in enumerate(smalls)])
    total_ref[...] = jnp.concatenate([common, bias, alpha, jnp.zeros((1, width), F32)])


def unpack(out_part, up_part, scalars_ref, zero_ref, one_ref, qkv_ref, out_ref, up_ref, down_ref, turn_ref):
    columns = qkv_ref.shape[2]
    for core, ref in enumerate((zero_ref, one_ref)):
        for chip in range(4):
            spot = scalars_ref[0] ^ (2 * chip + core)
            out_rows = pl.ds(pl.multiple_of(spot * out_part, out_part), out_part)
            up_rows = pl.ds(pl.multiple_of(spot * up_part, up_part), up_part)
            first = out_part
            out_ref[out_rows, :] = ref[chip, :first].astype(F32)
            turn_ref[up_rows, :] = ref[chip, first : first + up_part].astype(F32)
            first = first + up_part
            down_ref[up_rows, :] = ref[chip, first : first + up_part].astype(F32)
            first = first + up_part
            part = ref.shape[1] - first
            qkv_rows = pl.ds(pl.multiple_of(spot * part, part), part)
            for index in range(3):
                qkv_ref[index, qkv_rows, :] = ref[chip, first:, index * columns : (index + 1) * columns].astype(F32)
    up_ref[...] = jnp.transpose(turn_ref[...])


def whole(shape):
    return pl.BlockSpec(shape, lambda *_: (0,) * len(shape), memory_space=pltpu.VMEM)


def kernel_call(body, name, scalars, operands, in_specs, out_shapes, scratch=(), out_specs=None, grid=1, flops=10**9, vmem=16,
                aliases=None, far_in=False, far_out=()):
    spec = pltpu.PrefetchScalarGridSpec(
        num_scalar_prefetch=len(scalars),
        grid=(grid,),
        in_specs=in_specs,
        out_specs=out_specs or tuple(whole(shape.shape) for shape in out_shapes),
        scratch_shapes=list(scratch),
    )
    far = lambda array: pltpu.with_memory_space_constraint(array, pltpu.HBM) if far_in else array
    return pl.pallas_call(
        body,
        out_shape=tuple(
            pltpu.HBM(shape.shape, shape.dtype) if index in far_out else shape for index, shape in enumerate(out_shapes)
        ),
        grid_spec=spec,
        compiler_params=pltpu.CompilerParams(vmem_limit_bytes=vmem * MIB),
        input_output_aliases=aliases or {},
        cost_estimate=pl.CostEstimate(flops=flops, bytes_accessed=10**6, transcendentals=0),
        name=name,
    )(*map(far, scalars), *map(far, operands))


def shaped(*shape, dtype=BF16):
    return jax.ShapeDtypeStruct(shape, dtype)


ANYWHERE = pl.BlockSpec(memory_space=pl.ANY)


def run_forward(heads, scalars, alpha, normed, weights, base, count, starts, deps):
    rows, width = normed.shape
    columns = 3 * heads * 64
    total = heads * sum(range(TILE, rows + 1, TILE))
    stacked = lambda *shape: pl.BlockSpec((None,) + shape, lambda i, *_: (i, 0, 0), memory_space=pltpu.VMEM)
    if base == 0:
        weight_specs = [whole(weights[0].shape)]
    else:
        block = (4, None) + weights[0].shape[2:]
        weight_specs = [pl.BlockSpec(block, lambda i, *_: (0, i, 0, 0), memory_space=pltpu.VMEM)] * 2
    smem = pl.BlockSpec(memory_space=pltpu.SMEM)
    return kernel_call(
        functools.partial(attend_forward, heads, base, len(weights), len(deps)),
        "attend_forward",
        [scalars],
        [alpha, normed, starts, *weights, *deps],
        [smem, whole(normed.shape), whole(starts.shape)] + weight_specs + [ANYWHERE] * len(deps),
        [
            shaped(count, rows, columns),
            shaped(count, width, columns),
            shaped(rows, count * heads * 64),
            shaped(count, heads, rows, dtype=F32),
        ],
        [pltpu.VMEM((total, TILE), F32)],
        out_specs=(
            stacked(rows, columns),
            stacked(width, columns),
            pl.BlockSpec((rows, heads * 64), lambda i, *_: (0, i), memory_space=pltpu.VMEM),
            stacked(heads, rows),
        ),
        grid=count,
        flops=5 * 10**9 * count,
    )


def run_backward(heads, scalars, alpha, normed, qkv, tau, starts, dattended, base, count, slots, buffers, deps):
    rows, width = normed.shape
    columns = 3 * heads * 64
    smem = pl.BlockSpec(memory_space=pltpu.SMEM)
    stacked = lambda *shape: pl.BlockSpec((None,) + shape, lambda i, *_: (i, 0, 0), memory_space=pltpu.VMEM)
    dattended_spec = pl.BlockSpec((rows, heads * 64), lambda i, *_: (0, base + i), memory_space=pltpu.VMEM)
    parts = (width // PLANE, columns)
    message = pl.BlockSpec((4,) + parts, lambda i, *_: (base + i, 0, 0), memory_space=pltpu.VMEM)
    return kernel_call(
        functools.partial(attend_backward, heads, base),
        "attend_backward",
        [scalars],
        [alpha, normed, qkv, tau, starts, dattended, *buffers, *deps],
        [smem, whole(normed.shape), stacked(rows, columns), stacked(heads, rows), whole(starts.shape)]
        + [dattended_spec]
        + [ANYWHERE] * (len(buffers) + len(deps)),
        [
            shaped(count, rows, columns),
            shaped(4 * slots, *parts),
            shaped(4 * slots + 1, *parts),
            shaped(count, heads, TILE, dtype=F32),
        ],
        [
            pltpu.VMEM((rows, heads * 64), F32),
            pltpu.VMEM((rows, heads * 64), F32),
            pltpu.VMEM((PLANE,) + parts, BF16),
        ],
        out_specs=(stacked(rows, columns), message, message, stacked(heads, TILE)),
        grid=count,
        flops=4 * 10**9 * count,
        aliases={7: 1, 8: 2} if buffers else None,
        far_in=True,
    )


def split_wide(values):
    high = lax.reduce_precision(values, exponent_bits=8, mantissa_bits=7)
    return jnp.concatenate([high.astype(BF16), (values - high).astype(BF16)])


def join_wide(pair):
    pair = pair.astype(F32)
    half = pair.shape[0] // 2
    return pair[:half] + pair[half:]


def solution(mesh):
    batch_size = mesh.shape["batch"]
    tensor_size = mesh.shape["tensor"]

    def over_batch(array, hop):
        return lax.ppermute(array, "batch", [(i, i ^ hop) for i in range(batch_size)])

    def over_tensor(array, hop):
        return lax.ppermute(array, "tensor", [(i, i ^ hop) for i in range(tensor_size)])

    def line_gather(part):
        return [over_tensor(part, hop) for hop in range(1, tensor_size)]

    def chip_gather(part):
        return [part] + [over_batch(part, hop) for hop in (2, 4, 6)]

    def upper_sum(array, split):
        hop = PLANE
        while hop < batch_size:
            array = array + join(over_batch(cut(array, split), hop), split)
            hop *= 2
        return array

    def cut(array, split):
        return split_wide(array) if split else array.astype(BF16)

    def join(array, split):
        return join_wide(array) if split else array.astype(F32)

    def shards(inputs, doc_lengths, ln1_gain, ln1_bias, w_qkv, entmax_alpha, w_out, ln2_gain, ln2_bias,
               w_up, up_bias, w_down, down_bias, cotangent):
        seq_count, length, width = inputs.shape
        heads = entmax_alpha.shape[0]
        hidden = w_up.shape[1]
        rows = length // 2
        columns = heads * 64
        place = lax.axis_index("batch") % PLANE
        line = lax.axis_index("tensor")

        def own_part(array):
            return lax.dynamic_slice_in_dim(array, place * (array.shape[0] // PLANE), array.shape[0] // PLANE)

        out_part = w_out.shape[0] // PLANE
        up_part = hidden // PLANE
        part = width // PLANE
        span = 3 * columns
        rest_rows = out_part + 2 * up_part
        spot = place.reshape(1).astype(jnp.int32)
        row = lambda array: array.reshape(1, -1)
        by_place = lambda rows: pl.BlockSpec((rows, width), lambda i, ref: (ref[0], 0), memory_space=pltpu.VMEM)

        (qkv_part,) = kernel_call(
            pack_qkv,
            "pack_qkv",
            [spot],
            [w_qkv, row(up_bias), entmax_alpha],
            [
                pl.BlockSpec((3, part, columns), lambda i, ref: (0, ref[0], 0), memory_space=pltpu.VMEM),
                whole((1, hidden)),
                pl.BlockSpec(memory_space=pltpu.SMEM),
            ],
            [shaped(part + EXTRA, span)],
            far_in=True,
        )
        qkv_line = line_gather(qkv_part)
        extras = [far[part : part + 6].astype(F32) for far in qkv_line]
        extras = [(far[:2] + far[2:4] + far[4:]).reshape(-1) for far in extras]
        alphas = jnp.concatenate([entmax_alpha] + [far[hidden : hidden + heads] for far in extras])
        up_biases = jnp.stack([up_bias] + [far[:hidden] for far in extras])
        qkv_far = chip_gather(jnp.stack([far[:part] for far in qkv_line]))

        ends = jnp.cumsum(doc_lengths, axis=1)
        firsts = ends - doc_lengths
        big = jnp.sum(jnp.where(doc_lengths == rows, firsts, 0), axis=1)

        def unit_start(unit):
            return (jnp.take(big, unit // 2) + rows * (unit % 2)) % length

        start = unit_start(line)
        doc_places = (jnp.take(firsts, line // 2, axis=0) - start) % length
        spots = jnp.arange(rows, dtype=jnp.int32)
        starts = jnp.max(
            jnp.where(doc_places[:, None] <= spots[None, :], doc_places[:, None], 0), axis=0, keepdims=True
        )
        scalars = jnp.stack([place, line // 2, line, big[0], big[1], (length - start) % length]).astype(jnp.int32)

        rest_part, up_own = kernel_call(
            pack_rest,
            "pack_rest",
            [spot],
            [w_out, w_up, w_down],
            [by_place(out_part), whole(w_up.shape), by_place(up_part)],
            [shaped(rest_rows, width), shaped(hidden, width)],
            [pltpu.VMEM((hidden, width), F32)],
        )
        rest_line = line_gather(rest_part)

        sequence = pl.BlockSpec((1, length, width), lambda i, ref: (ref[1], 0, 0), memory_space=pltpu.VMEM)
        tokens, normed = kernel_call(
            prepare,
            "prepare",
            [scalars],
            [inputs, row(ln1_gain), row(ln1_bias)],
            [sequence, whole((1, width)), whole((1, width))],
            [shaped(rows, width)] * 2,
        )

        def stack(pieces, deps):
            (out,) = kernel_call(
                stack_four,
                "stack_four",
                [],
                [*pieces, *deps],
                [whole(pieces[0].shape)] * 4 + [ANYWHERE] * len(deps),
                [shaped(4, *pieces[0].shape)],
            )
            return out

        qkv_first, weight_first, attended_first, tau_first = run_forward(
            heads, scalars, entmax_alpha, normed, [w_qkv], 0, 1, starts, qkv_line
        )
        qkv_zero = stack(qkv_far, [attended_first])
        (cot,) = kernel_call(
            prepare_cotangent,
            "prepare_cotangent",
            [scalars],
            [cotangent, attended_first],
            [sequence, ANYWHERE],
            [shaped(rows, width)],
        )
        qkv_one = over_batch(qkv_zero, 1)
        qkv_rest, weight_rest, attended_rest, tau_rest = run_forward(
            heads, scalars, alphas, normed, [qkv_zero, qkv_one], 1, tensor_size - 1, starts, rest_line + [cot]
        )
        rest_zero = stack(chip_gather(jnp.stack(rest_line)), [attended_rest])
        rest_one = over_batch(rest_zero, 1)
        out_low, dresid, dattended, keep, send, small_two = kernel_call(
            functools.partial(feed_forward, tensor_size),
            "feed_forward",
            [scalars],
            [tokens, cot, row(ln2_gain), row(ln2_bias), up_biases, row(down_bias)]
            + [attended_first, attended_rest]
            + [w_out, up_own, w_down, rest_zero, rest_one],
            [whole((rows, width))] * 2
            + [whole((1, width))] * 2
            + [whole((tensor_size, hidden)), whole((1, width))]
            + [whole(attended_first.shape), whole(attended_rest.shape)]
            + [ANYWHERE] * 5,
            [
                shaped(rows, width),
                shaped(rows, width, dtype=F32),
                shaped(rows, tensor_size * columns),
                shaped(4, tensor_size, rest_rows, width),
                shaped(4, tensor_size, rest_rows, width),
                shaped(3 + tensor_size, width, dtype=F32),
            ],
            [
                pltpu.VMEM((tensor_size, columns, width), BF16),
                pltpu.VMEM((tensor_size, hidden, width), BF16),
                pltpu.VMEM((tensor_size, hidden, width), BF16),
                pltpu.VMEM((rows, width), F32),
                pltpu.VMEM((rows, width), F32),
                pltpu.VMEM((tensor_size, PLANE, out_part, width), BF16),
                pltpu.VMEM((tensor_size, PLANE, up_part, width), BF16),
                pltpu.VMEM((tensor_size, PLANE, up_part, width), BF16),
                pltpu.SemaphoreType.DMA((3 + 3 * PLANE,)),
            ],
            flops=8 * 10**9,
            far_out=(0, 1, 2),
            vmem=36,
        )

        def relay_two(first):
            right = lax.ppermute(first[0], "tensor", [(i, i + 1) for i in range(1, tensor_size - 1)])
            left = lax.ppermute(first[1], "tensor", [(i, i - 1) for i in range(1, tensor_size - 1)])
            return [right, left]

        def relay_one(chunk):
            right = lax.ppermute(chunk, "tensor", [(i, i + 1) for i in range(tensor_size - 1)])
            left = lax.ppermute(chunk, "tensor", [(i + 1, i) for i in range(tensor_size - 1)])
            return [right, left]

        def relay_three(second):
            return [lax.ppermute(jnp.where(line >= 2, second[0], second[1]), "tensor", [(2, 3), (1, 0)])]

        def wait_for(arrays, others):
            return list(
                kernel_call(
                    gate,
                    "gate",
                    [],
                    [*arrays, *others],
                    [ANYWHERE] * (len(arrays) + len(others)),
                    [shaped(*array.shape) for array in arrays],
                    out_specs=(ANYWHERE,) * len(arrays),
                    aliases={index: index for index in range(len(arrays))},
                )
            )

        def gather_units(far, deps):
            out = None
            for other in range(2):
                spec = pl.BlockSpec(
                    (1, length, width), lambda i, ref: (ref[1] ^ other, 0, 0), memory_space=pltpu.VMEM
                )
                sources = [*far[:-1], far[0] if other == 0 else far[-1]]
                extra = [*deps] if other == 0 else [out]
                (out,) = kernel_call(
                    functools.partial(assemble, other),
                    "assemble",
                    [scalars],
                    sources + extra,
                    [whole((rows, width))] * 6 + [ANYWHERE] * len(extra),
                    [shaped(seq_count, length, width)],
                    [pltpu.VMEM((length, width), F32)],
                    out_specs=(spec,),
                    aliases=None if other == 0 else {7: 0},
                )
            return out

        out_all = lax.all_gather(out_low, "tensor")
        piece = pl.BlockSpec((1, tensor_size, rest_rows, width), lambda i: (i, 0, 0, 0), memory_space=pltpu.VMEM)
        rest_half = kernel_call(
            add_parts,
            "add_parts",
            [],
            [keep, over_batch(send, 1)],
            [piece] * 2,
            [shaped(tensor_size, rest_rows, width)] * 4,
            grid=4,
        )

        dqkv_first, keep, message, alpha_first = run_backward(
            heads, scalars, entmax_alpha, normed, qkv_first, tau_first, starts, dattended, 0, 1, tensor_size, [], []
        )
        dqkv_rest, keep, message, alpha_rest = run_backward(
            heads, scalars, alphas, normed, qkv_rest, tau_rest, starts, dattended, 1, tensor_size - 1, tensor_size,
            [keep, message], list(rest_half),
        )
        def call(body, name, operands, out_shapes):
            return kernel_call(
                functools.partial(body, tensor_size),
                name,
                [],
                operands,
                [whole(array.shape) for array in operands],
                out_shapes,
            )

        def chip_exchange(pieces):
            return [over_batch(pieces[hop // 2], hop) for hop in (2, 4, 6)]

        rest_far = chip_exchange(rest_half)
        operands = [tokens, dresid, row(ln1_gain), small_two, dqkv_first[0], dqkv_rest, weight_first[0], weight_rest]
        operands += [alpha_first[0], alpha_rest]
        grad_chunk, message, small = kernel_call(
            functools.partial(finish, tensor_size, heads),
            "finish",
            [],
            operands + [message],
            [whole(array.shape) for array in operands] + [ANYWHERE],
            [shaped(rows, width), shaped(*message.shape), shaped(2 * SMALL, span, dtype=F32)],
            out_specs=(
                whole((rows, width)),
                pl.BlockSpec((1, part, span), lambda *_: (4 * tensor_size, 0, 0), memory_space=pltpu.VMEM),
                whole((2 * SMALL, span)),
            ),
            aliases={len(operands): 1},
        )
        grad_one = relay_one(grad_chunk)

        (message,) = wait_for([message], rest_far)
        halves = call(
            sum_core,
            "sum_core",
            [keep, over_batch(message, 1), small],
            [shaped(tensor_size + 1, part, span)] * 4 + [shaped(2 * SMALL, span, dtype=F32)],
        )
        rest_own, qkv_own_sum, small, *messages = call(
            sum_plane,
            "sum_plane",
            [rest_half[0]] + rest_far + [halves[0]] + chip_exchange(halves) + [halves[4]],
            [
                shaped(rest_rows, width, dtype=F32),
                shaped(part, span, dtype=F32),
                shaped(SMALL, width, dtype=F32),
            ]
            + [shaped(rest_rows + part + 2 * SMALL, width)] * (tensor_size - 1),
        )
        if batch_size > PLANE:
            rest_own, qkv_own_sum = upper_sum(rest_own, False), upper_sum(qkv_own_sum, False)
            small = upper_sum(small, True)
            messages = [upper_sum(one[: rest_rows + part], False).astype(BF16) for one in messages]
            messages = [jnp.concatenate([one, split_wide(small)]) for one in messages]
        received = [over_tensor(messages[hop - 1], hop) for hop in range(1, tensor_size)]
        grad_one = wait_for(grad_one, received[:1])
        grad_two = relay_two(grad_one)
        grad_far = [grad_chunk] + grad_one + grad_two + relay_three(grad_two)
        gathered, common = call(
            sum_line,
            "sum_line",
            [rest_own, qkv_own_sum, small] + received,
            [shaped(rest_rows + part, width), shaped(8, width, dtype=F32)],
        )
        spec = pl.BlockSpec((1, length, width), lambda i, ref: (i, 0, 0), memory_space=pltpu.VMEM)
        (output,) = kernel_call(
            assemble_all,
            "assemble_all",
            [scalars],
            [out_all, gathered],
            [pl.BlockSpec((2, rows, width), lambda i, ref: (i, 0, 0), memory_space=pltpu.VMEM), ANYWHERE],
            [shaped(seq_count, length, width)],
            out_specs=(spec,),
            grid=seq_count,
        )
        gathered = jnp.stack(chip_gather(gathered))
        other = over_batch(gathered, 1)
        grad_w_qkv, grad_w_out, grad_w_up, grad_w_down = kernel_call(
            functools.partial(unpack, out_part, up_part),
            "unpack",
            [scalars],
            [gathered, other],
            [whole(gathered.shape)] * 2,
            [
                shaped(3, width, columns, dtype=F32),
                shaped(columns, width, dtype=F32),
                shaped(width, hidden, dtype=F32),
                shaped(hidden, width, dtype=F32),
            ],
            [pltpu.VMEM((hidden, width), F32)],
        )
        grad_input = gather_units(grad_far, [grad_w_qkv])
        return (
            output,
            grad_input,
            common[0],
            common[1],
            grad_w_qkv,
            common[6, :heads],
            grad_w_out,
            common[2],
            common[3],
            grad_w_up,
            common[5],
            grad_w_down,
            common[4],
        )

    return jax.shard_map(
        shards,
        mesh=mesh,
        in_specs=(
            P("batch", None, None),
            P("batch", None),
            P(),
            P(),
            P(None, None, "tensor"),
            P("tensor"),
            P("tensor", None),
            P(),
            P(),
            P(None, "tensor"),
            P("tensor"),
            P("tensor", None),
            P(),
            P("batch", None, None),
        ),
        out_specs=(
            P("batch", None, None),
            P("batch", None, None),
            P(),
            P(),
            P(None, None, "tensor"),
            P("tensor"),
            P("tensor", None),
            P(),
            P(),
            P(None, "tensor"),
            P("tensor"),
            P("tensor", None),
            P(),
        ),
        check_vma=False,
    )
```

```python
import functools

import jax
import jax.numpy as jnp
from jax import lax
from jax.experimental import pallas as pl
from jax.experimental.pallas import tpu as pltpu
from jax.sharding import PartitionSpec as P

BISECT = 10
MASKED = -10000.0
NORM_EPS = 1e-05
LN2 = 0.6931471805599453
TILE = 128
EXTRA = 16
SMALL = 16
PLANE = 8
MIB = 1024 * 1024
BF16 = jnp.bfloat16
F32 = jnp.float32
GELU_A = 0.7978845608028654
GELU_B = 0.044715


def layer_norm(values, norm_gain, norm_shift):
    centre = values - jnp.mean(values, axis=-1, keepdims=True)
    spread = jnp.mean(centre * centre, axis=-1, keepdims=True)
    return centre * lax.rsqrt(spread + NORM_EPS) * norm_gain + norm_shift


def dot_nt(left, right):
    return lax.dot_general(left, right, (((1,), (1,)), ((), ())), preferred_element_type=F32)


def dot_nn(left, right):
    return lax.dot_general(left, right, (((1,), (0,)), ((), ())), preferred_element_type=F32)


def dot_tn(left, right):
    return lax.dot_general(left, right, (((0,), (0,)), ((), ())), preferred_element_type=F32)


def tile_mask(first, starts_ref):
    keys = lax.broadcasted_iota(jnp.int32, (first + TILE, TILE), 0)
    queries = lax.broadcasted_iota(jnp.int32, (first + TILE, TILE), 1) + first
    return (keys <= queries) & (keys >= starts_ref[:, first : first + TILE])


def head_lanes(values, head):
    lanes = lax.broadcasted_iota(jnp.int32, values.shape, 1)
    return jnp.where((lanes >= head * 64) & (lanes < head * 64 + 64), values, jnp.zeros_like(values))


def rolled(values, shift, rows):
    return pltpu.roll(values, shift, 0)[:rows]


def prepare_cotangent(scalars_ref, cotangent_ref, dep_ref, cot_ref):
    shift = scalars_ref[5]
    cot_ref[...] = rolled(cotangent_ref[0].astype(F32), shift, cot_ref.shape[0]).astype(BF16)


def prepare(scalars_ref, inputs_ref, gain_ref, bias_ref, tokens_ref, normed_ref):
    rows, length = tokens_ref.shape[0], inputs_ref.shape[1]
    shift = scalars_ref[5]
    tokens = rolled(inputs_ref[0].astype(F32), shift, rows)
    tokens_ref[...] = tokens.astype(BF16)
    normed_ref[...] = layer_norm(tokens, gain_ref[...], bias_ref[...]).astype(BF16)


def pack_qkv(place_ref, weight_ref, bias_ref, alpha_ref, out_ref):
    part, columns = weight_ref.shape[1:]
    for index in range(3):
        out_ref[:part, index * columns : (index + 1) * columns] = weight_ref[index]
    lanes = lax.broadcasted_iota(jnp.int32, (1, 2 * columns), 1)
    alphas = jnp.zeros((1, 2 * columns), F32)
    for head in range(alpha_ref.shape[0]):
        alphas = jnp.where(lanes == head, alpha_ref[head], alphas)
    rest = jnp.concatenate([bias_ref[:, 3 * columns :], alphas], axis=1)
    values = jnp.concatenate([bias_ref[:, : 3 * columns], rest])
    high = values.astype(BF16).astype(F32)
    middle = (values - high).astype(BF16).astype(F32)
    low = values - high - middle
    blank = jnp.zeros((EXTRA - 6, 3 * columns), F32)
    out_ref[part:, :] = jnp.concatenate([high, middle, low, blank]).astype(BF16)


def pack_rest(place_ref, out_weight_ref, up_ref, down_ref, *refs):
    part_ref, turned_ref, turn_ref = refs[-3:]
    out_part = out_weight_ref.shape[0]
    up_part = down_ref.shape[0]
    turn_ref[...] = jnp.transpose(up_ref[...].astype(F32))
    turned_ref[...] = turn_ref[...].astype(BF16)
    rows = pl.ds(pl.multiple_of(place_ref[0] * up_part, up_part), up_part)
    part_ref[:out_part, :] = out_weight_ref[...]
    part_ref[out_part : out_part + up_part, :] = turn_ref[rows, :].astype(BF16)
    part_ref[out_part + up_part :, :] = down_ref[...]


def stack_four(*refs):
    for index in range(4):
        refs[-1][index] = refs[index][...]


def assemble(other, scalars_ref, own_ref, right_one, left_one, right_two, left_two, far_ref, *refs):
    out_ref, both_ref = refs[-2:]
    pair = scalars_ref[1] ^ other
    rows = own_ref.shape[0]
    sources = ((own_ref, 0), (right_one, -1), (left_one, 1), (right_two, -2), (left_two, 2), (far_ref, 3), (far_ref, -3))
    for half in range(2):
        away = 2 * pair + half - scalars_ref[2]
        for ref, distance in sources:

            @pl.when(away == distance)
            def _():
                both_ref[half * rows : (half + 1) * rows, :] = ref[...].astype(F32)

    out_ref[0] = pltpu.roll(both_ref[...], scalars_ref[3 + pair], 0).astype(BF16)


def assemble_all(scalars_ref, all_ref, *refs):
    rows = all_ref.shape[1]
    both = all_ref[...].reshape(2 * rows, all_ref.shape[2]).astype(F32)
    refs[-1][0] = pltpu.roll(both, scalars_ref[3 + pl.program_id(0)], 0).astype(BF16)


def add_parts(keep_ref, sent_ref, *out_refs):
    for index, ref in enumerate(out_refs):

        @pl.when(pl.program_id(0) == index)
        def _():
            ref[...] = (keep_ref[0].astype(F32) + sent_ref[0].astype(F32)).astype(BF16)


def attend_forward(heads, base, weight_count, dep_count, scalars_ref, alpha_ref, normed_ref, starts_ref, *refs):
    slot = (base + pl.program_id(0)) * heads
    weight_refs = refs[:weight_count]
    qkv_ref, weight_out_ref, attended_ref, tau_ref, shifted_ref = refs[weight_count + dep_count :]
    rows = normed_ref.shape[0]
    if weight_count == 1:
        (weight_ref,) = weight_refs
        for index in range(3):
            weight_out_ref[:, index * heads * 64 : (index + 1) * heads * 64] = weight_ref[index]
    else:
        for core, weight_ref in enumerate(weight_refs):
            part = weight_ref.shape[1]
            for chip in range(4):
                row = pl.multiple_of((scalars_ref[0] ^ (2 * chip + core)) * part, part)
                weight_out_ref[pl.ds(row, part), :] = weight_ref[chip]
    width = heads * 64
    qkv = dot_nn(normed_ref[...], weight_out_ref[...]).astype(BF16)
    qkv_ref[...] = qkv
    queries = qkv[:, :width]
    keys = qkv[:, width : 2 * width]
    values_t = jnp.transpose(qkv[:, 2 * width :].astype(F32)).astype(BF16)
    tiles = [(h, first) for h in range(heads) for first in range(0, rows, TILE)]
    offsets = []
    total = 0
    for h, first in tiles:
        offsets.append(total)
        total += first + TILE
    highs, counts = [], []
    for (h, first), offset in zip(tiles, offsets):
        alpha_minus = alpha_ref[slot + h] - 1.0
        query = head_lanes(queries[first : first + TILE], h)
        scores = dot_nt(keys[: first + TILE], query) * 0.125
        shifted = jnp.where(tile_mask(first, starts_ref), alpha_minus * scores, MASKED)
        shifted_ref[offset : offset + first + TILE, :] = shifted
        spots = lax.broadcasted_iota(jnp.int32, (1, TILE), 1) + (first + 1)
        counts.append((spots - starts_ref[:, first : first + TILE]).astype(F32))
        highs.append(jnp.max(shifted, axis=0, keepdims=True))
    alpha_rows = jnp.concatenate(
        [jnp.full((rows // TILE, TILE), alpha_ref[slot + h] - 1.0, F32) for h in range(heads)]
    )
    bottom = jnp.concatenate(highs) - 1.0
    bracket = jnp.concatenate(highs) - jnp.exp(-alpha_rows * jnp.log(jnp.concatenate(counts))) - bottom
    cell = bracket * (1.0 / 2**BISECT)
    top = float(2**BISECT - 1)

    def evaluate(point):
        sums, slopes = [], []
        for index, ((h, first), offset) in enumerate(zip(tiles, offsets)):
            power = (1.0 / (alpha_ref[slot + h] - 1.0) - 1.0) * (1.0 / LN2)
            margin = jnp.maximum(shifted_ref[offset : offset + first + TILE, :] - point[index : index + 1], 0.0)
            slope = jnp.exp2(power * jnp.log(margin))
            slopes.append(jnp.sum(slope, axis=0, keepdims=True))
            sums.append(jnp.sum(slope * margin, axis=0, keepdims=True))
        return jnp.concatenate(sums), jnp.concatenate(slopes)

    def newton(point, sums, slopes):
        return point + (sums - jnp.exp((1.0 - alpha_rows) * jnp.log(sums))) / slopes

    def index_of(point):
        return jnp.clip(jnp.floor((point - bottom) / jnp.maximum(cell, 1e-30)), 0.0, top)

    point = bottom + 0.5 * bracket
    for _ in range(3):
        point = jnp.maximum(newton(point, *evaluate(point)), bottom)

    def unsettled(state):
        return state[1] > 0.0

    def settle(state):
        spot = state[0]
        after = bottom + (spot + 1.0) * cell
        sums, slopes = evaluate(after)
        higher = (sums >= 1.0) & (spot < top) & (after > bottom + spot * cell)
        spot = jnp.where(higher, jnp.maximum(spot + 1.0, index_of(newton(after, sums, slopes))), spot)
        return spot, jnp.max(jnp.where(higher, 1.0, 0.0))

    spot, _ = lax.while_loop(unsettled, settle, (index_of(point), jnp.float32(1.0)))
    low_rows = bottom + spot * cell
    lows = [low_rows[index : index + 1] for index in range(len(tiles))]
    for (h, first), offset, low in zip(tiles, offsets, lows):
        exponent = 1.0 / (alpha_ref[slot + h] - 1.0)
        shifted = shifted_ref[offset : offset + first + TILE, :]
        margin = jnp.maximum(shifted - low, 0.0)
        slope = jnp.exp2((exponent - 1.0) * (1.0 / LN2) * jnp.log(margin))
        slopes = exponent * jnp.sum(slope, axis=0, keepdims=True)
        summed = jnp.sum(slope * margin, axis=0, keepdims=True)
        tau = low + (summed - 1.0) / slopes
        tau_ref[h : h + 1, first : first + TILE] = tau
        margin = jnp.maximum(shifted - tau, 0.0)
        probs = jnp.exp2(exponent * (1.0 / LN2) * jnp.log(margin)).astype(BF16)
        out = dot_nn(values_t[h * 64 : h * 64 + 64, : first + TILE], probs)
        attended_ref[first : first + TILE, h * 64 : h * 64 + 64] = jnp.transpose(out).astype(BF16)


def attend_backward(heads, base, scalars_ref, alpha_ref, normed_ref, qkv_ref, tau_ref, starts_ref, dattended_ref, *refs):
    slot = (base + pl.program_id(0)) * heads
    dqkv_ref, keep_ref, send_ref, dalpha_ref, dkeys_ref, dvalues_ref, grad_ref = refs[-7:]
    rows = normed_ref.shape[0]
    width = heads * 64
    queries = qkv_ref[:, :width]
    keys = qkv_ref[:, width : 2 * width]
    values = qkv_ref[:, 2 * width :]
    keys_t = jnp.transpose(keys.astype(F32)).astype(BF16)
    dkeys_ref[...] = jnp.zeros_like(dkeys_ref)
    dvalues_ref[...] = jnp.zeros_like(dvalues_ref)
    for h in range(heads):
        alpha_minus = alpha_ref[slot + h] - 1.0
        exponent = 1.0 / alpha_minus
        dalpha = jnp.zeros((1, TILE), F32)
        for first in range(0, rows, TILE):
            end = first + TILE
            query = head_lanes(queries[first:end], h)
            dout = head_lanes(dattended_ref[first:end, :], h)
            scores = dot_nt(keys[:end], query) * 0.125
            shifted = jnp.where(tile_mask(first, starts_ref), alpha_minus * scores, MASKED)
            margin = jnp.maximum(shifted - tau_ref[h : h + 1, first:end], 0.0)
            log_margin = jnp.log(margin)
            slope = jnp.exp2((exponent - 1.0) * (1.0 / LN2) * log_margin)
            probs = slope * margin
            slope = exponent * slope
            dprobs = dot_nt(values[:end], dout)
            slope_sum = jnp.sum(slope, axis=0, keepdims=True)
            mixed = jnp.sum(slope * dprobs, axis=0, keepdims=True)
            centred = dprobs - mixed / slope_sum
            log_margin = jnp.where(margin > 0.0, log_margin, 0.0)
            alpha_part = slope * scores - (exponent * exponent) * (probs * log_margin)
            dalpha = dalpha + jnp.sum(alpha_part * centred, axis=0, keepdims=True)
            dscores = (alpha_minus * (slope * centred)).astype(BF16)
            dvalues_ref[:end, :] += dot_nn(probs.astype(BF16), dout)
            dkeys_ref[:end, :] += dot_nn(dscores, query)
            dquery_t = dot_nn(keys_t[h * 64 : h * 64 + 64, :end], dscores) * 0.125
            dqkv_ref[first:end, h * 64 : h * 64 + 64] = jnp.transpose(dquery_t).astype(BF16)
        dalpha_ref[h : h + 1, :] = dalpha
    dqkv_ref[:, width : 2 * width] = (dkeys_ref[...] * 0.125).astype(BF16)
    dqkv_ref[:, 2 * width :] = dvalues_ref[...].astype(BF16)
    grad = dot_tn(normed_ref[...], dqkv_ref[...]).astype(BF16)
    grad_ref[...] = grad.reshape(grad_ref.shape)
    for chip in range(4):
        keep_ref[chip] = grad_ref[scalars_ref[0] ^ (2 * chip)]
        send_ref[chip] = grad_ref[scalars_ref[0] ^ (2 * chip + 1)]


def norm_back(values, gain, dnormed):
    centre = values - jnp.mean(values, axis=-1, keepdims=True)
    scale = lax.rsqrt(jnp.mean(centre * centre, axis=-1, keepdims=True) + NORM_EPS)
    unit = centre * scale
    scaled = dnormed * gain
    mean = jnp.mean(scaled, axis=-1, keepdims=True)
    mixed = jnp.mean(scaled * unit, axis=-1, keepdims=True)
    dvalues = scale * (scaled - mean - unit * mixed)
    return dvalues, jnp.sum(dnormed * unit, axis=0, keepdims=True), jnp.sum(dnormed, axis=0, keepdims=True)


def feed_forward(slots, scalars_ref, tokens_ref, cot_ref, gain_ref, bias_ref, up_bias_ref, down_bias_ref, *refs):
    attended_refs = refs[:2]
    out_own, up_own, down_own, far_zero, far_one = refs[2:7]
    out_ref, dresid_ref, dattended_ref, keep_ref, send_ref, small_ref = refs[7:13]
    w_out, w_up, w_down, sums, dnormed_ref, grad_out, grad_up, grad_down, copies = refs[13:]
    place = scalars_ref[0]
    out_part = w_out.shape[1] // PLANE
    up_part = w_up.shape[1] // PLANE
    out_moves = [(out_own, w_out.at[0])]
    moves = [(up_own, w_up.at[0]), (down_own, w_down.at[0])]
    for core, far in enumerate((far_zero, far_one)):
        for chip in range(4):
            spot = place ^ (2 * chip + core)
            out_rows = pl.ds(pl.multiple_of(spot * out_part, out_part), out_part)
            up_rows = pl.ds(pl.multiple_of(spot * up_part, up_part), up_part)
            out_moves.append((far.at[chip, :, :out_part], w_out.at[1:, out_rows]))
            moves.append((far.at[chip, :, out_part : out_part + up_part], w_up.at[1:, up_rows]))
            moves.append((far.at[chip, :, out_part + up_part :], w_down.at[1:, up_rows]))
    started = []

    def begin(source, target):
        copy = pltpu.make_async_copy(source, target, copies.at[len(started)])
        copy.start()
        started.append(copy)

    for source, target in out_moves + moves:
        begin(source, target)
    for copy in started[: len(out_moves)]:
        copy.wait()

    width = tokens_ref.shape[1]
    attended = jnp.concatenate([ref[...] for ref in attended_refs], axis=1)
    out_weights = w_out[...].reshape(slots * w_out.shape[1], width)
    resid = tokens_ref[...].astype(F32) + dot_nn(attended, out_weights)
    sums[...] = resid
    normed = layer_norm(resid, gain_ref[...], bias_ref[...]).astype(BF16)
    dnormed_ref[...] = jnp.zeros_like(dnormed_ref)
    cot = cot_ref[...]
    for copy in started[len(out_moves) :]:
        copy.wait()
    for slot in range(slots):
        pre = dot_nt(normed, w_up[slot]) + up_bias_ref[slot : slot + 1, :]
        square = pre * pre
        bend = jnp.tanh(pre * (GELU_A + GELU_A * GELU_B * square))
        half = 0.5 + 0.5 * bend
        act = (pre * half).astype(BF16)
        slope = half + (0.5 * pre) * (1.0 - bend * bend) * (GELU_A + 3.0 * GELU_A * GELU_B * square)
        sums[...] += dot_nn(act, w_down[slot])
        dpre = (dot_nt(cot, w_down[slot]) * slope).astype(BF16)
        small_ref[3 + slot : 4 + slot, :] = jnp.sum(dpre.astype(F32), axis=0, keepdims=True)
        dnormed_ref[...] += dot_nn(dpre, w_up[slot])
        grad_down[slot] = dot_tn(act, cot).astype(BF16).reshape(PLANE, up_part, width)
        grad_up[slot] = dot_tn(dpre, normed).astype(BF16).reshape(PLANE, up_part, width)
    out_ref[...] = (sums[...] + down_bias_ref[...]).astype(BF16)
    dresid, small_ref[0:1, :], small_ref[1:2, :] = norm_back(resid, gain_ref[...], dnormed_ref[...])
    cot_full = cot.astype(F32)
    small_ref[2:3, :] = jnp.sum(cot_full, axis=0, keepdims=True)
    dresid = cot_full + dresid
    dresid_ref[...] = dresid
    dresid_low = dresid.astype(BF16)
    dattended_ref[...] = dot_nt(dresid_low, out_weights).astype(BF16)
    grad_out[...] = dot_tn(attended, dresid_low).astype(BF16).reshape(grad_out.shape)
    for core, target in enumerate((keep_ref, send_ref)):
        for chip in range(4):
            spot = place ^ (2 * chip + core)
            for slot in range(slots):
                target[chip, slot, :out_part] = grad_out[slot, spot]
                target[chip, slot, out_part : out_part + up_part] = grad_up[slot, spot]
                target[chip, slot, out_part + up_part :] = grad_down[slot, spot]


def finish(slots, heads, tokens_ref, dresid_ref, gain_ref, two_ref, *refs):
    dqkv_first, dqkv_rest, weight_first, weight_rest, alpha_first, alpha_rest = refs[:6]
    out_ref, message_ref, small_ref = refs[-3:]
    dqkv = jnp.concatenate([dqkv_first[...]] + [dqkv_rest[slot] for slot in range(slots - 1)], axis=1)
    weights = jnp.concatenate([weight_first[...]] + [weight_rest[slot] for slot in range(slots - 1)], axis=1)
    dnormed = dot_nt(dqkv, weights)
    dinput, gain, bias = norm_back(tokens_ref[...].astype(F32), gain_ref[...], dnormed)
    out_ref[...] = (dresid_ref[...] + dinput).astype(BF16)
    width = gain.shape[1]
    lanes = lax.broadcasted_iota(jnp.int32, (1, width), 1)
    alphas = []
    for slot in range(slots):
        values = alpha_first[...] if slot == 0 else alpha_rest[slot - 1]
        totals = jnp.sum(values, axis=1, keepdims=True)
        line = jnp.zeros((1, width), F32)
        for head in range(heads):
            line = jnp.where(lanes == head, totals[head : head + 1], line)
        alphas.append(line)
    blank = jnp.zeros((SMALL - 5 - 2 * slots, width), F32)
    values = jnp.concatenate([gain, bias, two_ref[...]] + alphas + [blank])
    span = message_ref.shape[2]
    side = jnp.concatenate([values[:, span:], jnp.zeros((SMALL, 2 * span - width), F32)], axis=1)
    small = jnp.concatenate([values[:, :span], side])
    small_ref[...] = small
    message_ref[0] = pair_of(small)


def pair_of(values):
    high = values.astype(BF16)
    return jnp.concatenate([high, (values - high.astype(F32)).astype(BF16)])


def value_of(pair):
    half = pair.shape[0] // 2
    return pair[:half].astype(F32) + pair[half:].astype(F32)


def tree(four):
    return (four[0] + four[1]) + (four[2] + four[3])


def sum_core(slots, keep_ref, received_ref, small_ref, *refs):
    total = small_ref[...] + value_of(received_ref[4 * slots])
    refs[4][...] = total
    pair = pair_of(total)
    for chip in range(4):
        for slot in range(slots):
            index = 4 * slot + chip
            refs[chip][slot] = (keep_ref[index].astype(F32) + received_ref[index].astype(F32)).astype(BF16)
        refs[chip][slots] = pair


def gate(*refs):
    pass


def sum_plane(slots, *refs):
    rest_refs, qkv_refs, small_ref = refs[:4], refs[4:8], refs[8]
    rest_out, qkv_out, small_out = refs[9:12]
    messages = refs[12:]
    rows = rest_out.shape[0]
    part, span = qkv_out.shape
    width = rest_out.shape[1]
    small = tree([small_ref[...]] + [value_of(ref[slots]) for ref in qkv_refs[1:]])
    small = jnp.concatenate([small[:SMALL], small[SMALL:, : width - span]], axis=1)
    small_out[...] = small
    pair = pair_of(small)
    for slot in range(slots):
        rest = tree([ref[slot].astype(F32) for ref in rest_refs])
        qkv = tree([ref[slot].astype(F32) for ref in qkv_refs])
        if slot == 0:
            rest_out[...] = rest
            qkv_out[...] = qkv
        else:
            message = messages[slot - 1]
            message[:rows] = rest.astype(BF16)
            message[rows : rows + part, :span] = qkv.astype(BF16)
            message[rows : rows + part, span:] = jnp.zeros((part, width - span), BF16)
            message[rows + part :] = pair


def sum_line(slots, rest_ref, qkv_ref, small_ref, *refs):
    received, out_ref, total_ref = refs[: slots - 1], refs[-2], refs[-1]
    rows = rest_ref.shape[0]
    part, span = qkv_ref.shape
    width = rest_ref.shape[1]
    out_ref[:rows] = tree([rest_ref[...]] + [ref[:rows].astype(F32) for ref in received]).astype(BF16)
    qkv = [ref[rows : rows + part, :span].astype(F32) for ref in received]
    out_ref[rows:, :span] = tree([qkv_ref[...]] + qkv).astype(BF16)
    out_ref[rows:, span:] = jnp.zeros((part, width - span), BF16)
    smalls = [small_ref[...]] + [value_of(ref[rows + part :]) for ref in received]
    common = tree([one[:5] for one in smalls])
    bias = tree([one[5 + slot : 6 + slot] for slot, one in enumerate(smalls)])
    alpha = tree([one[5 + slots + slot : 6 + slots + slot] for slot, one in enumerate(smalls)])
    total_ref[...] = jnp.concatenate([common, bias, alpha, jnp.zeros((1, width), F32)])


def unpack(out_part, up_part, scalars_ref, zero_ref, one_ref, qkv_ref, out_ref, up_ref, down_ref, turn_ref):
    columns = qkv_ref.shape[2]
    for core, ref in enumerate((zero_ref, one_ref)):
        for chip in range(4):
            spot = scalars_ref[0] ^ (2 * chip + core)
            out_rows = pl.ds(pl.multiple_of(spot * out_part, out_part), out_part)
            up_rows = pl.ds(pl.multiple_of(spot * up_part, up_part), up_part)
            first = out_part
            out_ref[out_rows, :] = ref[chip, :first].astype(F32)
            turn_ref[up_rows, :] = ref[chip, first : first + up_part].astype(F32)
            first = first + up_part
            down_ref[up_rows, :] = ref[chip, first : first + up_part].astype(F32)
            first = first + up_part
            part = ref.shape[1] - first
            qkv_rows = pl.ds(pl.multiple_of(spot * part, part), part)
            for index in range(3):
                qkv_ref[index, qkv_rows, :] = ref[chip, first:, index * columns : (index + 1) * columns].astype(F32)
    up_ref[...] = jnp.transpose(turn_ref[...])


def whole(shape):
    return pl.BlockSpec(shape, lambda *_: (0,) * len(shape), memory_space=pltpu.VMEM)


def kernel_call(body, name, scalars, operands, in_specs, out_shapes, scratch=(), out_specs=None, grid=1, flops=10**9, vmem=16,
                aliases=None, far_in=False, far_out=()):
    spec = pltpu.PrefetchScalarGridSpec(
        num_scalar_prefetch=len(scalars),
        grid=(grid,),
        in_specs=in_specs,
        out_specs=out_specs or tuple(whole(shape.shape) for shape in out_shapes),
        scratch_shapes=list(scratch),
    )
    far = lambda array: pltpu.with_memory_space_constraint(array, pltpu.HBM) if far_in else array
    return pl.pallas_call(
        body,
        out_shape=tuple(
            pltpu.HBM(shape.shape, shape.dtype) if index in far_out else shape for index, shape in enumerate(out_shapes)
        ),
        grid_spec=spec,
        compiler_params=pltpu.CompilerParams(vmem_limit_bytes=vmem * MIB),
        input_output_aliases=aliases or {},
        cost_estimate=pl.CostEstimate(flops=flops, bytes_accessed=10**6, transcendentals=0),
        name=name,
    )(*map(far, scalars), *map(far, operands))


def shaped(*shape, dtype=BF16):
    return jax.ShapeDtypeStruct(shape, dtype)


ANYWHERE = pl.BlockSpec(memory_space=pl.ANY)


def run_forward(heads, scalars, alpha, normed, weights, base, count, starts, deps):
    rows, width = normed.shape
    columns = 3 * heads * 64
    total = heads * sum(range(TILE, rows + 1, TILE))
    stacked = lambda *shape: pl.BlockSpec((None,) + shape, lambda i, *_: (i, 0, 0), memory_space=pltpu.VMEM)
    if base == 0:
        weight_specs = [whole(weights[0].shape)]
    else:
        block = (4, None) + weights[0].shape[2:]
        weight_specs = [pl.BlockSpec(block, lambda i, *_: (0, i, 0, 0), memory_space=pltpu.VMEM)] * 2
    smem = pl.BlockSpec(memory_space=pltpu.SMEM)
    return kernel_call(
        functools.partial(attend_forward, heads, base, len(weights), len(deps)),
        "attend_forward",
        [scalars],
        [alpha, normed, starts, *weights, *deps],
        [smem, whole(normed.shape), whole(starts.shape)] + weight_specs + [ANYWHERE] * len(deps),
        [
            shaped(count, rows, columns),
            shaped(count, width, columns),
            shaped(rows, count * heads * 64),
            shaped(count, heads, rows, dtype=F32),
        ],
        [pltpu.VMEM((total, TILE), F32)],
        out_specs=(
            stacked(rows, columns),
            stacked(width, columns),
            pl.BlockSpec((rows, heads * 64), lambda i, *_: (0, i), memory_space=pltpu.VMEM),
            stacked(heads, rows),
        ),
        grid=count,
        flops=5 * 10**9 * count,
    )


def run_backward(heads, scalars, alpha, normed, qkv, tau, starts, dattended, base, count, slots, buffers, deps):
    rows, width = normed.shape
    columns = 3 * heads * 64
    smem = pl.BlockSpec(memory_space=pltpu.SMEM)
    stacked = lambda *shape: pl.BlockSpec((None,) + shape, lambda i, *_: (i, 0, 0), memory_space=pltpu.VMEM)
    dattended_spec = pl.BlockSpec((rows, heads * 64), lambda i, *_: (0, base + i), memory_space=pltpu.VMEM)
    parts = (width // PLANE, columns)
    message = pl.BlockSpec((4,) + parts, lambda i, *_: (base + i, 0, 0), memory_space=pltpu.VMEM)
    return kernel_call(
        functools.partial(attend_backward, heads, base),
        "attend_backward",
        [scalars],
        [alpha, normed, qkv, tau, starts, dattended, *buffers, *deps],
        [smem, whole(normed.shape), stacked(rows, columns), stacked(heads, rows), whole(starts.shape)]
        + [dattended_spec]
        + [ANYWHERE] * (len(buffers) + len(deps)),
        [
            shaped(count, rows, columns),
            shaped(4 * slots, *parts),
            shaped(4 * slots + 1, *parts),
            shaped(count, heads, TILE, dtype=F32),
        ],
        [
            pltpu.VMEM((rows, heads * 64), F32),
            pltpu.VMEM((rows, heads * 64), F32),
            pltpu.VMEM((PLANE,) + parts, BF16),
        ],
        out_specs=(stacked(rows, columns), message, message, stacked(heads, TILE)),
        grid=count,
        flops=4 * 10**9 * count,
        aliases={7: 1, 8: 2} if buffers else None,
        far_in=True,
    )


def split_wide(values):
    high = lax.reduce_precision(values, exponent_bits=8, mantissa_bits=7)
    return jnp.concatenate([high.astype(BF16), (values - high).astype(BF16)])


def join_wide(pair):
    pair = pair.astype(F32)
    half = pair.shape[0] // 2
    return pair[:half] + pair[half:]


def solution(mesh):
    batch_size = mesh.shape["batch"]
    tensor_size = mesh.shape["tensor"]

    def over_batch(array, hop):
        return lax.ppermute(array, "batch", [(i, i ^ hop) for i in range(batch_size)])

    def over_tensor(array, hop):
        return lax.ppermute(array, "tensor", [(i, i ^ hop) for i in range(tensor_size)])

    def line_gather(part):
        return [over_tensor(part, hop) for hop in range(1, tensor_size)]

    def chip_gather(part):
        return [part] + [over_batch(part, hop) for hop in (2, 4, 6)]

    def upper_sum(array, split):
        hop = PLANE
        while hop < batch_size:
            array = array + join(over_batch(cut(array, split), hop), split)
            hop *= 2
        return array

    def cut(array, split):
        return split_wide(array) if split else array.astype(BF16)

    def join(array, split):
        return join_wide(array) if split else array.astype(F32)

    def shards(inputs, doc_lengths, ln1_gain, ln1_bias, w_qkv, entmax_alpha, w_out, ln2_gain, ln2_bias,
               w_up, up_bias, w_down, down_bias, cotangent):
        seq_count, length, width = inputs.shape
        heads = entmax_alpha.shape[0]
        hidden = w_up.shape[1]
        rows = length // 2
        columns = heads * 64
        place = lax.axis_index("batch") % PLANE
        line = lax.axis_index("tensor")

        def own_part(array):
            return lax.dynamic_slice_in_dim(array, place * (array.shape[0] // PLANE), array.shape[0] // PLANE)

        out_part = w_out.shape[0] // PLANE
        up_part = hidden // PLANE
        part = width // PLANE
        span = 3 * columns
        rest_rows = out_part + 2 * up_part
        spot = place.reshape(1).astype(jnp.int32)
        row = lambda array: array.reshape(1, -1)
        by_place = lambda rows: pl.BlockSpec((rows, width), lambda i, ref: (ref[0], 0), memory_space=pltpu.VMEM)

        (qkv_part,) = kernel_call(
            pack_qkv,
            "pack_qkv",
            [spot],
            [w_qkv, row(up_bias), entmax_alpha],
            [
                pl.BlockSpec((3, part, columns), lambda i, ref: (0, ref[0], 0), memory_space=pltpu.VMEM),
                whole((1, hidden)),
                pl.BlockSpec(memory_space=pltpu.SMEM),
            ],
            [shaped(part + EXTRA, span)],
            far_in=True,
        )
        qkv_line = line_gather(qkv_part)
        extras = [far[part : part + 6].astype(F32) for far in qkv_line]
        extras = [(far[:2] + far[2:4] + far[4:]).reshape(-1) for far in extras]
        alphas = jnp.concatenate([entmax_alpha] + [far[hidden : hidden + heads] for far in extras])
        up_biases = jnp.stack([up_bias] + [far[:hidden] for far in extras])
        qkv_far = chip_gather(jnp.stack([far[:part] for far in qkv_line]))

        ends = jnp.cumsum(doc_lengths, axis=1)
        firsts = ends - doc_lengths
        big = jnp.sum(jnp.where(doc_lengths == rows, firsts, 0), axis=1)

        def unit_start(unit):
            return (jnp.take(big, unit // 2) + rows * (unit % 2)) % length

        start = unit_start(line)
        doc_places = (jnp.take(firsts, line // 2, axis=0) - start) % length
        spots = jnp.arange(rows, dtype=jnp.int32)
        starts = jnp.max(
            jnp.where(doc_places[:, None] <= spots[None, :], doc_places[:, None], 0), axis=0, keepdims=True
        )
        scalars = jnp.stack([place, line // 2, line, big[0], big[1], (length - start) % length]).astype(jnp.int32)

        rest_part, up_own = kernel_call(
            pack_rest,
            "pack_rest",
            [spot],
            [w_out, w_up, w_down],
            [by_place(out_part), whole(w_up.shape), by_place(up_part)],
            [shaped(rest_rows, width), shaped(hidden, width)],
            [pltpu.VMEM((hidden, width), F32)],
        )
        rest_line = line_gather(rest_part)

        sequence = pl.BlockSpec((1, length, width), lambda i, ref: (ref[1], 0, 0), memory_space=pltpu.VMEM)
        tokens, normed = kernel_call(
            prepare,
            "prepare",
            [scalars],
            [inputs, row(ln1_gain), row(ln1_bias)],
            [sequence, whole((1, width)), whole((1, width))],
            [shaped(rows, width)] * 2,
        )

        def stack(pieces, deps):
            (out,) = kernel_call(
                stack_four,
                "stack_four",
                [],
                [*pieces, *deps],
                [whole(pieces[0].shape)] * 4 + [ANYWHERE] * len(deps),
                [shaped(4, *pieces[0].shape)],
            )
            return out

        qkv_first, weight_first, attended_first, tau_first = run_forward(
            heads, scalars, entmax_alpha, normed, [w_qkv], 0, 1, starts, qkv_line
        )
        qkv_zero = stack(qkv_far, [attended_first])
        (cot,) = kernel_call(
            prepare_cotangent,
            "prepare_cotangent",
            [scalars],
            [cotangent, attended_first],
            [sequence, ANYWHERE],
            [shaped(rows, width)],
        )
        qkv_one = over_batch(qkv_zero, 1)
        qkv_rest, weight_rest, attended_rest, tau_rest = run_forward(
            heads, scalars, alphas, normed, [qkv_zero, qkv_one], 1, tensor_size - 1, starts, rest_line + [cot]
        )
        rest_zero = stack(chip_gather(jnp.stack(rest_line)), [attended_rest])
        rest_one = over_batch(rest_zero, 1)
        out_low, dresid, dattended, keep, send, small_two = kernel_call(
            functools.partial(feed_forward, tensor_size),
            "feed_forward",
            [scalars],
            [tokens, cot, row(ln2_gain), row(ln2_bias), up_biases, row(down_bias)]
            + [attended_first, attended_rest]
            + [w_out, up_own, w_down, rest_zero, rest_one],
            [whole((rows, width))] * 2
            + [whole((1, width))] * 2
            + [whole((tensor_size, hidden)), whole((1, width))]
            + [whole(attended_first.shape), whole(attended_rest.shape)]
            + [ANYWHERE] * 5,
            [
                shaped(rows, width),
                shaped(rows, width, dtype=F32),
                shaped(rows, tensor_size * columns),
                shaped(4, tensor_size, rest_rows, width),
                shaped(4, tensor_size, rest_rows, width),
                shaped(3 + tensor_size, width, dtype=F32),
            ],
            [
                pltpu.VMEM((tensor_size, columns, width), BF16),
                pltpu.VMEM((tensor_size, hidden, width), BF16),
                pltpu.VMEM((tensor_size, hidden, width), BF16),
                pltpu.VMEM((rows, width), F32),
                pltpu.VMEM((rows, width), F32),
                pltpu.VMEM((tensor_size, PLANE, out_part, width), BF16),
                pltpu.VMEM((tensor_size, PLANE, up_part, width), BF16),
                pltpu.VMEM((tensor_size, PLANE, up_part, width), BF16),
                pltpu.SemaphoreType.DMA((3 + 3 * PLANE,)),
            ],
            flops=8 * 10**9,
            far_out=(0, 1, 2),
            vmem=36,
        )

        def relay_two(first):
            right = lax.ppermute(first[0], "tensor", [(i, i + 1) for i in range(1, tensor_size - 1)])
            left = lax.ppermute(first[1], "tensor", [(i, i - 1) for i in range(1, tensor_size - 1)])
            return [right, left]

        def relay_one(chunk):
            right = lax.ppermute(chunk, "tensor", [(i, i + 1) for i in range(tensor_size - 1)])
            left = lax.ppermute(chunk, "tensor", [(i + 1, i) for i in range(tensor_size - 1)])
            return [right, left]

        def relay_three(second):
            return [lax.ppermute(jnp.where(line >= 2, second[0], second[1]), "tensor", [(2, 3), (1, 0)])]

        def wait_for(arrays, others):
            return list(
                kernel_call(
                    gate,
                    "gate",
                    [],
                    [*arrays, *others],
                    [ANYWHERE] * (len(arrays) + len(others)),
                    [shaped(*array.shape) for array in arrays],
                    out_specs=(ANYWHERE,) * len(arrays),
                    aliases={index: index for index in range(len(arrays))},
                )
            )

        def gather_units(far, deps):
            out = None
            for other in range(2):
                spec = pl.BlockSpec(
                    (1, length, width), lambda i, ref: (ref[1] ^ other, 0, 0), memory_space=pltpu.VMEM
                )
                sources = [*far[:-1], far[0] if other == 0 else far[-1]]
                extra = [*deps] if other == 0 else [out]
                (out,) = kernel_call(
                    functools.partial(assemble, other),
                    "assemble",
                    [scalars],
                    sources + extra,
                    [whole((rows, width))] * 6 + [ANYWHERE] * len(extra),
                    [shaped(seq_count, length, width)],
                    [pltpu.VMEM((length, width), F32)],
                    out_specs=(spec,),
                    aliases=None if other == 0 else {7: 0},
                )
            return out

        out_all = lax.all_gather(out_low, "tensor")
        piece = pl.BlockSpec((1, tensor_size, rest_rows, width), lambda i: (i, 0, 0, 0), memory_space=pltpu.VMEM)
        rest_half = kernel_call(
            add_parts,
            "add_parts",
            [],
            [keep, over_batch(send, 1)],
            [piece] * 2,
            [shaped(tensor_size, rest_rows, width)] * 4,
            grid=4,
        )

        dqkv_first, keep, message, alpha_first = run_backward(
            heads, scalars, entmax_alpha, normed, qkv_first, tau_first, starts, dattended, 0, 1, tensor_size, [], []
        )
        dqkv_rest, keep, message, alpha_rest = run_backward(
            heads, scalars, alphas, normed, qkv_rest, tau_rest, starts, dattended, 1, tensor_size - 1, tensor_size,
            [keep, message], list(rest_half),
        )
        def call(body, name, operands, out_shapes):
            return kernel_call(
                functools.partial(body, tensor_size),
                name,
                [],
                operands,
                [whole(array.shape) for array in operands],
                out_shapes,
            )

        def chip_exchange(pieces):
            return [over_batch(pieces[hop // 2], hop) for hop in (2, 4, 6)]

        rest_far = chip_exchange(rest_half)
        operands = [tokens, dresid, row(ln1_gain), small_two, dqkv_first[0], dqkv_rest, weight_first[0], weight_rest]
        operands += [alpha_first[0], alpha_rest]
        grad_chunk, message, small = kernel_call(
            functools.partial(finish, tensor_size, heads),
            "finish",
            [],
            operands + [message],
            [whole(array.shape) for array in operands] + [ANYWHERE],
            [shaped(rows, width), shaped(*message.shape), shaped(2 * SMALL, span, dtype=F32)],
            out_specs=(
                whole((rows, width)),
                pl.BlockSpec((1, part, span), lambda *_: (4 * tensor_size, 0, 0), memory_space=pltpu.VMEM),
                whole((2 * SMALL, span)),
            ),
            aliases={len(operands): 1},
        )
        grad_one = relay_one(grad_chunk)

        (message,) = wait_for([message], rest_far)
        halves = call(
            sum_core,
            "sum_core",
            [keep, over_batch(message, 1), small],
            [shaped(tensor_size + 1, part, span)] * 4 + [shaped(2 * SMALL, span, dtype=F32)],
        )
        rest_own, qkv_own_sum, small, *messages = call(
            sum_plane,
            "sum_plane",
            [rest_half[0]] + rest_far + [halves[0]] + chip_exchange(halves) + [halves[4]],
            [
                shaped(rest_rows, width, dtype=F32),
                shaped(part, span, dtype=F32),
                shaped(SMALL, width, dtype=F32),
            ]
            + [shaped(rest_rows + part + 2 * SMALL, width)] * (tensor_size - 1),
        )
        if batch_size > PLANE:
            rest_own, qkv_own_sum = upper_sum(rest_own, False), upper_sum(qkv_own_sum, False)
            small = upper_sum(small, True)
            messages = [upper_sum(one[: rest_rows + part], False).astype(BF16) for one in messages]
            messages = [jnp.concatenate([one, split_wide(small)]) for one in messages]
        received = [over_tensor(messages[hop - 1], hop) for hop in range(1, tensor_size)]
        grad_one = wait_for(grad_one, received[:1])
        grad_two = relay_two(grad_one)
        grad_far = [grad_chunk] + grad_one + grad_two + relay_three(grad_two)
        gathered, common = call(
            sum_line,
            "sum_line",
            [rest_own, qkv_own_sum, small] + received,
            [shaped(rest_rows + part, width), shaped(8, width, dtype=F32)],
        )
        spec = pl.BlockSpec((1, length, width), lambda i, ref: (i, 0, 0), memory_space=pltpu.VMEM)
        (output,) = kernel_call(
            assemble_all,
            "assemble_all",
            [scalars],
            [out_all, gathered],
            [pl.BlockSpec((2, rows, width), lambda i, ref: (i, 0, 0), memory_space=pltpu.VMEM), ANYWHERE],
            [shaped(seq_count, length, width)],
            out_specs=(spec,),
            grid=seq_count,
            far_in=True,
        )
        gathered = jnp.stack(chip_gather(gathered))
        other = over_batch(gathered, 1)
        grad_w_qkv, grad_w_out, grad_w_up, grad_w_down = kernel_call(
            functools.partial(unpack, out_part, up_part),
            "unpack",
            [scalars],
            [gathered, other],
            [whole(gathered.shape)] * 2,
            [
                shaped(3, width, columns, dtype=F32),
                shaped(columns, width, dtype=F32),
                shaped(width, hidden, dtype=F32),
                shaped(hidden, width, dtype=F32),
            ],
            [pltpu.VMEM((hidden, width), F32)],
        )
        grad_input = gather_units(grad_far, [grad_w_qkv])
        return (
            output,
            grad_input,
            common[0],
            common[1],
            grad_w_qkv,
            common[6, :heads],
            grad_w_out,
            common[2],
            common[3],
            grad_w_up,
            common[5],
            grad_w_down,
            common[4],
        )

    return jax.shard_map(
        shards,
        mesh=mesh,
        in_specs=(
            P("batch", None, None),
            P("batch", None),
            P(),
            P(),
            P(None, None, "tensor"),
            P("tensor"),
            P("tensor", None),
            P(),
            P(),
            P(None, "tensor"),
            P("tensor"),
            P("tensor", None),
            P(),
            P("batch", None, None),
        ),
        out_specs=(
            P("batch", None, None),
            P("batch", None, None),
            P(),
            P(),
            P(None, None, "tensor"),
            P("tensor"),
            P("tensor", None),
            P(),
            P(),
            P(None, "tensor"),
            P("tensor"),
            P("tensor", None),
            P(),
        ),
        check_vma=False,
    )
```
